32 devices in a mesh: parts: 2 (over y), aux: 4 (over x, core), occ: 4 (over z).
Axes of the slice: x: 2, y: 2, z: 4, core: 2. Of those that a mesh axis runs over, the one named last changes fastest.
Arguments:
- factors: bfloat16 [8, 896, 6144], P(('parts', 'aux'), 'occ'), parts along dimension 0, may hold values from -4 to 4
- block_mask: int32 [96, 8], P('parts'), parts along dimension 0, may hold values from 0 to 1, as said below
- block_lists: int32 [16, 24], P(('parts', 'occ')), parts along dimension 0, may hold values from -1 to 47, as said below
Outputs:
- exchange: float32 [12288, 6144], P(('parts', 'aux'), 'occ'), parts along dimension 0
The draws below stay inside these ranges and needn't reach their ends.
There are 2 independent parts, one for each index of `parts`. The reference program is written for one: setup_inputs(seed, part) draws one part's arguments, and reference() takes and returns one part's arrays. A program takes and returns all parts, laid end to end along the dimension named above; each array names one. Nothing has to cross between parts.
Inputs may be any that keep to these rules, and one draw needn't show every extreme that they name: block_mask[b, o] is 1 exactly when b appears in block_lists[o]. `block_lists`: each row lists distinct kept basis blocks in increasing order, then -1 in its unused slots; some row fills all 24 slots.
All inputs are finite; a program needn't handle non-finite values.
Results may differ from the reference program's by a relative error of at most 0.0003.
Values may be sent and summed in bfloat16 or wider, within the bound.
No kernel may reach another device: no remote copies, remote signals or barrier semaphores. Data moves between devices by JAX's collectives and lax.ppermute only.
A program may use at most 192 MiB of HBM per device.

```python
import jax
import jax.numpy as jnp
from jax import lax

NBF = 6144
NOCC = 896
BLK = 128
OBLK = 112
CAP = 24
NAUX = 4
NB = 48
NOB = 8


def screening(key):
    key_len, key_pick, key_center, key_jitter = jax.random.split(key, 4)
    lengths = jax.random.randint(key_len, (NOB,), CAP // 3, CAP * 2 // 3 + 1)
    busiest = jax.random.randint(key_pick, (), 0, NOB)
    lengths = jnp.where(jnp.arange(NOB) == busiest, CAP, lengths)
    centers = jax.random.randint(key_center, (NOB, 1), 0, NB)
    blocks = jnp.arange(NB, dtype=jnp.int32)[None, :]
    jitter = jax.random.randint(key_jitter, (NOB, NB), 0, 12)
    scores = (jnp.abs(blocks - centers) * 4 + jitter) * NB + blocks
    ranking = jnp.argsort(jnp.argsort(scores, axis=1), axis=1)
    retained = ranking < lengths[:, None]
    ordering = jnp.argsort(jnp.where(retained, 0, NB) + blocks, axis=1)[:, :CAP]
    slot_pos = jnp.arange(CAP)[None, :]
    listing = jnp.where(slot_pos < lengths[:, None], ordering, -1)
    return (retained, listing)


def draw_block_mask(key, part):
    retained, listing = screening(key)
    return retained.T.astype(jnp.int32)


def draw_block_lists(key, part):
    retained, listing = screening(key)
    return listing.astype(jnp.int32)


def raised(array, rng, source, target, parts, factor):
    def block_of(axis_at):
        return (jnp.arange(array.shape[axis_at]) // (array.shape[axis_at] // parts)).reshape((-1,) + (1,) * (array.ndim - 1 - axis_at))

    first = jax.random.permutation(rng, parts)[block_of(target)]
    second = (block_of(target) + parts // 2) % parts
    return jnp.where((block_of(source) == first) | (block_of(source) == second), factor * array, array)


def levels(stream_key, shape, shards, smallest, largest):
    def one(position, shards_of):
        steps = jax.random.uniform(jax.random.fold_in(jax.random.fold_in(stream_key, 6), position), (shards_of,), jnp.float32, smallest / len(shards), largest / len(shards))
        return jnp.repeat(jnp.exp(steps), shape[position] // shards_of).reshape((-1,) + (1,) * (len(shape) - position - 1))

    loudness = one(*shards[0])
    for cut in shards[1:]:
        loudness = loudness * one(*cut)
    return loudness


def noise_with(key, extent, scale, bound, shards, heavy, held_as=jnp.bfloat16):
    drawn = scale * jax.random.normal(key, extent, jnp.float32)
    if shards:
        drawn = drawn * levels(key, extent, shards, -0.22, 0.18)
    return jnp.clip(raised(drawn, jax.random.fold_in(key, 3), *heavy), -bound, bound).astype(held_as)


def setup_inputs(seed: int = 0, part: int = 0) -> dict:
    arg_keys = jax.random.split(jax.random.key(seed), 4)
    part_splits = jax.random.split(jax.random.fold_in(arg_keys[3], part), 4)
    factors = noise_with(part_splits[0], (NAUX, NOCC, NBF), ((NAUX * OBLK) ** -0.25), 4.0, ((0, 4), (1, 4)), (1, 2, 4, 2.0))
    block_mask = draw_block_mask(jax.random.fold_in(jax.random.fold_in(arg_keys[3], part), 71), part)
    block_lists = draw_block_lists(jax.random.fold_in(jax.random.fold_in(arg_keys[3], part), 71), part)
    return dict(factors=factors, block_mask=block_mask, block_lists=block_lists)


def reference(factors, block_mask, block_lists):
    row_weight = jnp.repeat(jnp.repeat(block_mask.T, OBLK, axis=0), BLK, axis=1)
    screened = jnp.where(row_weight[None] > 0, factors, jnp.zeros_like(factors))
    blocks = jnp.arange(NB, dtype=jnp.int32)
    exchange = jnp.zeros((NBF, NB, BLK), jnp.float32)
    for orbital in range(NOB):
        left_rows = screened[:, orbital * OBLK:(orbital + 1) * OBLK, :].reshape(NAUX * OBLK, NBF)
        right_cols = factors[:, orbital * OBLK:(orbital + 1) * OBLK, :].reshape(NAUX, OBLK, NB, BLK)
        picker = (block_lists[orbital][:, None] == blocks[None, :]).astype(jnp.float32)
        compact = jnp.einsum("qibk,cb->qick", right_cols.astype(jnp.float32), picker)
        compact = compact.astype(factors.dtype).reshape(NAUX * OBLK, CAP * BLK)
        partial_value = lax.dot_general(left_rows, compact, (((0,), (0,)), ((), ())), preferred_element_type=jnp.float32)
        placed = jnp.einsum("mck,cb->mbk", partial_value.reshape(NBF, CAP, BLK), picker, precision=lax.Precision.HIGHEST)
        exchange = exchange + placed
    return exchange.reshape(NBF, NBF)
```

```python
import functools

import jax
import jax.numpy as jnp
from jax import lax
from jax.experimental import pallas as pl
from jax.experimental.pallas import tpu as pltpu
from jax.sharding import PartitionSpec as P

BLK = 128
OBLK = 112
NB = 48


def pick_kernel(lists, factors, items, sem):
    orbitals, slots = lists.shape

    def start(slot, carry):
        for orbital in range(orbitals):
            block = jnp.maximum(lists[orbital, slot], 0)
            columns = pl.ds(pl.multiple_of(block * BLK, BLK), BLK)
            rows = pl.ds(orbital * OBLK, OBLK)
            pltpu.make_async_copy(
                factors.at[0, rows, columns], items.at[orbital * slots + slot], sem
            ).start()
        return carry

    lax.fori_loop(0, slots, start, 0)
    pltpu.make_async_copy(items, items, sem).wait()


def pick(factors, block_lists):
    orbitals, slots = block_lists.shape
    count = orbitals * slots
    return pl.pallas_call(
        pick_kernel,
        grid_spec=pltpu.PrefetchScalarGridSpec(
            num_scalar_prefetch=1,
            grid=(),
            in_specs=[pl.BlockSpec(memory_space=pl.ANY)],
            out_specs=pl.BlockSpec(memory_space=pl.ANY),
            scratch_shapes=[pltpu.SemaphoreType.DMA(())],
        ),
        out_shape=jax.ShapeDtypeStruct((count, OBLK, BLK), factors.dtype),
        cost_estimate=pl.CostEstimate(
            flops=0, bytes_accessed=4 * count * OBLK * BLK, transcendentals=0
        ),
        name="pick",
    )(block_lists, factors)


def product_kernel(origins, orbitals, row_blocks, col_blocks, pos, meta, *refs):
    sources = refs[: -6]
    out, lhs, rhs, acc, in_sem, out_sem = refs[-6:]
    per_origin = len(sources) // origins
    row_tile = 2 if row_blocks % 2 == 0 else 1
    col_tile = 4 if col_blocks % 4 == 0 else 3 if col_blocks % 3 == 0 else 1
    first_row, first_col = meta[0], meta[1]

    def place(orbital, block):
        return pos[orbital * NB + block]

    def any_kept(orbital, first, count):
        best = place(orbital, first)
        for step in range(1, count):
            best = jnp.maximum(best, place(orbital, first + step))
        return best >= 0

    def transfers(finish):
        for origin in range(origins):
            for inner in range(orbitals):
                orbital = meta[2 + origin] * orbitals + inner
                local = origin * orbitals + inner
                wanted = jnp.logical_and(
                    any_kept(orbital, first_row, row_blocks), any_kept(orbital, first_col, col_blocks)
                )

                @pl.when(wanted)
                def _(orbital=orbital, local=local, origin=origin):
                    for held, first, blocks in ((lhs, first_row, row_blocks), (rhs, first_col, col_blocks)):
                        def step(block, carry, held=held, first=first):
                            item = place(orbital, first + block)
                            columns = pl.ds(pl.multiple_of(block * BLK, BLK), BLK)

                            @pl.when(item >= 0)
                            def _():
                                for aux in range(per_origin):
                                    copy = pltpu.make_async_copy(
                                        sources[origin * per_origin + aux].at[item],
                                        held.at[local, aux, :, columns],
                                        in_sem,
                                    )
                                    if finish:
                                        copy.wait()
                                    else:
                                        copy.start()

                            if not finish:
                                @pl.when(item < 0)
                                def _():
                                    held[local, :, :, columns] = jnp.zeros(
                                        (per_origin, OBLK, BLK), held.dtype
                                    )
                            return carry

                        lax.fori_loop(0, blocks, step, 0)

    transfers(False)
    transfers(True)
    depth = per_origin * OBLK
    height = row_tile * BLK
    width = col_tile * BLK
    row_tiles = row_blocks // row_tile

    def leaving(tile):
        slot = lax.rem(tile, 2)
        return pltpu.make_async_copy(
            acc.at[slot],
            out.at[pl.ds(pl.multiple_of(tile * height, height), height)],
            out_sem.at[slot],
        )

    def row_step(tile, carry):
        slot = lax.rem(tile, 2)

        @pl.when(tile >= 2)
        def _():
            leaving(tile - 2).wait()

        acc[slot] = jnp.zeros(acc.shape[1:], acc.dtype)

        def orbital_step(local, carry):
            orbital = meta[2 + local // orbitals] * orbitals + lax.rem(local, orbitals)

            @pl.when(any_kept(orbital, first_row + tile * row_tile, row_tile))
            def _():
                rows = pl.ds(pl.multiple_of(tile * height, height), height)
                left = lhs[local, :, :, rows].reshape(depth, height)
                for col in range(col_blocks // col_tile):
                    @pl.when(any_kept(orbital, first_col + col * col_tile, col_tile))
                    def _():
                        span = slice(col * width, (col + 1) * width)
                        right = rhs[local, :, :, span].reshape(depth, width)
                        acc[slot, :, span] += lax.dot_general(
                            left, right, (((0,), (0,)), ((), ())), preferred_element_type=jnp.float32
                        )

            return carry

        lax.fori_loop(0, origins * orbitals, orbital_step, 0)
        leaving(tile).start()
        return carry

    lax.fori_loop(0, row_tiles, row_step, 0)
    for tile in range(max(0, row_tiles - 2), row_tiles):
        leaving(tile).wait()


def product(pos, meta, sources, origins, orbitals, row_blocks, col_blocks):
    per_origin = len(sources) // origins
    rows, cols = row_blocks * BLK, col_blocks * BLK
    row_tile = 2 if row_blocks % 2 == 0 else 1
    total = origins * orbitals
    return pl.pallas_call(
        functools.partial(product_kernel, origins, orbitals, row_blocks, col_blocks),
        grid_spec=pltpu.PrefetchScalarGridSpec(
            num_scalar_prefetch=2,
            grid=(),
            in_specs=[pl.BlockSpec(memory_space=pl.ANY)] * len(sources),
            out_specs=pl.BlockSpec(memory_space=pl.ANY),
            scratch_shapes=[
                pltpu.VMEM((total, per_origin, OBLK, rows), jnp.bfloat16),
                pltpu.VMEM((total, per_origin, OBLK, cols), jnp.bfloat16),
                pltpu.VMEM((2, row_tile * BLK, cols), jnp.float32),
                pltpu.SemaphoreType.DMA(()),
                pltpu.SemaphoreType.DMA((2,)),
            ],
        ),
        out_shape=jax.ShapeDtypeStruct((rows, cols), jnp.float32),
        compiler_params=pltpu.CompilerParams(vmem_limit_bytes=48 * 1024 * 1024),
        cost_estimate=pl.CostEstimate(
            flops=2 * rows * cols * total * per_origin * OBLK,
            bytes_accessed=4 * rows * cols + 2 * total * per_origin * OBLK * (rows + cols),
            transcendentals=0,
        ),
        name="product",
    )(pos, meta, *sources)


def on_device(shape, factors, block_mask, block_lists):
    aux_count, occ_count = shape["aux"], shape["occ"]
    orbitals, slots = block_lists.shape
    aux, occ = lax.axis_index("aux"), lax.axis_index("occ")
    row_blocks, col_blocks = NB // aux_count, NB // occ_count
    kept = block_mask.T > 0
    earlier = jnp.arange(NB)[None, :] < jnp.arange(NB)[:, None]
    rank = jnp.sum(kept[:, None, :] & earlier[None], axis=2, dtype=jnp.int32)
    shift = (jnp.arange(kept.shape[0], dtype=jnp.int32) % orbitals * slots)[:, None]
    pos = jnp.where(kept, rank + shift, -1).reshape(-1)
    own = pick(factors, block_lists)

    if aux_count == 4 and occ_count == 4:
        up = [(z, z + 1) for z in range(3)]
        down = [(z + 1, z) for z in range(3)]
        ups, downs = [own], [own]
        for _ in range(3):
            ups.append(lax.ppermute(ups[-1], "occ", up))
            downs.append(lax.ppermute(downs[-1], "occ", down))
        merged = [
            own,
            jnp.where(occ == 0, downs[1], ups[1]),
            jnp.where(occ == 0, downs[2], jnp.where(occ == 3, ups[2], downs[1])),
            jnp.where(
                occ == 0, downs[3], jnp.where(occ == 1, downs[2], jnp.where(occ == 2, ups[2], ups[3]))
            ),
        ]
        arrival = jnp.array([[0, 1, 2, 3], [1, 0, 2, 3], [2, 1, 3, 0], [3, 2, 1, 0]], jnp.int32)
        origin_of = lax.dynamic_index_in_dim(arrival, occ, 0, keepdims=False)
        over_x = [(0, 2), (2, 0), (1, 3), (3, 1)]
        over_core = [(0, 1), (1, 0), (2, 3), (3, 2)]
        sources = []
        for held in merged:
            far = lax.ppermute(held, "aux", over_x)
            sources += [
                held, far, lax.ppermute(held, "aux", over_core), lax.ppermute(far, "aux", over_core)
            ]
    else:
        everything = lax.all_gather(lax.all_gather(own, "aux"), "occ")
        sources = [everything[z, a] for z in range(occ_count) for a in range(aux_count)]
        origin_of = jnp.arange(occ_count, dtype=jnp.int32)
    meta = jnp.concatenate(
        [jnp.stack([aux * row_blocks, occ * col_blocks]).astype(jnp.int32), origin_of]
    )
    return product(pos, meta, sources, occ_count, orbitals, row_blocks, col_blocks)


def solution(mesh):
    placed = (P(("parts", "aux"), "occ", None), P("parts", None), P(("parts", "occ"), None))
    return jax.shard_map(
        functools.partial(on_device, dict(mesh.shape)),
        mesh=mesh,
        in_specs=placed,
        out_specs=P(("parts", "aux"), "occ"),
        check_vma=False,
    )
```

```python
import functools

import jax
import jax.numpy as jnp
from jax import lax
from jax.experimental import pallas as pl
from jax.experimental.pallas import tpu as pltpu
from jax.sharding import PartitionSpec as P

BLK = 128
OBLK = 112
NB = 48


def pick_kernel(lists, factors, items):
    orbitals, slots = lists.shape

    def step(slot, carry):
        for orbital in range(orbitals):
            block = jnp.maximum(lists[orbital, slot], 0)
            columns = pl.ds(pl.multiple_of(block * BLK, BLK), BLK)
            rows = slice(orbital * OBLK, (orbital + 1) * OBLK)
            items[orbital * slots + slot] = factors[0, rows, columns]
        return carry

    lax.fori_loop(0, slots, step, 0)


def pick(factors, block_lists):
    orbitals, slots = block_lists.shape
    count = orbitals * slots
    return pl.pallas_call(
        pick_kernel,
        grid_spec=pltpu.PrefetchScalarGridSpec(
            num_scalar_prefetch=1,
            grid=(),
            in_specs=[pl.BlockSpec(memory_space=pltpu.VMEM)],
            out_specs=pl.BlockSpec(memory_space=pltpu.VMEM),
        ),
        out_shape=jax.ShapeDtypeStruct((count, OBLK, BLK), factors.dtype),
        compiler_params=pltpu.CompilerParams(vmem_limit_bytes=16 * 1024 * 1024),
        cost_estimate=pl.CostEstimate(
            flops=0, bytes_accessed=4 * count * OBLK * BLK, transcendentals=0
        ),
        name="pick",
    )(block_lists, factors)


def choose_kernel(which, *refs):
    choices, out, sem = refs[:-2], refs[-2], refs[-1]
    for index, choice in enumerate(choices):
        @pl.when(which[0] == index)
        def _():
            copy = pltpu.make_async_copy(choice, out, sem)
            copy.start()
            copy.wait()


def choose(which, choices):
    shape = jax.ShapeDtypeStruct(choices[0].shape, choices[0].dtype)
    return pl.pallas_call(
        choose_kernel,
        grid_spec=pltpu.PrefetchScalarGridSpec(
            num_scalar_prefetch=1,
            grid=(),
            in_specs=[pl.BlockSpec(memory_space=pl.ANY)] * len(choices),
            out_specs=pl.BlockSpec(memory_space=pltpu.VMEM),
            scratch_shapes=[pltpu.SemaphoreType.DMA(())],
        ),
        out_shape=shape,
        compiler_params=pltpu.CompilerParams(vmem_limit_bytes=16 * 1024 * 1024),
        cost_estimate=pl.CostEstimate(flops=0, bytes_accessed=4 * shape.size, transcendentals=0),
        name="choose",
    )(which.reshape(1).astype(jnp.int32), *choices)


def product_kernel(origins, orbitals, row_blocks, col_blocks, pos, meta, *refs):
    sources = refs[: -6]
    out, lhs, rhs, acc, in_sem, out_sem = refs[-6:]
    per_origin = len(sources) // origins
    row_tile = 2 if row_blocks % 2 == 0 else 1
    col_tile = 4 if col_blocks % 4 == 0 else 3 if col_blocks % 3 == 0 else 1
    first_row, first_col = meta[0], meta[1]

    def place(orbital, block):
        return pos[orbital * NB + block]

    def any_kept(orbital, first, count):
        best = place(orbital, first)
        for step in range(1, count):
            best = jnp.maximum(best, place(orbital, first + step))
        return best >= 0

    def transfers(finish):
        for origin in range(origins):
            for inner in range(orbitals):
                orbital = meta[2 + origin] * orbitals + inner
                local = origin * orbitals + inner
                wanted = jnp.logical_and(
                    any_kept(orbital, first_row, row_blocks), any_kept(orbital, first_col, col_blocks)
                )

                @pl.when(wanted)
                def _(orbital=orbital, local=local, origin=origin):
                    for held, first, blocks in ((lhs, first_row, row_blocks), (rhs, first_col, col_blocks)):
                        def step(block, carry, held=held, first=first):
                            item = place(orbital, first + block)
                            columns = pl.ds(pl.multiple_of(block * BLK, BLK), BLK)

                            @pl.when(item >= 0)
                            def _():
                                for aux in range(per_origin):
                                    copy = pltpu.make_async_copy(
                                        sources[origin * per_origin + aux].at[item],
                                        held.at[local, aux, :, columns],
                                        in_sem,
                                    )
                                    if finish:
                                        copy.wait()
                                    else:
                                        copy.start()

                            if not finish:
                                @pl.when(item < 0)
                                def _():
                                    held[local, :, :, columns] = jnp.zeros(
                                        (per_origin, OBLK, BLK), held.dtype
                                    )
                            return carry

                        lax.fori_loop(0, blocks, step, 0)

    transfers(False)
    transfers(True)
    depth = per_origin * OBLK
    height = row_tile * BLK
    width = col_tile * BLK
    row_tiles = row_blocks // row_tile

    def leaving(tile):
        slot = lax.rem(tile, 2)
        return pltpu.make_async_copy(
            acc.at[slot],
            out.at[pl.ds(pl.multiple_of(tile * height, height), height)],
            out_sem.at[slot],
        )

    def row_step(tile, carry):
        slot = lax.rem(tile, 2)

        @pl.when(tile >= 2)
        def _():
            leaving(tile - 2).wait()

        acc[slot] = jnp.zeros(acc.shape[1:], acc.dtype)

        def orbital_step(local, carry):
            orbital = meta[2 + local // orbitals] * orbitals + lax.rem(local, orbitals)

            @pl.when(any_kept(orbital, first_row + tile * row_tile, row_tile))
            def _():
                rows = pl.ds(pl.multiple_of(tile * height, height), height)
                left = lhs[local, :, :, rows].reshape(depth, height)
                for col in range(col_blocks // col_tile):
                    @pl.when(any_kept(orbital, first_col + col * col_tile, col_tile))
                    def _():
                        span = slice(col * width, (col + 1) * width)
                        right = rhs[local, :, :, span].reshape(depth, width)
                        acc[slot, :, span] += lax.dot_general(
                            left, right, (((0,), (0,)), ((), ())), preferred_element_type=jnp.float32
                        )

            return carry

        lax.fori_loop(0, origins * orbitals, orbital_step, 0)
        leaving(tile).start()
        return carry

    lax.fori_loop(0, row_tiles, row_step, 0)
    for tile in range(max(0, row_tiles - 2), row_tiles):
        leaving(tile).wait()


def product(pos, meta, sources, origins, orbitals, row_blocks, col_blocks):
    per_origin = len(sources) // origins
    rows, cols = row_blocks * BLK, col_blocks * BLK
    row_tile = 2 if row_blocks % 2 == 0 else 1
    total = origins * orbitals
    return pl.pallas_call(
        functools.partial(product_kernel, origins, orbitals, row_blocks, col_blocks),
        grid_spec=pltpu.PrefetchScalarGridSpec(
            num_scalar_prefetch=2,
            grid=(),
            in_specs=[pl.BlockSpec(memory_space=pl.ANY)] * len(sources),
            out_specs=pl.BlockSpec(memory_space=pl.ANY),
            scratch_shapes=[
                pltpu.VMEM((total, per_origin, OBLK, rows), jnp.bfloat16),
                pltpu.VMEM((total, per_origin, OBLK, cols), jnp.bfloat16),
                pltpu.VMEM((2, row_tile * BLK, cols), jnp.float32),
                pltpu.SemaphoreType.DMA(()),
                pltpu.SemaphoreType.DMA((2,)),
            ],
        ),
        out_shape=jax.ShapeDtypeStruct((rows, cols), jnp.float32),
        compiler_params=pltpu.CompilerParams(vmem_limit_bytes=48 * 1024 * 1024),
        cost_estimate=pl.CostEstimate(
            flops=2 * rows * cols * total * per_origin * OBLK,
            bytes_accessed=4 * rows * cols + 2 * total * per_origin * OBLK * (rows + cols),
            transcendentals=0,
        ),
        name="product",
    )(pos, meta, *sources)


def on_device(shape, factors, block_mask, block_lists):
    aux_count, occ_count = shape["aux"], shape["occ"]
    orbitals, slots = block_lists.shape
    aux, occ = lax.axis_index("aux"), lax.axis_index("occ")
    row_blocks, col_blocks = NB // aux_count, NB // occ_count
    kept = block_mask.T > 0
    earlier = jnp.arange(NB)[None, :] < jnp.arange(NB)[:, None]
    rank = jnp.sum(kept[:, None, :] & earlier[None], axis=2, dtype=jnp.int32)
    shift = (jnp.arange(kept.shape[0], dtype=jnp.int32) % orbitals * slots)[:, None]
    pos = jnp.where(kept, rank + shift, -1).reshape(-1)
    own = pick(factors, block_lists)

    if aux_count == 4 and occ_count == 4:
        up = [(z, z + 1) for z in range(3)]
        down = [(z + 1, z) for z in range(3)]
        ups, downs = [own], [own]
        for _ in range(3):
            ups.append(lax.ppermute(ups[-1], "occ", up))
            downs.append(lax.ppermute(downs[-1], "occ", down))
        merged = [
            own,
            choose(jnp.minimum(occ, 1), [downs[1], ups[1]]),
            choose(jnp.array([0, 1, 1, 2], jnp.int32)[occ], [downs[2], downs[1], ups[2]]),
            choose(occ, [downs[3], downs[2], ups[2], ups[3]]),
        ]
        arrival = jnp.array([[0, 1, 2, 3], [1, 0, 2, 3], [2, 1, 3, 0], [3, 2, 1, 0]], jnp.int32)
        origin_of = lax.dynamic_index_in_dim(arrival, occ, 0, keepdims=False)
        over_x = [(0, 2), (2, 0), (1, 3), (3, 1)]
        over_core = [(0, 1), (1, 0), (2, 3), (3, 2)]
        sources = []
        for held in merged:
            far = lax.ppermute(held, "aux", over_x)
            sources += [
                held, far, lax.ppermute(held, "aux", over_core), lax.ppermute(far, "aux", over_core)
            ]
    else:
        everything = lax.all_gather(lax.all_gather(own, "aux"), "occ")
        sources = [everything[z, a] for z in range(occ_count) for a in range(aux_count)]
        origin_of = jnp.arange(occ_count, dtype=jnp.int32)
    meta = jnp.concatenate(
        [jnp.stack([aux * row_blocks, occ * col_blocks]).astype(jnp.int32), origin_of]
    )
    return product(pos, meta, sources, occ_count, orbitals, row_blocks, col_blocks)


def solution(mesh):
    placed = (P(("parts", "aux"), "occ", None), P("parts", None), P(("parts", "occ"), None))
    return jax.shard_map(
        functools.partial(on_device, dict(mesh.shape)),
        mesh=mesh,
        in_specs=placed,
        out_specs=P(("parts", "aux"), "occ"),
        check_vma=False,
    )
```

```python
import functools

import jax
import jax.numpy as jnp
from jax import lax
from jax.experimental import pallas as pl
from jax.experimental.pallas import tpu as pltpu
from jax.sharding import PartitionSpec as P

BLK = 128
OBLK = 112
NB = 48
NOB = 8
PLACES = NOB * NB
STRIDE = 64
ROUNDS = 5
HOPS = ROUNDS - 1
LEVELS = (12, 14, 16, 17, 18, 20, 24, 48)
MIB = 1024 * 1024


def pick_kernel(lists, factors, items):
    orbitals, slots = lists.shape

    def step(slot, carry):
        for orbital in range(orbitals):
            block = jnp.maximum(lists[orbital, slot], 0)
            columns = pl.ds(pl.multiple_of(block * BLK, BLK), BLK)
            rows = slice(orbital * OBLK, (orbital + 1) * OBLK)
            items[orbital * slots + slot] = factors[0, rows, columns]
        return carry

    lax.fori_loop(0, slots, step, 0)


def pick(factors, block_lists):
    orbitals, slots = block_lists.shape
    count = orbitals * slots
    return pl.pallas_call(
        pick_kernel,
        grid_spec=pltpu.PrefetchScalarGridSpec(
            num_scalar_prefetch=1,
            grid=(),
            in_specs=[pl.BlockSpec(memory_space=pltpu.VMEM)],
            out_specs=pl.BlockSpec(memory_space=pltpu.VMEM),
        ),
        out_shape=jax.ShapeDtypeStruct((count, OBLK, BLK), factors.dtype),
        compiler_params=pltpu.CompilerParams(vmem_limit_bytes=16 * MIB),
        cost_estimate=pl.CostEstimate(
            flops=0, bytes_accessed=4 * count * OBLK * BLK, transcendentals=0
        ),
        name="pick",
    )(block_lists, factors)


def as_number(condition):
    return jnp.where(condition, 1.0, 0.0)


def place_facts(shape, axis):
    place = lax.broadcasted_iota(jnp.int32, shape, axis).astype(jnp.float32)
    orbital = jnp.floor((place + 0.5) / NB)
    block = place - NB * orbital
    quarter = jnp.floor((block + 0.5) / (NB // 4))
    return place, orbital, quarter, jnp.floor((quarter + 0.5) / 2), jnp.floor((orbital + 0.5) / 2)


def plan_kernel(slots, where, masks, out):
    levels = len(LEVELS)
    rows = 2 * levels
    wide = (rows, PLACES)
    _, orbital, quarter, half, origin = place_facts(wide, 1)
    row = lax.broadcasted_iota(jnp.int32, wide, 0)
    kept = jnp.where(row < levels, masks[0:1, :], masks[1:2, :])
    capacity = jnp.zeros(wide, jnp.float32)
    for index, size in enumerate(LEVELS):
        capacity = jnp.where((row == index) | (row == index + levels), float(size), capacity)

    square = (PLACES, PLACES)
    down_place, down_orbital, _, _, _ = place_facts(square, 0)
    over_place, over_orbital, _, _, _ = place_facts(square, 1)
    same = as_number(down_orbital == over_orbital)
    before = as_number(down_place < over_place)
    within = (same * before).astype(jnp.bfloat16)
    same, before = same.astype(jnp.bfloat16), before.astype(jnp.bfloat16)

    def times(parts, matrix):
        stacked = jnp.concatenate(parts, axis=0).astype(jnp.bfloat16)
        product = jnp.dot(stacked, matrix, preferred_element_type=jnp.float32)
        return [product[index * rows:(index + 1) * rows] for index in range(len(parts))]

    touching = times([kept * as_number(quarter == z) for z in range(4)], same)
    need = [kept * as_number(touch > 0) for touch in touching]
    zero = jnp.zeros(wide, jnp.float32)

    def union(parts):
        best = zero
        for part in parts:
            best = jnp.maximum(best, part)
        return best

    x_need = []
    for x in range(2):
        touched = as_number(touching[2 * x] + touching[2 * x + 1] > 0)
        here = as_number(half == x)
        x_need.append([
            need[z] * jnp.maximum(here, as_number(quarter == z) * touched) for z in range(4)
        ])
    mine = [kept * as_number(origin == z) for z in range(4)]
    need_up = [union(need[z + 1:]) for z in range(4)]
    far_up = [union(need[z + 2:]) for z in range(4)]
    need_down = [union(need[:z]) for z in range(4)]
    far_down = [union(need[:max(z - 1, 0)]) for z in range(4)]
    up = [mine[z] * need_up[z] for z in range(4)]
    down = [mine[z] * need_down[z] for z in range(4)]
    cross = [[mine[z] * x_need[x][z] for z in range(4)] for x in range(2)]
    up_code, down_code = [zero] * 4, [zero] * 4
    cross_code = [[zero] * 4, [zero] * 4]

    for turn in range(ROUNDS):
        parts = []
        if turn < HOPS:
            for z in range(3):
                parts += [up[z] * far_up[z], up[z] - up[z] * far_up[z]]
                parts += [down[z + 1] * far_down[z + 1], down[z + 1] - down[z + 1] * far_down[z + 1]]
        parts += [cross[x][z] for x in range(2) for z in range(4)]
        ranks = iter(zip(parts, times(parts, before)))

        def taken(pairs):
            rank, total = zero, 0.0
            chosen = zero
            for part, counted in pairs:
                rank = rank + part * (counted + total)
                total = total + jnp.sum(part, axis=1, keepdims=True)
                chosen = chosen + part
            chosen = chosen * as_number(rank < capacity)
            return chosen, chosen * (rank + float(turn * STRIDE + 1))

        up_sent, down_sent = [], []
        if turn < HOPS:
            for z in range(3):
                sent, code = taken([next(ranks), next(ranks)])
                up_sent.append(sent)
                up_code[z] = up_code[z] + code
                up[z] = up[z] - sent
                sent, code = taken([next(ranks), next(ranks)])
                down_sent.append(sent)
                down_code[z + 1] = down_code[z + 1] + code
                down[z + 1] = down[z + 1] - sent
        for x in range(2):
            for z in range(4):
                sent, code = taken([next(ranks)])
                cross_code[x][z] = cross_code[x][z] + code
                cross[x][z] = cross[x][z] - sent
        if turn < HOPS:
            for z in range(3):
                up[z + 1] = up[z + 1] + up_sent[z] * need_up[z + 1]
                down[z] = down[z] + down_sent[z] * need_down[z]
                for x in range(2):
                    cross[x][z + 1] = cross[x][z + 1] + up_sent[z] * x_need[x][z + 1]
                    cross[x][z] = cross[x][z] + down_sent[z] * x_need[x][z]

    left = zero
    for part in up + down + cross[0] + cross[1]:
        left = left + part
    left = jnp.sum(left, axis=1, keepdims=True)
    left = left[:levels] + left[levels:]
    order = lax.broadcasted_iota(jnp.int32, (levels, 1), 0).astype(jnp.float32)
    level = jnp.min(jnp.where(left > 0, float(levels - 1), order), axis=0, keepdims=True)
    level_row = as_number(
        lax.broadcasted_iota(jnp.int32, (levels, PLACES), 0).astype(jnp.float32) == level
    )
    me_x, me_z = where[0], where[1]

    def at(parts, z):
        total = jnp.zeros((levels, PLACES), jnp.float32)
        for index, part in enumerate(parts):
            total = total + jnp.where(z == index, 1.0, 0.0) * part[:levels]
        return jnp.sum(total * level_row, axis=0, keepdims=True)

    cross_here = [jnp.where(me_x == 0, cross_code[0][z], cross_code[1][z]) for z in range(4)]
    cross_there = [jnp.where(me_x == 0, cross_code[1][z], cross_code[0][z]) for z in range(4)]
    def turn_of(code):
        return jnp.floor((code - 0.5) / STRIDE)

    got_up, got_down = at(up_code, me_z - 1), at(down_code, me_z + 1)
    got_cross = at(cross_here, me_z)
    inner = jnp.dot(kept.astype(jnp.bfloat16), within, preferred_element_type=jnp.float32)[0:1]
    one_orbital, one_origin = orbital[0:1], origin[0:1]
    slot = inner + slots * (one_orbital - 2 * one_origin)
    owned = kept[0:1] * as_number(one_origin == me_z.astype(jnp.float32))
    held = (
        owned * (slot + 1)
        + as_number(got_up > 0) * (got_up + STRIDE * (1 + turn_of(got_up)))
        + as_number(got_down > 0) * (got_down + STRIDE * (2 + turn_of(got_down)))
        - 1
    )
    crossed = got_cross - 1

    buffer = jnp.floor((held + 0.5) / STRIDE)
    tall = (PLACES, PLACES)
    target = lax.broadcasted_iota(jnp.int32, tall, 0).astype(jnp.float32) + 1
    pair = jnp.concatenate([buffer, held - STRIDE * buffer] + [jnp.zeros_like(held)] * 6, axis=0)
    lists = []
    for parts in (up_code, down_code, cross_there):
        sent = at(parts, me_z)
        chosen = as_number(target == sent).astype(jnp.bfloat16)
        both = lax.dot_general(
            pair.astype(jnp.bfloat16), chosen, (((1,), (1,)), ((), ())),
            preferred_element_type=jnp.float32,
        )
        lists.append(both[0:1] * STRIDE + both[1:2])
    flat = level + jnp.zeros((1, PLACES), jnp.float32)
    result = jnp.concatenate(lists + [held, crossed, flat, flat, flat], axis=0)
    out[...] = result.astype(jnp.int32)


def plan(where, masks, slots):
    return pl.pallas_call(
        functools.partial(plan_kernel, slots),
        grid_spec=pltpu.PrefetchScalarGridSpec(
            num_scalar_prefetch=1,
            grid=(),
            in_specs=[pl.BlockSpec(memory_space=pltpu.VMEM)],
            out_specs=pl.BlockSpec(memory_space=pltpu.VMEM),
        ),
        out_shape=jax.ShapeDtypeStruct((8, PLACES), jnp.int32),
        compiler_params=pltpu.CompilerParams(vmem_limit_bytes=32 * MIB),
        name="plan",
    )(where, masks)


def branch(which, low, high, run):
    if high - low == 1:
        run(low)
        return
    middle = (low + high) // 2

    @pl.when(which < middle)
    def _():
        branch(which, low, middle, run)

    @pl.when(which >= middle)
    def _():
        branch(which, middle, high, run)


def gather_kernel(turn, held, streams, table, *refs):
    buffers, outs, sems = refs[:held], refs[-1 - streams:-1], refs[-1]
    size = outs[0].shape[0]

    def step(index, carry):
        for stream in range(streams):
            row = stream if streams == 3 else 2
            code = table[row * PLACES + turn * STRIDE + index]
            branch(
                code // STRIDE, 0, held,
                lambda n, stream=stream, code=code: pltpu.make_async_copy(
                    buffers[n].at[lax.rem(code, STRIDE)], outs[stream].at[index], sems.at[stream]
                ).start(),
            )
        return carry

    lax.fori_loop(0, size, step, 0)
    for stream in range(streams):
        pltpu.make_async_copy(outs[stream], outs[stream], sems.at[stream]).wait()


def gather(turn, size, table, buffers, after):
    streams = 3 if turn < HOPS else 1
    shape = jax.ShapeDtypeStruct((size, OBLK, BLK), buffers[0].dtype)
    return pl.pallas_call(
        functools.partial(gather_kernel, turn, len(buffers), streams),
        grid_spec=pltpu.PrefetchScalarGridSpec(
            num_scalar_prefetch=1,
            grid=(),
            in_specs=[pl.BlockSpec(memory_space=pl.ANY)] * (len(buffers) + len(after)),
            out_specs=[pl.BlockSpec(memory_space=pltpu.VMEM)] * streams,
            scratch_shapes=[pltpu.SemaphoreType.DMA((streams,))],
        ),
        out_shape=[shape] * streams,
        compiler_params=pltpu.CompilerParams(vmem_limit_bytes=16 * MIB),
        cost_estimate=pl.CostEstimate(
            flops=0, bytes_accessed=4 * streams * size * OBLK * BLK, transcendentals=0
        ),
        name="gather",
    )(table, *buffers, *after)


def product_kernel(groups, orbitals, row_blocks, col_blocks, loc, meta, *refs):
    flat = iter(refs[:-6])
    sources = [[[next(flat) for _ in range(aux)] for _ in range(count)] for count, aux in groups]
    out, lhs, rhs, acc, in_sem, out_sem = refs[-6:]
    total_aux = sum(aux for _, aux in groups)
    row_tile = 2 if row_blocks % 2 == 0 else 1
    col_tile = 4 if col_blocks % 4 == 0 else 3 if col_blocks % 3 == 0 else 1
    first_row, first_col = meta[0], meta[1]
    depth = total_aux * OBLK
    height = row_tile * BLK
    width = col_tile * BLK
    row_tiles = row_blocks // row_tile

    def code_of(group, orbital, block):
        return loc[group * PLACES + orbital * NB + block]

    def any_kept(orbital, first, count):
        best = code_of(0, orbital, first)
        for step in range(1, count):
            best = jnp.maximum(best, code_of(0, orbital, first + step))
        return best >= 0

    def transfers(finish):
        def one(orbital, carry):
            wanted = jnp.logical_and(
                any_kept(orbital, first_row, row_blocks), any_kept(orbital, first_col, col_blocks)
            )

            @pl.when(wanted)
            def _():
                for held, first, blocks in ((lhs, first_row, row_blocks), (rhs, first_col, col_blocks)):
                    def step(block, carry, held=held, first=first):
                        code = code_of(0, orbital, first + block)
                        columns = pl.ds(pl.multiple_of(block * BLK, BLK), BLK)

                        @pl.when(code >= 0)
                        def _():
                            start_aux = 0
                            for group, (count, aux_count) in enumerate(groups):
                                place = code_of(group, orbital, first + block)

                                def run(n, group=group, place=place, start_aux=start_aux, aux_count=aux_count):
                                    for aux in range(aux_count):
                                        copy = pltpu.make_async_copy(
                                            sources[group][n][aux].at[lax.rem(place, STRIDE)],
                                            held.at[orbital, start_aux + aux, :, columns],
                                            in_sem,
                                        )
                                        if finish:
                                            copy.wait()
                                        else:
                                            copy.start()

                                if finish:
                                    run(0)
                                else:
                                    branch(place // STRIDE, 0, count, run)
                                start_aux += aux_count

                        if not finish:
                            @pl.when(code < 0)
                            def _():
                                held[orbital, :, :, columns] = jnp.zeros(
                                    (total_aux, OBLK, BLK), held.dtype
                                )
                        return carry

                    lax.fori_loop(0, blocks, step, 0)
            return carry

        lax.fori_loop(0, orbitals, one, 0)

    transfers(False)
    transfers(True)

    def leaving(tile):
        slot = lax.rem(tile, 2)
        return pltpu.make_async_copy(
            acc.at[slot],
            out.at[pl.ds(pl.multiple_of(tile * height, height), height)],
            out_sem.at[slot],
        )

    def row_step(tile, carry):
        slot = lax.rem(tile, 2)

        @pl.when(tile >= 2)
        def _():
            leaving(tile - 2).wait()

        acc[slot] = jnp.zeros(acc.shape[1:], acc.dtype)

        def orbital_step(orbital, carry):
            wanted = jnp.logical_and(
                any_kept(orbital, first_row + tile * row_tile, row_tile),
                any_kept(orbital, first_col, col_blocks),
            )

            @pl.when(wanted)
            def _():
                rows = pl.ds(pl.multiple_of(tile * height, height), height)
                left = lhs[orbital, :, :, rows].reshape(depth, height).T
                for col in range(col_blocks // col_tile):
                    @pl.when(any_kept(orbital, first_col + col * col_tile, col_tile))
                    def _():
                        span = slice(col * width, (col + 1) * width)
                        right = rhs[orbital, :, :, span].reshape(depth, width)
                        acc[slot, :, span] += jnp.dot(
                            left, right, preferred_element_type=jnp.float32
                        )

            return carry

        lax.fori_loop(0, orbitals, orbital_step, 0)
        leaving(tile).start()
        return carry

    lax.fori_loop(0, row_tiles, row_step, 0)
    for tile in range(max(0, row_tiles - 2), row_tiles):
        leaving(tile).wait()


def product(loc, meta, sources, orbitals, row_blocks, col_blocks):
    groups = [(len(group), len(group[0])) for group in sources]
    flat = [ref for group in sources for refs in group for ref in refs]
    total_aux = sum(aux for _, aux in groups)
    rows, cols = row_blocks * BLK, col_blocks * BLK
    row_tile = 2 if row_blocks % 2 == 0 else 1
    return pl.pallas_call(
        functools.partial(product_kernel, groups, orbitals, row_blocks, col_blocks),
        grid_spec=pltpu.PrefetchScalarGridSpec(
            num_scalar_prefetch=2,
            grid=(),
            in_specs=[pl.BlockSpec(memory_space=pl.ANY)] * len(flat),
            out_specs=pl.BlockSpec(memory_space=pl.ANY),
            scratch_shapes=[
                pltpu.VMEM((orbitals, total_aux, OBLK, rows), jnp.bfloat16),
                pltpu.VMEM((orbitals, total_aux, OBLK, cols), jnp.bfloat16),
                pltpu.VMEM((2, row_tile * BLK, cols), jnp.float32),
                pltpu.SemaphoreType.DMA(()),
                pltpu.SemaphoreType.DMA((2,)),
            ],
        ),
        out_shape=jax.ShapeDtypeStruct((rows, cols), jnp.float32),
        compiler_params=pltpu.CompilerParams(vmem_limit_bytes=40 * MIB),
        cost_estimate=pl.CostEstimate(
            flops=2 * rows * cols * orbitals * total_aux * OBLK,
            bytes_accessed=4 * rows * cols + 2 * orbitals * total_aux * OBLK * (rows + cols),
            transcendentals=0,
        ),
        name="product",
    )(loc, meta, *flat)


def rounds(size, finish, table, own):
    upward = [(z, z + 1) for z in range(3)]
    downward = [(z + 1, z) for z in range(3)]

    def to_core(held):
        return lax.ppermute(held, "aux", [(0, 1), (1, 0), (2, 3), (3, 2)])

    def arrived(first, second):
        return [held for pair in zip(first, second) for held in pair]

    ups, downs, crossed = [], [], []
    core_ups, core_downs, core_crossed = [], [], []
    core_own = to_core(own)
    for turn in range(ROUNDS):
        after = crossed[-1:]
        if turn >= 2:
            after = after + [core_ups[turn - 2], core_downs[turn - 2], core_crossed[turn - 2]]
        if turn == 1:
            after = after + [core_own]
        chunks = gather(turn, size, table, [own] + arrived(ups, downs), after)
        if turn < HOPS:
            ups.append(lax.ppermute(chunks[0], "occ", upward))
            downs.append(lax.ppermute(chunks[1], "occ", downward))
        crossed.append(lax.ppermute(chunks[-1], "aux", [(0, 2), (2, 0), (1, 3), (3, 1)]))
        if turn < HOPS:
            core_ups.append(to_core(ups[-1]))
            core_downs.append(to_core(downs[-1]))
        core_crossed.append(to_core(crossed[-1]))
    near = list(zip([own] + arrived(ups, downs), [core_own] + arrived(core_ups, core_downs)))
    return finish(table[3 * PLACES:5 * PLACES], [near, list(zip(crossed, core_crossed))])


def on_device(shape, factors, block_mask, block_lists):
    aux_count, occ_count = shape["aux"], shape["occ"]
    own_orbitals, slots = block_lists.shape
    aux, occ = lax.axis_index("aux"), lax.axis_index("occ")
    row_blocks, col_blocks = NB // aux_count, NB // occ_count
    meta = jnp.stack([aux * row_blocks, occ * col_blocks]).astype(jnp.int32)

    def finish(loc, sources):
        return product(loc, meta, sources, NOB, row_blocks, col_blocks)

    kept = block_mask.T > 0
    own = pick(factors, block_lists)
    if aux_count == 4 and occ_count == 4 and shape["parts"] == 2:
        mask = as_number(kept).reshape(1, PLACES)
        other = lax.ppermute(mask, "parts", [(0, 1), (1, 0)])
        where = jnp.stack([aux // 2, occ]).astype(jnp.int32)
        table = plan(where, jnp.concatenate([mask, other]), slots)
        return lax.switch(
            table[5, 0],
            [functools.partial(rounds, size, finish) for size in LEVELS],
            table.reshape(-1),
            own,
        )
    everything = lax.all_gather(lax.all_gather(own, "aux"), "occ")
    sources = [[everything[z, a] for a in range(aux_count)] for z in range(occ_count)]
    earlier = jnp.arange(NB)[None, :] < jnp.arange(NB)[:, None]
    rank = jnp.sum(kept[:, None, :] & earlier[None], axis=2, dtype=jnp.int32)
    orbital = jnp.arange(NOB, dtype=jnp.int32)[:, None]
    start = orbital // own_orbitals * STRIDE + orbital % own_orbitals * slots
    return finish(jnp.where(kept, rank + start, -1).reshape(-1), [sources])


def solution(mesh):
    placed = (P(("parts", "aux"), "occ", None), P("parts", None), P(("parts", "occ"), None))
    return jax.shard_map(
        functools.partial(on_device, dict(mesh.shape)),
        mesh=mesh,
        in_specs=placed,
        out_specs=P(("parts", "aux"), "occ"),
        check_vma=False,
    )
```

```python
import functools

import jax
import jax.numpy as jnp
from jax import lax
from jax.experimental import pallas as pl
from jax.experimental.pallas import tpu as pltpu
from jax.sharding import PartitionSpec as P

BLK = 128
OBLK = 112
NB = 48
NOB = 8
PLACES = NOB * NB
STRIDE = 64
ROUNDS = 5
HOPS = ROUNDS - 1
LEVELS = (12, 14, 16, 17, 18, 20, 24, 48)
MIB = 1024 * 1024


def pick_kernel(lists, factors, items):
    orbitals, slots = lists.shape

    def step(slot, carry):
        for orbital in range(orbitals):
            block = jnp.maximum(lists[orbital, slot], 0)
            columns = pl.ds(pl.multiple_of(block * BLK, BLK), BLK)
            rows = slice(orbital * OBLK, (orbital + 1) * OBLK)
            items[orbital * slots + slot] = factors[0, rows, columns]
        return carry

    lax.fori_loop(0, slots, step, 0)


def pick(factors, block_lists):
    orbitals, slots = block_lists.shape
    count = orbitals * slots
    return pl.pallas_call(
        pick_kernel,
        grid_spec=pltpu.PrefetchScalarGridSpec(
            num_scalar_prefetch=1,
            grid=(),
            in_specs=[pl.BlockSpec(memory_space=pltpu.VMEM)],
            out_specs=pl.BlockSpec(memory_space=pltpu.VMEM),
        ),
        out_shape=jax.ShapeDtypeStruct((count, OBLK, BLK), factors.dtype),
        compiler_params=pltpu.CompilerParams(vmem_limit_bytes=16 * MIB),
        cost_estimate=pl.CostEstimate(
            flops=0, bytes_accessed=4 * count * OBLK * BLK, transcendentals=0
        ),
        name="pick",
    )(block_lists, factors)


def as_number(condition):
    return jnp.where(condition, 1.0, 0.0)


def place_facts(shape, axis):
    place = lax.broadcasted_iota(jnp.int32, shape, axis).astype(jnp.float32)
    orbital = jnp.floor((place + 0.5) / NB)
    block = place - NB * orbital
    quarter = jnp.floor((block + 0.5) / (NB // 4))
    return place, orbital, quarter, jnp.floor((quarter + 0.5) / 2), jnp.floor((orbital + 0.5) / 2)


def plan_kernel(slots, where, masks, out):
    levels = len(LEVELS)
    rows = 2 * levels
    wide = (rows, PLACES)
    _, orbital, quarter, half, origin = place_facts(wide, 1)
    row = lax.broadcasted_iota(jnp.int32, wide, 0)
    kept = jnp.where(row < levels, masks[0:1, :], masks[1:2, :])
    capacity = jnp.zeros(wide, jnp.float32)
    for index, size in enumerate(LEVELS):
        capacity = jnp.where((row == index) | (row == index + levels), float(size), capacity)

    square = (PLACES, PLACES)
    down_place, down_orbital, _, _, _ = place_facts(square, 0)
    over_place, over_orbital, _, _, _ = place_facts(square, 1)
    same = as_number(down_orbital == over_orbital)
    before = as_number(down_place < over_place)
    within = (same * before).astype(jnp.bfloat16)
    same, before = same.astype(jnp.bfloat16), before.astype(jnp.bfloat16)

    def times(parts, matrix):
        stacked = jnp.concatenate(parts, axis=0).astype(jnp.bfloat16)
        product = jnp.dot(stacked, matrix, preferred_element_type=jnp.float32)
        return [product[index * rows:(index + 1) * rows] for index in range(len(parts))]

    touching = times([kept * as_number(quarter == z) for z in range(4)], same)
    need = [kept * as_number(touch > 0) for touch in touching]
    zero = jnp.zeros(wide, jnp.float32)

    def union(parts):
        best = zero
        for part in parts:
            best = jnp.maximum(best, part)
        return best

    x_need = []
    for x in range(2):
        touched = as_number(touching[2 * x] + touching[2 * x + 1] > 0)
        here = as_number(half == x)
        x_need.append([
            need[z] * jnp.maximum(here, as_number(quarter == z) * touched) for z in range(4)
        ])
    mine = [kept * as_number(origin == z) for z in range(4)]
    need_up = [union(need[z + 1:]) for z in range(4)]
    far_up = [union(need[z + 2:]) for z in range(4)]
    need_down = [union(need[:z]) for z in range(4)]
    far_down = [union(need[:max(z - 1, 0)]) for z in range(4)]
    up = [mine[z] * need_up[z] for z in range(4)]
    down = [mine[z] * need_down[z] for z in range(4)]
    cross = [[mine[z] * x_need[x][z] for z in range(4)] for x in range(2)]
    up_code, down_code = [zero] * 4, [zero] * 4
    cross_code = [[zero] * 4, [zero] * 4]

    for turn in range(ROUNDS):
        parts = []
        if turn < HOPS:
            for z in range(3):
                parts += [up[z] * far_up[z], up[z] - up[z] * far_up[z]]
                parts += [down[z + 1] * far_down[z + 1], down[z + 1] - down[z + 1] * far_down[z + 1]]
        parts += [cross[x][z] for x in range(2) for z in range(4)]
        ranks = iter(zip(parts, times(parts, before)))

        def taken(pairs):
            rank, total = zero, 0.0
            chosen = zero
            for part, counted in pairs:
                rank = rank + part * (counted + total)
                total = total + jnp.sum(part, axis=1, keepdims=True)
                chosen = chosen + part
            chosen = chosen * as_number(rank < capacity)
            return chosen, chosen * (rank + float(turn * STRIDE + 1))

        up_sent, down_sent = [], []
        if turn < HOPS:
            for z in range(3):
                sent, code = taken([next(ranks), next(ranks)])
                up_sent.append(sent)
                up_code[z] = up_code[z] + code
                up[z] = up[z] - sent
                sent, code = taken([next(ranks), next(ranks)])
                down_sent.append(sent)
                down_code[z + 1] = down_code[z + 1] + code
                down[z + 1] = down[z + 1] - sent
        for x in range(2):
            for z in range(4):
                sent, code = taken([next(ranks)])
                cross_code[x][z] = cross_code[x][z] + code
                cross[x][z] = cross[x][z] - sent
        if turn < HOPS:
            for z in range(3):
                up[z + 1] = up[z + 1] + up_sent[z] * need_up[z + 1]
                down[z] = down[z] + down_sent[z] * need_down[z]
                for x in range(2):
                    cross[x][z + 1] = cross[x][z + 1] + up_sent[z] * x_need[x][z + 1]
                    cross[x][z] = cross[x][z] + down_sent[z] * x_need[x][z]

    left = zero
    for part in up + down + cross[0] + cross[1]:
        left = left + part
    left = jnp.sum(left, axis=1, keepdims=True)
    left = left[:levels] + left[levels:]
    order = lax.broadcasted_iota(jnp.int32, (levels, 1), 0).astype(jnp.float32)
    level = jnp.min(jnp.where(left > 0, float(levels - 1), order), axis=0, keepdims=True)
    level_row = as_number(
        lax.broadcasted_iota(jnp.int32, (levels, PLACES), 0).astype(jnp.float32) == level
    )
    me_x, me_z = where[0], where[1]
    odd = lax.rem(me_z, 2).astype(jnp.float32)

    def at(parts, z):
        total = jnp.zeros((levels, PLACES), jnp.float32)
        for index, part in enumerate(parts):
            total = total + jnp.where(z == index, 1.0, 0.0) * part[:levels]
        return jnp.sum(total * level_row, axis=0, keepdims=True)

    cross_here = [jnp.where(me_x == 0, cross_code[0][z], cross_code[1][z]) for z in range(4)]
    cross_there = [jnp.where(me_x == 0, cross_code[1][z], cross_code[0][z]) for z in range(4)]
    def turn_of(code):
        return jnp.floor((code - 0.5) / STRIDE)

    got_up, got_down = at(up_code, me_z - 1), at(down_code, me_z + 1)
    got_cross = at(cross_here, me_z)
    inner = jnp.dot(kept.astype(jnp.bfloat16), within, preferred_element_type=jnp.float32)[0:1]
    one_orbital, one_origin = orbital[0:1], origin[0:1]
    slot = inner + slots * (one_orbital - 2 * one_origin)
    owned = kept[0:1] * as_number(one_origin == me_z.astype(jnp.float32))
    held = (
        owned * (slot + 1)
        + as_number(got_up > 0) * (got_up + STRIDE * (2 - odd + turn_of(got_up)))
        + as_number(got_down > 0) * (got_down + STRIDE * (1 + odd + turn_of(got_down)))
        - 1
    )
    crossed = got_cross - 1

    buffer = jnp.floor((held + 0.5) / STRIDE)
    tall = (PLACES, PLACES)
    target = lax.broadcasted_iota(jnp.int32, tall, 0).astype(jnp.float32) + 1
    pair = jnp.concatenate([buffer, held - STRIDE * buffer] + [jnp.zeros_like(held)] * 6, axis=0)
    lists = []
    sent_up, sent_down = at(up_code, me_z), at(down_code, me_z)
    for sent in (
        jnp.where(odd > 0, sent_down, sent_up),
        jnp.where(odd > 0, sent_up, sent_down),
        at(cross_there, me_z),
    ):
        chosen = as_number(target == sent).astype(jnp.bfloat16)
        both = lax.dot_general(
            pair.astype(jnp.bfloat16), chosen, (((1,), (1,)), ((), ())),
            preferred_element_type=jnp.float32,
        )
        lists.append(both[0:1] * STRIDE + both[1:2])
    flat = level + jnp.zeros((1, PLACES), jnp.float32)
    result = jnp.concatenate(lists + [held, crossed, flat, flat, flat], axis=0)
    out[...] = result.astype(jnp.int32)


def plan(where, masks, slots):
    return pl.pallas_call(
        functools.partial(plan_kernel, slots),
        grid_spec=pltpu.PrefetchScalarGridSpec(
            num_scalar_prefetch=1,
            grid=(),
            in_specs=[pl.BlockSpec(memory_space=pltpu.VMEM)],
            out_specs=pl.BlockSpec(memory_space=pltpu.VMEM),
        ),
        out_shape=jax.ShapeDtypeStruct((8, PLACES), jnp.int32),
        compiler_params=pltpu.CompilerParams(vmem_limit_bytes=32 * MIB),
        name="plan",
    )(where, masks)


def branch(which, low, high, run):
    if high - low == 1:
        run(low)
        return
    middle = (low + high) // 2

    @pl.when(which < middle)
    def _():
        branch(which, low, middle, run)

    @pl.when(which >= middle)
    def _():
        branch(which, middle, high, run)


def gather_kernel(turn, held, streams, table, *refs):
    buffers, outs, sems = refs[:held], refs[-1 - streams:-1], refs[-1]
    size = outs[0].shape[0]

    def step(index, carry):
        for stream in range(streams):
            row = stream if streams == 3 else 2
            code = table[row * PLACES + turn * STRIDE + index]
            branch(
                code // STRIDE, 0, held,
                lambda n, stream=stream, code=code: pltpu.make_async_copy(
                    buffers[n].at[lax.rem(code, STRIDE)], outs[stream].at[index], sems.at[stream]
                ).start(),
            )
        return carry

    lax.fori_loop(0, size, step, 0)
    for stream in range(streams):
        pltpu.make_async_copy(outs[stream], outs[stream], sems.at[stream]).wait()


def gather(turn, size, table, buffers, after):
    streams = 3 if turn < HOPS else 1
    shape = jax.ShapeDtypeStruct((size, OBLK, BLK), buffers[0].dtype)
    return pl.pallas_call(
        functools.partial(gather_kernel, turn, len(buffers), streams),
        grid_spec=pltpu.PrefetchScalarGridSpec(
            num_scalar_prefetch=1,
            grid=(),
            in_specs=[pl.BlockSpec(memory_space=pl.ANY)] * (len(buffers) + len(after)),
            out_specs=[pl.BlockSpec(memory_space=pltpu.VMEM)] * streams,
            scratch_shapes=[pltpu.SemaphoreType.DMA((streams,))],
        ),
        out_shape=[shape] * streams,
        compiler_params=pltpu.CompilerParams(vmem_limit_bytes=16 * MIB),
        cost_estimate=pl.CostEstimate(
            flops=0, bytes_accessed=4 * streams * size * OBLK * BLK, transcendentals=0
        ),
        name="gather",
    )(table, *buffers, *after)


def product_kernel(groups, orbitals, row_blocks, col_blocks, loc, meta, *refs):
    flat = iter(refs[:-6])
    sources = [[[next(flat) for _ in range(aux)] for _ in range(count)] for count, aux in groups]
    out, lhs, rhs, acc, in_sem, out_sem = refs[-6:]
    total_aux = sum(aux for _, aux in groups)
    row_tile = 2 if row_blocks % 2 == 0 else 1
    col_tile = 4 if col_blocks % 4 == 0 else 3 if col_blocks % 3 == 0 else 1
    first_row, first_col = meta[0], meta[1]
    depth = total_aux * OBLK
    padded = lhs.shape[2]
    height = row_tile * BLK
    width = col_tile * BLK
    row_tiles = row_blocks // row_tile

    def code_of(group, orbital, block):
        return loc[group * PLACES + orbital * NB + block]

    def any_kept(orbital, first, count):
        best = code_of(0, orbital, first)
        for step in range(1, count):
            best = jnp.maximum(best, code_of(0, orbital, first + step))
        return best >= 0

    def transfers(finish):
        def one(orbital, carry):
            wanted = jnp.logical_and(
                any_kept(orbital, first_row, row_blocks), any_kept(orbital, first_col, col_blocks)
            )

            @pl.when(wanted)
            def _():
                for held, first, blocks in ((lhs, first_row, row_blocks), (rhs, first_col, col_blocks)):
                    def step(block, carry, held=held, first=first):
                        code = code_of(0, orbital, first + block)

                        @pl.when(code >= 0)
                        def _():
                            if padded > depth and not finish:
                                held[orbital, block, depth:] = jnp.zeros(
                                    (padded - depth, BLK), held.dtype
                                )
                            start_aux = 0
                            for group, (count, aux_count) in enumerate(groups):
                                place = code_of(group, orbital, first + block)

                                def run(n, group=group, place=place, start_aux=start_aux, aux_count=aux_count):
                                    for aux in range(aux_count):
                                        copy = pltpu.make_async_copy(
                                            sources[group][n][aux].at[lax.rem(place, STRIDE)],
                                            held.at[orbital, block, pl.ds((start_aux + aux) * OBLK, OBLK)],
                                            in_sem,
                                        )
                                        if finish:
                                            copy.wait()
                                        else:
                                            copy.start()

                                if finish:
                                    run(0)
                                else:
                                    branch(place // STRIDE, 0, count, run)
                                start_aux += aux_count

                        if not finish:
                            @pl.when(code < 0)
                            def _():
                                held[orbital, block] = jnp.zeros((padded, BLK), held.dtype)
                        return carry

                    lax.fori_loop(0, blocks, step, 0)
            return carry

        lax.fori_loop(0, orbitals, one, 0)

    transfers(False)
    transfers(True)

    def leaving(tile):
        slot = lax.rem(tile, 2)
        return pltpu.make_async_copy(
            acc.at[slot],
            out.at[pl.ds(pl.multiple_of(tile * height, height), height)],
            out_sem.at[slot],
        )

    def row_step(tile, carry):
        slot = lax.rem(tile, 2)

        @pl.when(tile >= 2)
        def _():
            leaving(tile - 2).wait()

        acc[slot] = jnp.zeros(acc.shape[1:], acc.dtype)

        def orbital_step(orbital, carry):
            wanted = jnp.logical_and(
                any_kept(orbital, first_row + tile * row_tile, row_tile),
                any_kept(orbital, first_col, col_blocks),
            )

            @pl.when(wanted)
            def _():
                left = jnp.concatenate(
                    [lhs[orbital, tile * row_tile + step] for step in range(row_tile)], axis=1
                ).T
                for col in range(col_blocks // col_tile):
                    @pl.when(any_kept(orbital, first_col + col * col_tile, col_tile))
                    def _():
                        span = slice(col * width, (col + 1) * width)
                        right = jnp.concatenate(
                            [rhs[orbital, col * col_tile + step] for step in range(col_tile)], axis=1
                        )
                        acc[slot, :, span] += jnp.dot(
                            left, right, preferred_element_type=jnp.float32
                        )

            return carry

        lax.fori_loop(0, orbitals, orbital_step, 0)
        leaving(tile).start()
        return carry

    lax.fori_loop(0, row_tiles, row_step, 0)
    for tile in range(max(0, row_tiles - 2), row_tiles):
        leaving(tile).wait()


def product(loc, meta, sources, orbitals, row_blocks, col_blocks):
    groups = [(len(group), len(group[0])) for group in sources]
    flat = [ref for group in sources for refs in group for ref in refs]
    total_aux = sum(aux for _, aux in groups)
    rows, cols = row_blocks * BLK, col_blocks * BLK
    row_tile = 2 if row_blocks % 2 == 0 else 1
    padded = -(-total_aux * OBLK // 256) * 256
    scratch = 2 * orbitals * padded * (rows + cols) + 8 * row_tile * BLK * cols
    return pl.pallas_call(
        functools.partial(product_kernel, groups, orbitals, row_blocks, col_blocks),
        grid_spec=pltpu.PrefetchScalarGridSpec(
            num_scalar_prefetch=2,
            grid=(),
            in_specs=[pl.BlockSpec(memory_space=pl.ANY)] * len(flat),
            out_specs=pl.BlockSpec(memory_space=pl.ANY),
            scratch_shapes=[
                pltpu.VMEM((orbitals, row_blocks, padded, BLK), jnp.bfloat16),
                pltpu.VMEM((orbitals, col_blocks, padded, BLK), jnp.bfloat16),
                pltpu.VMEM((2, row_tile * BLK, cols), jnp.float32),
                pltpu.SemaphoreType.DMA(()),
                pltpu.SemaphoreType.DMA((2,)),
            ],
        ),
        out_shape=jax.ShapeDtypeStruct((rows, cols), jnp.float32),
        compiler_params=pltpu.CompilerParams(vmem_limit_bytes=scratch + 3 * MIB),
        cost_estimate=pl.CostEstimate(
            flops=2 * rows * cols * orbitals * total_aux * OBLK,
            bytes_accessed=4 * rows * cols + 2 * orbitals * total_aux * OBLK * (rows + cols),
            transcendentals=0,
        ),
        name="product",
    )(loc, meta, *flat)


def rounds(size, finish, table, own):
    first = [(0, 1), (1, 0), (2, 3), (3, 2)]
    second = [(1, 2), (2, 1), (0, 0), (3, 3)]
    across = [(0, 2), (2, 0), (1, 3), (3, 1)]

    def to_core(held):
        return lax.ppermute(held, "aux", first)

    moved, crossed, core_moved, core_crossed = [], [], [], []
    core_own = to_core(own)
    for turn in range(ROUNDS):
        after = crossed[-1:]
        if turn >= 2:
            after = after + core_moved[2 * turn - 4:2 * turn - 2] + [core_crossed[turn - 2]]
        if turn == 1:
            after = after + [core_own]
        chunks = gather(turn, size, table, [own] + moved, after)
        if turn < HOPS:
            moved.append(lax.ppermute(chunks[0], "occ", first))
            moved.append(lax.ppermute(chunks[1], "occ", second))
        crossed.append(lax.ppermute(chunks[-1], "aux", across))
        if turn < HOPS:
            core_moved += [to_core(held) for held in moved[-2:]]
        core_crossed.append(to_core(crossed[-1]))
    near = list(zip([own] + moved, [core_own] + core_moved))
    return finish(table[3 * PLACES:5 * PLACES], [near, list(zip(crossed, core_crossed))])


def on_device(shape, factors, block_mask, block_lists):
    aux_count, occ_count = shape["aux"], shape["occ"]
    own_orbitals, slots = block_lists.shape
    aux, occ = lax.axis_index("aux"), lax.axis_index("occ")
    row_blocks, col_blocks = NB // aux_count, NB // occ_count
    meta = jnp.stack([aux * row_blocks, occ * col_blocks]).astype(jnp.int32)

    def finish(loc, sources):
        return product(loc, meta, sources, NOB, row_blocks, col_blocks)

    kept = block_mask.T > 0
    own = pick(factors, block_lists)
    if aux_count == 4 and occ_count == 4 and shape["parts"] == 2:
        mask = as_number(kept).reshape(1, PLACES)
        other = lax.ppermute(mask, "parts", [(0, 1), (1, 0)])
        where = jnp.stack([aux // 2, occ]).astype(jnp.int32)
        table = plan(where, jnp.concatenate([mask, other]), slots)
        return lax.switch(
            table[5, 0],
            [functools.partial(rounds, size, finish) for size in LEVELS],
            table.reshape(-1),
            own,
        )
    everything = lax.all_gather(lax.all_gather(own, "aux"), "occ")
    sources = [[everything[z, a] for a in range(aux_count)] for z in range(occ_count)]
    earlier = jnp.arange(NB)[None, :] < jnp.arange(NB)[:, None]
    rank = jnp.sum(kept[:, None, :] & earlier[None], axis=2, dtype=jnp.int32)
    orbital = jnp.arange(NOB, dtype=jnp.int32)[:, None]
    start = orbital // own_orbitals * STRIDE + orbital % own_orbitals * slots
    return finish(jnp.where(kept, rank + start, -1).reshape(-1), [sources])


def solution(mesh):
    placed = (P(("parts", "aux"), "occ", None), P("parts", None), P(("parts", "occ"), None))
    return jax.shard_map(
        functools.partial(on_device, dict(mesh.shape)),
        mesh=mesh,
        in_specs=placed,
        out_specs=P(("parts", "aux"), "occ"),
        check_vma=False,
    )
```

```python
import functools

import jax
import jax.numpy as jnp
from jax import lax
from jax.experimental import pallas as pl
from jax.experimental.pallas import tpu as pltpu
from jax.sharding import PartitionSpec as P

BLK = 128
OBLK = 112
NB = 48
NOB = 8
PLACES = NOB * NB
STRIDE = 64
ROUNDS = 5
HOPS = ROUNDS - 1
LEVELS = (12, 14, 16, 17, 18, 20, 24, 48)
MIB = 1024 * 1024


def pick_kernel(lists, factors, items, picked, sems):
    orbitals, slots = lists.shape

    def leaving(orbital):
        span = pl.ds(orbital * slots, slots)
        return pltpu.make_async_copy(picked.at[span], items.at[span], sems.at[orbital])

    for orbital in range(orbitals):
        rows = slice(orbital * OBLK, (orbital + 1) * OBLK)

        def step(slot, carry):
            block = jnp.maximum(lists[orbital, slot], 0)
            columns = pl.ds(pl.multiple_of(block * BLK, BLK), BLK)
            picked[orbital * slots + slot] = factors[0, rows, columns]
            return carry

        lax.fori_loop(0, slots, step, 0)
        leaving(orbital).start()
    for orbital in range(orbitals):
        leaving(orbital).wait()


def pick(factors, block_lists):
    orbitals, slots = block_lists.shape
    count = orbitals * slots
    return pl.pallas_call(
        pick_kernel,
        grid_spec=pltpu.PrefetchScalarGridSpec(
            num_scalar_prefetch=1,
            grid=(),
            in_specs=[pl.BlockSpec(memory_space=pltpu.VMEM)],
            out_specs=pl.BlockSpec(memory_space=pltpu.HBM),
            scratch_shapes=[
                pltpu.VMEM((count, OBLK, BLK), factors.dtype),
                pltpu.SemaphoreType.DMA((orbitals,)),
            ],
        ),
        out_shape=jax.ShapeDtypeStruct((count, OBLK, BLK), factors.dtype),
        compiler_params=pltpu.CompilerParams(vmem_limit_bytes=16 * MIB),
        cost_estimate=pl.CostEstimate(
            flops=0, bytes_accessed=4 * count * OBLK * BLK, transcendentals=0
        ),
        name="pick",
    )(block_lists, factors)


def as_number(condition):
    return jnp.where(condition, 1.0, 0.0)


def place_facts(shape, axis):
    place = lax.broadcasted_iota(jnp.int32, shape, axis).astype(jnp.float32)
    orbital = jnp.floor((place + 0.5) / NB)
    block = place - NB * orbital
    quarter = jnp.floor((block + 0.5) / (NB // 4))
    return place, orbital, quarter, jnp.floor((quarter + 0.5) / 2), jnp.floor((orbital + 0.5) / 2)


def plan_kernel(slots, where, masks, out):
    levels = len(LEVELS)
    rows = 2 * levels
    wide = (rows, PLACES)
    _, orbital, quarter, half, origin = place_facts(wide, 1)
    row = lax.broadcasted_iota(jnp.int32, wide, 0)
    kept = jnp.where(row < levels, masks[0:1, :], masks[1:2, :])
    capacity = jnp.zeros(wide, jnp.float32)
    for index, size in enumerate(LEVELS):
        capacity = jnp.where((row == index) | (row == index + levels), float(size), capacity)

    square = (PLACES, PLACES)
    down_place, down_orbital, _, _, _ = place_facts(square, 0)
    over_place, over_orbital, _, _, _ = place_facts(square, 1)
    same = as_number(down_orbital == over_orbital)
    before = as_number(down_place < over_place)
    within = (same * before).astype(jnp.bfloat16)
    same, before = same.astype(jnp.bfloat16), before.astype(jnp.bfloat16)

    def times(parts, matrix):
        stacked = jnp.concatenate(parts, axis=0).astype(jnp.bfloat16)
        product = jnp.dot(stacked, matrix, preferred_element_type=jnp.float32)
        return [product[index * rows:(index + 1) * rows] for index in range(len(parts))]

    touching = times([kept * as_number(quarter == z) for z in range(4)], same)
    need = [kept * as_number(touch > 0) for touch in touching]
    zero = jnp.zeros(wide, jnp.float32)

    def union(parts):
        best = zero
        for part in parts:
            best = jnp.maximum(best, part)
        return best

    x_need = []
    for x in range(2):
        touched = as_number(touching[2 * x] + touching[2 * x + 1] > 0)
        here = as_number(half == x)
        x_need.append([
            need[z] * jnp.maximum(here, as_number(quarter == z) * touched) for z in range(4)
        ])
    mine = [kept * as_number(origin == z) for z in range(4)]
    need_up = [union(need[z + 1:]) for z in range(4)]
    far_up = [union(need[z + 2:]) for z in range(4)]
    need_down = [union(need[:z]) for z in range(4)]
    far_down = [union(need[:max(z - 1, 0)]) for z in range(4)]
    up = [mine[z] * need_up[z] for z in range(4)]
    down = [mine[z] * need_down[z] for z in range(4)]
    cross = [[mine[z] * x_need[x][z] for z in range(4)] for x in range(2)]
    up_code, down_code = [zero] * 4, [zero] * 4
    cross_code = [[zero] * 4, [zero] * 4]

    for turn in range(ROUNDS):
        parts = []
        if turn < HOPS:
            for z in range(3):
                parts += [up[z] * far_up[z], up[z] - up[z] * far_up[z]]
                parts += [down[z + 1] * far_down[z + 1], down[z + 1] - down[z + 1] * far_down[z + 1]]
        parts += [cross[x][z] for x in range(2) for z in range(4)]
        ranks = iter(zip(parts, times(parts, before)))

        def taken(pairs):
            rank, total = zero, 0.0
            chosen = zero
            for part, counted in pairs:
                rank = rank + part * (counted + total)
                total = total + jnp.sum(part, axis=1, keepdims=True)
                chosen = chosen + part
            chosen = chosen * as_number(rank < capacity)
            return chosen, chosen * (rank + float(turn * STRIDE + 1))

        up_sent, down_sent = [], []
        if turn < HOPS:
            for z in range(3):
                sent, code = taken([next(ranks), next(ranks)])
                up_sent.append(sent)
                up_code[z] = up_code[z] + code
                up[z] = up[z] - sent
                sent, code = taken([next(ranks), next(ranks)])
                down_sent.append(sent)
                down_code[z + 1] = down_code[z + 1] + code
                down[z + 1] = down[z + 1] - sent
        for x in range(2):
            for z in range(4):
                sent, code = taken([next(ranks)])
                cross_code[x][z] = cross_code[x][z] + code
                cross[x][z] = cross[x][z] - sent
        if turn < HOPS:
            for z in range(3):
                up[z + 1] = up[z + 1] + up_sent[z] * need_up[z + 1]
                down[z] = down[z] + down_sent[z] * need_down[z]
                for x in range(2):
                    cross[x][z + 1] = cross[x][z + 1] + up_sent[z] * x_need[x][z + 1]
                    cross[x][z] = cross[x][z] + down_sent[z] * x_need[x][z]

    left = zero
    for part in up + down + cross[0] + cross[1]:
        left = left + part
    left = jnp.sum(left, axis=1, keepdims=True)
    left = left[:levels] + left[levels:]
    order = lax.broadcasted_iota(jnp.int32, (levels, 1), 0).astype(jnp.float32)
    level = jnp.min(jnp.where(left > 0, float(levels - 1), order), axis=0, keepdims=True)
    level_row = as_number(
        lax.broadcasted_iota(jnp.int32, (levels, PLACES), 0).astype(jnp.float32) == level
    )
    me_x, me_z = where[0] // 2, where[1]
    odd = lax.rem(me_z, 2).astype(jnp.float32)

    def at(parts, z):
        total = jnp.zeros((levels, PLACES), jnp.float32)
        for index, part in enumerate(parts):
            total = total + jnp.where(z == index, 1.0, 0.0) * part[:levels]
        return jnp.sum(total * level_row, axis=0, keepdims=True)

    cross_here = [jnp.where(me_x == 0, cross_code[0][z], cross_code[1][z]) for z in range(4)]
    cross_there = [jnp.where(me_x == 0, cross_code[1][z], cross_code[0][z]) for z in range(4)]
    def turn_of(code):
        return jnp.floor((code - 0.5) / STRIDE)

    got_up, got_down = at(up_code, me_z - 1), at(down_code, me_z + 1)
    got_cross = at(cross_here, me_z)
    inner = jnp.dot(kept.astype(jnp.bfloat16), within, preferred_element_type=jnp.float32)[0:1]
    one_orbital, one_origin = orbital[0:1], origin[0:1]
    slot = inner + slots * (one_orbital - 2 * one_origin)
    owned = kept[0:1] * as_number(one_origin == me_z.astype(jnp.float32))
    held = (
        owned * (slot + 1)
        + as_number(got_up > 0) * (got_up + STRIDE * (2 - odd + turn_of(got_up)))
        + as_number(got_down > 0) * (got_down + STRIDE * (1 + odd + turn_of(got_down)))
        - 1
    )
    crossed = got_cross - 1
    near = jnp.maximum(
        as_number(quarter[0:1] == where[0].astype(jnp.float32)),
        as_number(quarter[0:1] == me_z.astype(jnp.float32)),
    )
    arrival = jnp.maximum(
        as_number(got_up + got_down > 0) * turn_of(got_up + got_down),
        as_number(got_cross > 0) * turn_of(got_cross),
    )
    lane = lax.broadcasted_iota(jnp.int32, (1, PLACES), 1)
    stage = jnp.zeros((1, PLACES), jnp.float32)
    for index in range(NOB):
        inside = as_number(one_orbital == float(index)) * near * kept[0:1]
        stage = jnp.where(
            lane == index, jnp.max(arrival * inside, axis=1, keepdims=True), stage
        )

    buffer = jnp.floor((held + 0.5) / STRIDE)
    tall = (PLACES, PLACES)
    target = lax.broadcasted_iota(jnp.int32, tall, 0).astype(jnp.float32) + 1
    pair = jnp.concatenate([buffer, held - STRIDE * buffer] + [jnp.zeros_like(held)] * 6, axis=0)
    lists = []
    sent_up, sent_down = at(up_code, me_z), at(down_code, me_z)
    for sent in (
        jnp.where(odd > 0, sent_down, sent_up),
        jnp.where(odd > 0, sent_up, sent_down),
        at(cross_there, me_z),
    ):
        chosen = as_number(target == sent).astype(jnp.bfloat16)
        both = lax.dot_general(
            pair.astype(jnp.bfloat16), chosen, (((1,), (1,)), ((), ())),
            preferred_element_type=jnp.float32,
        )
        lists.append(both[0:1] * STRIDE + both[1:2])
    flat = level + jnp.zeros((1, PLACES), jnp.float32)
    result = jnp.concatenate(lists + [held, crossed, stage, flat, flat], axis=0)
    out[...] = result.astype(jnp.int32)


def plan(where, masks, slots):
    return pl.pallas_call(
        functools.partial(plan_kernel, slots),
        grid_spec=pltpu.PrefetchScalarGridSpec(
            num_scalar_prefetch=1,
            grid=(),
            in_specs=[pl.BlockSpec(memory_space=pltpu.VMEM)],
            out_specs=pl.BlockSpec(memory_space=pltpu.VMEM),
        ),
        out_shape=jax.ShapeDtypeStruct((8, PLACES), jnp.int32),
        compiler_params=pltpu.CompilerParams(vmem_limit_bytes=32 * MIB),
        name="plan",
    )(where, masks)


def branch(which, low, high, run):
    if high - low == 1:
        run(low)
        return
    middle = (low + high) // 2

    @pl.when(which < middle)
    def _():
        branch(which, low, middle, run)

    @pl.when(which >= middle)
    def _():
        branch(which, middle, high, run)


def gather_kernel(turn, held, streams, table, *refs):
    buffers, outs, sems = refs[:held], refs[-1 - streams:-1], refs[-1]
    size = outs[0].shape[0]

    def step(index, carry):
        for stream in range(streams):
            row = stream if streams == 3 else 2
            code = table[row * PLACES + turn * STRIDE + index]
            branch(
                code // STRIDE, 0, held,
                lambda n, stream=stream, code=code: pltpu.make_async_copy(
                    buffers[n].at[lax.rem(code, STRIDE)], outs[stream].at[index], sems.at[stream]
                ).start(),
            )
        return carry

    lax.fori_loop(0, size, step, 0)
    for stream in range(streams):
        pltpu.make_async_copy(outs[stream], outs[stream], sems.at[stream]).wait()


def gather(turn, size, table, buffers, after):
    streams = 3 if turn < HOPS else 1
    shape = jax.ShapeDtypeStruct((size, OBLK, BLK), buffers[0].dtype)
    return pl.pallas_call(
        functools.partial(gather_kernel, turn, len(buffers), streams),
        grid_spec=pltpu.PrefetchScalarGridSpec(
            num_scalar_prefetch=1,
            grid=(),
            in_specs=[pl.BlockSpec(memory_space=pltpu.HBM)] * len(buffers)
            + [pl.BlockSpec(memory_space=pl.ANY)] * len(after),
            out_specs=[pl.BlockSpec(memory_space=pltpu.VMEM)] * streams,
            scratch_shapes=[pltpu.SemaphoreType.DMA((streams,))],
        ),
        out_shape=[shape] * streams,
        compiler_params=pltpu.CompilerParams(vmem_limit_bytes=16 * MIB),
        cost_estimate=pl.CostEstimate(
            flops=0, bytes_accessed=4 * streams * size * OBLK * BLK, transcendentals=0
        ),
        name="gather",
    )(table, *buffers, *after)


def product_kernel(groups, orbitals, row_blocks, col_blocks, stage, first, extra, loc, meta, *refs):
    flat = iter(refs)
    before = None if first else next(flat)
    sources = [[[next(flat) for _ in range(aux)] for _ in range(count)] for count, aux in groups]
    for _ in range(extra):
        next(flat)
    out, done, lhs, rhs, acc, state, in_sems, acc_sems, out_sems = flat
    total_aux = sum(aux for _, aux in groups)
    row_tile = 2 if row_blocks % 2 == 0 else 1
    col_tile = 4 if col_blocks % 4 == 0 else 3 if col_blocks % 3 == 0 else 1
    col_tiles = col_blocks // col_tile
    first_row, first_col = meta[0], meta[1]
    depth = total_aux * OBLK
    padded = lhs.shape[2]
    height = row_tile * BLK
    width = col_tile * BLK
    row_tiles = row_blocks // row_tile
    sides = ((lhs, first_row, row_blocks), (rhs, first_col, col_blocks))

    def code_of(group, orbital, block):
        return loc[group * PLACES + orbital * NB + block]

    def any_kept(orbital, start, count):
        best = code_of(0, orbital, start)
        for step in range(1, count):
            best = jnp.maximum(best, code_of(0, orbital, start + step))
        return best >= 0

    def fetch(orbital, carry):
        state[orbital] = 0
        wanted = jnp.logical_and(
            loc[len(groups) * PLACES + orbital] == stage, any_kept(orbital, first_row, row_blocks)
        )

        @pl.when(wanted)
        def _():
            columns = jnp.int32(0)
            for col in range(col_tiles):
                held = any_kept(orbital, first_col + col * col_tile, col_tile)
                columns = columns + jnp.where(held, 1 << col, 0)
            state[orbital] = columns

        @pl.when(state[orbital] > 0)
        def _():
            for held, start, blocks in sides:
                def step(block, carry, held=held, start=start):
                    code = code_of(0, orbital, start + block)

                    @pl.when(code >= 0)
                    def _():
                        if padded > depth:
                            held[orbital, block, depth:] = jnp.zeros((padded - depth, BLK), held.dtype)
                        start_aux = 0
                        for group, (count, aux_count) in enumerate(groups):
                            place = code_of(group, orbital, start + block)

                            def run(n, group=group, place=place, start_aux=start_aux, aux_count=aux_count):
                                for aux in range(aux_count):
                                    pltpu.make_async_copy(
                                        sources[group][n][aux].at[lax.rem(place, STRIDE)],
                                        held.at[orbital, block, pl.ds((start_aux + aux) * OBLK, OBLK)],
                                        in_sems.at[orbital],
                                    ).start()

                            branch(place // STRIDE, 0, count, run)
                            start_aux += aux_count

                    @pl.when(code < 0)
                    def _():
                        held[orbital, block] = jnp.zeros((padded, BLK), held.dtype)

                    return carry

                lax.fori_loop(0, blocks, step, 0)

        return carry

    def landed(orbital, carry):
        @pl.when(state[orbital] > 0)
        def _():
            for held, start, blocks in sides:
                def step(block, carry, held=held, start=start):
                    @pl.when(code_of(0, orbital, start + block) >= 0)
                    def _():
                        whole = held.at[orbital, block, pl.ds(0, depth)]
                        pltpu.make_async_copy(whole, whole, in_sems.at[orbital]).wait()

                    return carry

                lax.fori_loop(0, blocks, step, 0)

        return carry

    def span_of(tile):
        return pl.ds(pl.multiple_of(tile * height, height), height)

    def entering(tile):
        return pltpu.make_async_copy(before.at[span_of(tile)], acc.at[span_of(tile)], acc_sems.at[tile])

    def leaving(tile):
        return pltpu.make_async_copy(acc.at[span_of(tile)], out.at[span_of(tile)], out_sems.at[tile])

    def touch(tile, carry):
        def one(orbital, met):
            hit = jnp.logical_and(
                state[orbital] > 0, any_kept(orbital, first_row + tile * row_tile, row_tile)
            )
            return met + jnp.where(hit, 1 << orbital, 0)

        met = lax.fori_loop(0, orbitals, one, jnp.int32(0))
        state[orbitals + tile] = met

        if first:
            acc[span_of(tile)] = jnp.zeros((height, acc.shape[1]), acc.dtype)
        else:
            @pl.when(met > 0)
            def _():
                entering(tile).start()

        return carry

    lax.fori_loop(0, orbitals, fetch, 0)
    lax.fori_loop(0, row_tiles, touch, 0)
    done[...] = jnp.zeros(done.shape, done.dtype)
    lax.fori_loop(0, orbitals, landed, 0)

    def row_step(tile, carry):
        rows = span_of(tile)
        met = state[orbitals + tile]

        def orbital_step(orbital, carry):
            columns = state[orbital]

            @pl.when(lax.rem(lax.shift_right_logical(met, orbital), 2) == 1)
            def _():
                left = jnp.concatenate(
                    [lhs[orbital, tile * row_tile + step] for step in range(row_tile)], axis=1
                ).T
                for col in range(col_tiles):
                    @pl.when(lax.rem(columns // (1 << col), 2) == 1)
                    def _():
                        span = slice(col * width, (col + 1) * width)
                        right = jnp.concatenate(
                            [rhs[orbital, col * col_tile + step] for step in range(col_tile)], axis=1
                        )
                        acc[rows, span] += jnp.dot(left, right, preferred_element_type=jnp.float32)

            return carry

        def work():
            if not first:
                entering(tile).wait()
            lax.fori_loop(0, orbitals, orbital_step, 0)
            leaving(tile).start()

        if first:
            work()
        else:
            pl.when(met > 0)(work)
        return carry

    def row_end(tile, carry):
        if first:
            leaving(tile).wait()
        else:
            @pl.when(state[orbitals + tile] > 0)
            def _():
                leaving(tile).wait()

        return carry

    lax.fori_loop(0, row_tiles, row_step, 0)
    lax.fori_loop(0, row_tiles, row_end, 0)


def product(loc, meta, sources, held, after, stage, orbitals, row_blocks, col_blocks):
    groups = [(len(group), len(group[0])) for group in sources]
    flat = [ref for group in sources for refs in group for ref in refs]
    total_aux = sum(aux for _, aux in groups)
    rows, cols = row_blocks * BLK, col_blocks * BLK
    row_tiles = row_blocks // (2 if row_blocks % 2 == 0 else 1)
    padded = -(-total_aux * OBLK // 256) * 256
    first = held is None
    in_hbm = pl.BlockSpec(memory_space=pltpu.HBM)
    return pl.pallas_call(
        functools.partial(
            product_kernel, groups, orbitals, row_blocks, col_blocks, stage, first, len(after)
        ),
        grid_spec=pltpu.PrefetchScalarGridSpec(
            num_scalar_prefetch=2,
            grid=(),
            in_specs=[in_hbm] * (len(flat) + (not first))
            + [pl.BlockSpec(memory_space=pl.ANY)] * len(after),
            out_specs=[in_hbm, pl.BlockSpec(memory_space=pltpu.VMEM)],
            scratch_shapes=[
                pltpu.VMEM((orbitals, row_blocks, padded, BLK), jnp.bfloat16),
                pltpu.VMEM((orbitals, col_blocks, padded, BLK), jnp.bfloat16),
                pltpu.VMEM((rows, cols), jnp.float32),
                pltpu.SMEM((orbitals + row_tiles,), jnp.int32),
                pltpu.SemaphoreType.DMA((orbitals,)),
                pltpu.SemaphoreType.DMA((row_tiles,)),
                pltpu.SemaphoreType.DMA((row_tiles,)),
            ],
        ),
        out_shape=[
            jax.ShapeDtypeStruct((rows, cols), jnp.float32),
            jax.ShapeDtypeStruct((8, 128), jnp.float32),
        ],
        input_output_aliases={} if first else {2: 0},
        compiler_params=pltpu.CompilerParams(
            vmem_limit_bytes=2 * orbitals * padded * (rows + cols) + 4 * rows * cols + 3 * MIB
        ),
        cost_estimate=pl.CostEstimate(
            flops=2 * rows * cols * total_aux * OBLK, bytes_accessed=4 * rows * cols, transcendentals=0
        ),
        name="product",
    )(loc, meta, *([] if first else [held]), *flat, *after)


def rounds(size, add, table, own):
    first = [(0, 1), (1, 0), (2, 3), (3, 2)]
    second = []
    for aux in range(4):
        here, there = aux * 4, (aux ^ 1) * 4
        second += [(here, there), (here + 1, here + 2), (here + 2, here + 1), (here + 3, there + 3)]
    across = [(0, 2), (2, 0), (1, 3), (3, 1)]

    def to_core(held):
        return lax.ppermute(held, "aux", first)

    moved, crossed, core_moved, core_crossed = [], [], [], []
    core_own = to_core(own)
    total, done = None, []
    for turn in range(ROUNDS + 1):
        chunks = []
        if turn < ROUNDS:
            chunks = gather(turn, size, table, [own] + moved, crossed[-1:] + done)
        if turn > 0:
            near = list(zip([own] + moved, [core_own] + core_moved))
            far = list(zip(crossed, core_crossed))
            total, token = add(table[3 * PLACES:6 * PLACES], [near, far], total, chunks[:1], turn - 1)
            done = [token]
        if turn < HOPS:
            moved.append(lax.ppermute(chunks[0], "occ", first))
            moved.append(lax.ppermute(chunks[1], ("aux", "occ"), second))
            core_moved += [to_core(held) for held in moved[-2:]]
        if turn < ROUNDS:
            crossed.append(lax.ppermute(chunks[-1], "aux", across))
            core_crossed.append(to_core(crossed[-1]))
    return total


def on_device(shape, factors, block_mask, block_lists):
    aux_count, occ_count = shape["aux"], shape["occ"]
    own_orbitals, slots = block_lists.shape
    aux, occ = lax.axis_index("aux"), lax.axis_index("occ")
    row_blocks, col_blocks = NB // aux_count, NB // occ_count
    meta = jnp.stack([aux * row_blocks, occ * col_blocks]).astype(jnp.int32)

    def add(loc, sources, held, after, stage):
        return product(loc, meta, sources, held, after, stage, NOB, row_blocks, col_blocks)

    kept = block_mask.T > 0
    own = pick(factors, block_lists)
    if aux_count == 4 and occ_count == 4 and shape["parts"] == 2:
        mask = as_number(kept).reshape(1, PLACES)
        other = lax.ppermute(mask, "parts", [(0, 1), (1, 0)])
        where = jnp.stack([aux, occ]).astype(jnp.int32)
        table = plan(where, jnp.concatenate([mask, other]), slots)
        return lax.switch(
            table[6, 0],
            [functools.partial(rounds, size, add) for size in LEVELS],
            table.reshape(-1),
            own,
        )
    everything = lax.all_gather(lax.all_gather(own, "aux"), "occ")
    sources = [[everything[z, a] for a in range(aux_count)] for z in range(occ_count)]
    earlier = jnp.arange(NB)[None, :] < jnp.arange(NB)[:, None]
    rank = jnp.sum(kept[:, None, :] & earlier[None], axis=2, dtype=jnp.int32)
    orbital = jnp.arange(NOB, dtype=jnp.int32)[:, None]
    start = orbital // own_orbitals * STRIDE + orbital % own_orbitals * slots
    loc = jnp.concatenate([
        jnp.where(kept, rank + start, -1).reshape(-1), jnp.zeros(PLACES, jnp.int32)
    ])
    return add(loc, [sources], None, [], 0)[0]


def solution(mesh):
    placed = (P(("parts", "aux"), "occ", None), P("parts", None), P(("parts", "occ"), None))
    return jax.shard_map(
        functools.partial(on_device, dict(mesh.shape)),
        mesh=mesh,
        in_specs=placed,
        out_specs=P(("parts", "aux"), "occ"),
        check_vma=False,
    )
```

```python
import functools

import jax
import jax.numpy as jnp
from jax import lax
from jax.experimental import pallas as pl
from jax.experimental.pallas import tpu as pltpu
from jax.sharding import PartitionSpec as P

BLK = 128
OBLK = 112
NB = 48
NOB = 8
PLACES = NOB * NB
STRIDE = 64
ROUNDS = 5
HOPS = ROUNDS - 1
LEVELS = (12, 14, 16, 17, 18, 20, 24, 48)
MIB = 1024 * 1024


def pick_kernel(lists, factors, items):
    orbitals, slots = lists.shape

    def step(slot, carry):
        for orbital in range(orbitals):
            block = jnp.maximum(lists[orbital, slot], 0)
            columns = pl.ds(pl.multiple_of(block * BLK, BLK), BLK)
            rows = slice(orbital * OBLK, (orbital + 1) * OBLK)
            items[orbital * slots + slot] = factors[0, rows, columns]
        return carry

    lax.fori_loop(0, slots, step, 0)


def pick(factors, block_lists):
    orbitals, slots = block_lists.shape
    count = orbitals * slots
    return pl.pallas_call(
        pick_kernel,
        grid_spec=pltpu.PrefetchScalarGridSpec(
            num_scalar_prefetch=1,
            grid=(),
            in_specs=[pl.BlockSpec(memory_space=pltpu.VMEM)],
            out_specs=pl.BlockSpec(memory_space=pltpu.VMEM),
        ),
        out_shape=jax.ShapeDtypeStruct((count, OBLK, BLK), factors.dtype),
        compiler_params=pltpu.CompilerParams(vmem_limit_bytes=16 * MIB),
        cost_estimate=pl.CostEstimate(
            flops=0, bytes_accessed=4 * count * OBLK * BLK, transcendentals=0
        ),
        name="pick",
    )(block_lists, factors)


def as_number(condition):
    return jnp.where(condition, 1.0, 0.0)


def place_facts(shape, axis):
    place = lax.broadcasted_iota(jnp.int32, shape, axis).astype(jnp.float32)
    orbital = jnp.floor((place + 0.5) / NB)
    block = place - NB * orbital
    quarter = jnp.floor((block + 0.5) / (NB // 4))
    return place, orbital, quarter, jnp.floor((quarter + 0.5) / 2), jnp.floor((orbital + 0.5) / 2)


def plan_kernel(slots, where, masks, out):
    levels = len(LEVELS)
    rows = 2 * levels
    wide = (rows, PLACES)
    _, orbital, quarter, half, origin = place_facts(wide, 1)
    row = lax.broadcasted_iota(jnp.int32, wide, 0)
    kept = jnp.where(row < levels, masks[0:1, :], masks[1:2, :])
    capacity = jnp.zeros(wide, jnp.float32)
    for index, size in enumerate(LEVELS):
        capacity = jnp.where((row == index) | (row == index + levels), float(size), capacity)

    square = (PLACES, PLACES)
    down_place, down_orbital, _, _, _ = place_facts(square, 0)
    over_place, over_orbital, _, _, _ = place_facts(square, 1)
    same = as_number(down_orbital == over_orbital)
    before = as_number(down_place < over_place)
    within = (same * before).astype(jnp.bfloat16)
    same, before = same.astype(jnp.bfloat16), before.astype(jnp.bfloat16)

    def times(parts, matrix):
        stacked = jnp.concatenate(parts, axis=0).astype(jnp.bfloat16)
        product = jnp.dot(stacked, matrix, preferred_element_type=jnp.float32)
        return [product[index * rows:(index + 1) * rows] for index in range(len(parts))]

    touching = times([kept * as_number(quarter == z) for z in range(4)], same)
    need = [kept * as_number(touch > 0) for touch in touching]
    zero = jnp.zeros(wide, jnp.float32)

    def union(parts):
        best = zero
        for part in parts:
            best = jnp.maximum(best, part)
        return best

    x_need = []
    for x in range(2):
        touched = as_number(touching[2 * x] + touching[2 * x + 1] > 0)
        here = as_number(half == x)
        x_need.append([
            need[z] * jnp.maximum(here, as_number(quarter == z) * touched) for z in range(4)
        ])
    mine = [kept * as_number(origin == z) for z in range(4)]
    need_up = [union(need[z + 1:]) for z in range(4)]
    far_up = [union(need[z + 2:]) for z in range(4)]
    need_down = [union(need[:z]) for z in range(4)]
    far_down = [union(need[:max(z - 1, 0)]) for z in range(4)]
    up = [mine[z] * need_up[z] for z in range(4)]
    down = [mine[z] * need_down[z] for z in range(4)]
    cross = [[mine[z] * x_need[x][z] for z in range(4)] for x in range(2)]
    up_code, down_code = [zero] * 4, [zero] * 4
    cross_code = [[zero] * 4, [zero] * 4]

    for turn in range(ROUNDS):
        parts = []
        if turn < HOPS:
            for z in range(3):
                parts += [up[z] * far_up[z], up[z] - up[z] * far_up[z]]
                parts += [down[z + 1] * far_down[z + 1], down[z + 1] - down[z + 1] * far_down[z + 1]]
        parts += [cross[x][z] for x in range(2) for z in range(4)]
        ranks = iter(zip(parts, times(parts, before)))

        def taken(pairs):
            rank, total = zero, 0.0
            chosen = zero
            for part, counted in pairs:
                rank = rank + part * (counted + total)
                total = total + jnp.sum(part, axis=1, keepdims=True)
                chosen = chosen + part
            chosen = chosen * as_number(rank < capacity)
            return chosen, chosen * (rank + float(turn * STRIDE + 1))

        up_sent, down_sent = [], []
        if turn < HOPS:
            for z in range(3):
                sent, code = taken([next(ranks), next(ranks)])
                up_sent.append(sent)
                up_code[z] = up_code[z] + code
                up[z] = up[z] - sent
                sent, code = taken([next(ranks), next(ranks)])
                down_sent.append(sent)
                down_code[z + 1] = down_code[z + 1] + code
                down[z + 1] = down[z + 1] - sent
        for x in range(2):
            for z in range(4):
                sent, code = taken([next(ranks)])
                cross_code[x][z] = cross_code[x][z] + code
                cross[x][z] = cross[x][z] - sent
        if turn < HOPS:
            for z in range(3):
                up[z + 1] = up[z + 1] + up_sent[z] * need_up[z + 1]
                down[z] = down[z] + down_sent[z] * need_down[z]
                for x in range(2):
                    cross[x][z + 1] = cross[x][z + 1] + up_sent[z] * x_need[x][z + 1]
                    cross[x][z] = cross[x][z] + down_sent[z] * x_need[x][z]

    left = zero
    for part in up + down + cross[0] + cross[1]:
        left = left + part
    left = jnp.sum(left, axis=1, keepdims=True)
    left = left[:levels] + left[levels:]
    order = lax.broadcasted_iota(jnp.int32, (levels, 1), 0).astype(jnp.float32)
    level = jnp.min(jnp.where(left > 0, float(levels - 1), order), axis=0, keepdims=True)
    level_row = as_number(
        lax.broadcasted_iota(jnp.int32, (levels, PLACES), 0).astype(jnp.float32) == level
    )
    me_x, me_z = where[0] // 2, where[1]
    odd = lax.rem(me_z, 2).astype(jnp.float32)

    def at(parts, z):
        total = jnp.zeros((levels, PLACES), jnp.float32)
        for index, part in enumerate(parts):
            total = total + jnp.where(z == index, 1.0, 0.0) * part[:levels]
        return jnp.sum(total * level_row, axis=0, keepdims=True)

    cross_here = [jnp.where(me_x == 0, cross_code[0][z], cross_code[1][z]) for z in range(4)]
    cross_there = [jnp.where(me_x == 0, cross_code[1][z], cross_code[0][z]) for z in range(4)]
    def turn_of(code):
        return jnp.floor((code - 0.5) / STRIDE)

    got_up, got_down = at(up_code, me_z - 1), at(down_code, me_z + 1)
    got_cross = at(cross_here, me_z)
    inner = jnp.dot(kept.astype(jnp.bfloat16), within, preferred_element_type=jnp.float32)[0:1]
    one_orbital, one_origin = orbital[0:1], origin[0:1]
    slot = inner + slots * (one_orbital - 2 * one_origin)
    owned = kept[0:1] * as_number(one_origin == me_z.astype(jnp.float32))
    held = (
        owned * (slot + 1)
        + as_number(got_up > 0) * (got_up + STRIDE * (2 - odd + turn_of(got_up)))
        + as_number(got_down > 0) * (got_down + STRIDE * (1 + odd + turn_of(got_down)))
        - 1
    )
    crossed = got_cross - 1
    near = jnp.maximum(
        as_number(quarter[0:1] == where[0].astype(jnp.float32)),
        as_number(quarter[0:1] == me_z.astype(jnp.float32)),
    )
    arrival = jnp.maximum(
        as_number(got_up + got_down > 0) * turn_of(got_up + got_down),
        as_number(got_cross > 0) * turn_of(got_cross),
    )
    lane = lax.broadcasted_iota(jnp.int32, (1, PLACES), 1)
    stage = jnp.zeros((1, PLACES), jnp.float32)
    for index in range(NOB):
        inside = as_number(one_orbital == float(index)) * near * kept[0:1]
        stage = jnp.where(
            lane == index, jnp.max(arrival * inside, axis=1, keepdims=True), stage
        )

    buffer = jnp.floor((held + 0.5) / STRIDE)
    tall = (PLACES, PLACES)
    target = lax.broadcasted_iota(jnp.int32, tall, 0).astype(jnp.float32) + 1
    pair = jnp.concatenate([buffer, held - STRIDE * buffer] + [jnp.zeros_like(held)] * 6, axis=0)
    lists = []
    sent_up, sent_down = at(up_code, me_z), at(down_code, me_z)
    for sent in (
        jnp.where(odd > 0, sent_down, sent_up),
        jnp.where(odd > 0, sent_up, sent_down),
        at(cross_there, me_z),
    ):
        chosen = as_number(target == sent).astype(jnp.bfloat16)
        both = lax.dot_general(
            pair.astype(jnp.bfloat16), chosen, (((1,), (1,)), ((), ())),
            preferred_element_type=jnp.float32,
        )
        lists.append(both[0:1] * STRIDE + both[1:2])
    flat = level + jnp.zeros((1, PLACES), jnp.float32)
    result = jnp.concatenate(lists + [held, crossed, stage, flat, flat], axis=0)
    out[...] = result.astype(jnp.int32)


def plan(where, masks, slots):
    return pl.pallas_call(
        functools.partial(plan_kernel, slots),
        grid_spec=pltpu.PrefetchScalarGridSpec(
            num_scalar_prefetch=1,
            grid=(),
            in_specs=[pl.BlockSpec(memory_space=pltpu.VMEM)],
            out_specs=pl.BlockSpec(memory_space=pltpu.VMEM),
        ),
        out_shape=jax.ShapeDtypeStruct((8, PLACES), jnp.int32),
        compiler_params=pltpu.CompilerParams(vmem_limit_bytes=32 * MIB),
        name="plan",
    )(where, masks)


def branch(which, low, high, run):
    if high - low == 1:
        run(low)
        return
    middle = (low + high) // 2

    @pl.when(which < middle)
    def _():
        branch(which, low, middle, run)

    @pl.when(which >= middle)
    def _():
        branch(which, middle, high, run)


def gather_kernel(turn, held, streams, passed, table, *refs):
    buffers, refs = refs[:held], refs[held:]
    arrived, outs = refs[:passed], refs[len(refs) - streams - (passed > 0):]
    size = outs[0].shape[0]

    def step(index, carry):
        for stream in range(streams):
            row = stream if streams == 3 else 2
            code = table[row * PLACES + turn * STRIDE + index]

            def run(n, stream=stream, code=code):
                outs[stream][index] = buffers[n][lax.rem(code, STRIDE)]

            branch(code // STRIDE, 0, held, run)
        for place in range(passed):
            outs[streams][place * size + index] = arrived[place][index]
        return carry

    lax.fori_loop(0, size, step, 0)


def gather(turn, size, table, buffers, arrived, after):
    streams = 3 if turn < HOPS else 1
    dtype = buffers[0].dtype
    shapes = [jax.ShapeDtypeStruct((size, OBLK, BLK), dtype)] * streams
    if arrived:
        shapes.append(jax.ShapeDtypeStruct((size * len(arrived), OBLK, BLK), dtype))
    in_vmem = pl.BlockSpec(memory_space=pltpu.VMEM)
    return pl.pallas_call(
        functools.partial(gather_kernel, turn, len(buffers), streams, len(arrived)),
        grid_spec=pltpu.PrefetchScalarGridSpec(
            num_scalar_prefetch=1,
            grid=(),
            in_specs=[in_vmem] * (len(buffers) + len(arrived))
            + [pl.BlockSpec(memory_space=pl.ANY)] * len(after),
            out_specs=[in_vmem] * len(shapes),
        ),
        out_shape=shapes,
        compiler_params=pltpu.CompilerParams(vmem_limit_bytes=32 * MIB),
        cost_estimate=pl.CostEstimate(
            flops=0, bytes_accessed=4 * streams * size * OBLK * BLK, transcendentals=0
        ),
        name="gather",
    )(table, *buffers, *arrived, *after)


def product_kernel(groups, orbitals, row_blocks, col_blocks, stage, first, extra, loc, meta, *refs):
    flat = iter(refs)
    before = None if first else next(flat)
    sources = [
        [[(next(flat), offset) for offset in offsets] for offsets in buffers] for buffers in groups
    ]
    for _ in range(extra):
        next(flat)
    out, done, items, acc, unit, state, in_sems, acc_sems, out_sems = flat
    group_aux = [len(buffers[0]) for buffers in groups]
    row_tile = 2 if row_blocks % 2 == 0 else 1
    col_tile = 4 if col_blocks % 4 == 0 else 3 if col_blocks % 3 == 0 else 1
    col_tiles = col_blocks // col_tile
    first_row, first_col = meta[0], meta[1]
    room, blocks = items.shape[:2]
    depth = sum(group_aux) * OBLK
    padded = items.shape[2]
    height, width = row_tile * BLK, col_tile * BLK
    row_tiles = row_blocks // row_tile
    met_at, columns_at = orbitals, orbitals + row_tiles

    def code_of(group, orbital, block):
        return loc[group * PLACES + orbital * NB + block]

    def any_kept(orbital, start, count):
        best = code_of(0, orbital, start)
        for step in range(1, count):
            best = jnp.maximum(best, code_of(0, orbital, start + step))
        return best >= 0

    def whole_block(block):
        return jnp.where(block < row_blocks, first_row + block, first_col + block - row_blocks)

    def span_of(tile):
        return pl.ds(pl.multiple_of(tile * height, height), height)

    def entering(tile):
        return pltpu.make_async_copy(before.at[span_of(tile)], acc.at[span_of(tile)], acc_sems.at[tile])

    def leaving(tile):
        return pltpu.make_async_copy(acc.at[span_of(tile)], out.at[span_of(tile)], out_sems.at[tile])

    def survey(orbital, count):
        wanted = jnp.logical_and(
            loc[len(groups) * PLACES + orbital] == stage,
            jnp.logical_and(
                any_kept(orbital, first_row, row_blocks), any_kept(orbital, first_col, col_blocks)
            ),
        )

        @pl.when(wanted)
        def _():
            state[count] = orbital
            columns = jnp.int32(0)
            for col in range(col_tiles):
                held = any_kept(orbital, first_col + col * col_tile, col_tile)
                columns = columns + jnp.where(held, 1 << col, 0)
            state[columns_at + count] = columns
            for tile in range(row_tiles):
                held = any_kept(orbital, first_row + tile * row_tile, row_tile)
                state[met_at + tile] = state[met_at + tile] + jnp.where(held, 1 << count, 0)

        return count + jnp.where(wanted, 1, 0)

    for tile in range(row_tiles):
        state[met_at + tile] = 0
    count = lax.fori_loop(0, orbitals, survey, jnp.int32(0))
    done[...] = jnp.zeros(done.shape, done.dtype)

    def fetch(begin):
        def one(slot, carry):
            orbital = state[begin + slot]

            def step(block, carry):
                code = code_of(0, orbital, whole_block(block))

                @pl.when(code >= 0)
                def _():
                    if padded > depth:
                        items[slot, block, depth:] = jnp.zeros((padded - depth, BLK), items.dtype)
                    start_aux = 0
                    for group, buffers in enumerate(sources):
                        place = code_of(group, orbital, whole_block(block))

                        def run(n, buffers=buffers, place=place, start_aux=start_aux):
                            for aux, (buffer, offset) in enumerate(buffers[n]):
                                pltpu.make_async_copy(
                                    buffer.at[lax.rem(place, STRIDE) + offset],
                                    items.at[slot, block, pl.ds((start_aux + aux) * OBLK, OBLK)],
                                    in_sems.at[slot],
                                ).start()

                        branch(place // STRIDE, 0, len(buffers), run)
                        start_aux += group_aux[group]

                @pl.when(code < 0)
                def _():
                    items[slot, block] = jnp.zeros((padded, BLK), items.dtype)

                return carry

            return lax.fori_loop(0, blocks, step, carry)

        lax.fori_loop(0, jnp.minimum(count - begin, room), one, 0)

    def landed(begin):
        def one(slot, carry):
            orbital = state[begin + slot]

            def step(block, carry):
                @pl.when(code_of(0, orbital, whole_block(block)) >= 0)
                def _():
                    whole = items.at[slot, block, pl.ds(0, depth)]
                    pltpu.make_async_copy(whole, whole, in_sems.at[slot]).wait()

                return carry

            return lax.fori_loop(0, blocks, step, carry)

        lax.fori_loop(0, jnp.minimum(count - begin, room), one, 0)

    def multiply(begin, tile):
        rows = span_of(tile)

        def one(slot, carry):
            @pl.when(lax.rem(lax.shift_right_logical(state[met_at + tile], begin + slot), 2) == 1)
            def _():
                left = jnp.concatenate(
                    [items[slot, tile * row_tile + step] for step in range(row_tile)], axis=1
                )
                turned = lax.dot_general(
                    unit[...], left, (((1,), (1,)), ((), ())), preferred_element_type=jnp.float32
                ).astype(left.dtype)
                columns = state[columns_at + begin + slot]

                def column(col, carry):
                    @pl.when(lax.rem(lax.shift_right_logical(columns, col), 2) == 1)
                    def _():
                        right = jnp.concatenate(
                            [items[slot, row_blocks + col * col_tile + step] for step in range(col_tile)],
                            axis=1,
                        )
                        span = pl.ds(pl.multiple_of(col * width, width), width)
                        acc[rows, span] += jnp.dot(turned, right, preferred_element_type=jnp.float32)

                    return carry

                lax.fori_loop(0, col_tiles, column, 0)

            return carry

        lax.fori_loop(0, jnp.minimum(count - begin, room), one, 0)

    fetch(0)
    if first:
        def clear(tile, carry):
            acc[span_of(tile)] = jnp.zeros((height, acc.shape[1]), acc.dtype)
            return carry
    else:
        def clear(tile, carry):
            @pl.when(state[met_at + tile] > 0)
            def _():
                entering(tile).start()
            return carry

    lax.fori_loop(0, row_tiles, clear, 0)
    across = lax.broadcasted_iota(jnp.int32, unit.shape, 1)
    unit[...] = as_number(lax.broadcasted_iota(jnp.int32, unit.shape, 0) == across).astype(unit.dtype)
    passes = (count + room - 1) // room
    if first:
        passes = jnp.maximum(passes, 1)

    def one_pass(turn, carry):
        begin = turn * room

        @pl.when(turn > 0)
        def _():
            fetch(begin)

        landed(begin)

        def row_step(tile, carry):
            touched = jnp.logical_or(first, state[met_at + tile] > 0)

            @pl.when(touched)
            def _():
                if not first:
                    @pl.when(turn == 0)
                    def _():
                        entering(tile).wait()
                multiply(begin, tile)

                @pl.when(turn == passes - 1)
                def _():
                    leaving(tile).start()

            return carry

        lax.fori_loop(0, row_tiles, row_step, 0)
        return carry

    lax.fori_loop(0, passes, one_pass, 0)

    def row_end(tile, carry):
        @pl.when(jnp.logical_or(first, state[met_at + tile] > 0))
        def _():
            leaving(tile).wait()

        return carry

    lax.fori_loop(0, row_tiles, row_end, 0)


def product(loc, meta, sources, held, after, stage, orbitals, row_blocks, col_blocks):
    groups = [[[offset for _, offset in refs] for refs in group] for group in sources]
    flat = [array for group in sources for refs in group for array, _ in refs]
    total_aux = sum(len(group[0]) for group in sources)
    rows, cols = row_blocks * BLK, col_blocks * BLK
    row_tile = 2 if row_blocks % 2 == 0 else 1
    row_tiles = row_blocks // row_tile
    padded = -(-total_aux * OBLK // 256) * 256
    room = 4
    first = held is None
    in_hbm = pl.BlockSpec(memory_space=pltpu.HBM)
    in_any = pl.BlockSpec(memory_space=pl.ANY)
    return pl.pallas_call(
        functools.partial(
            product_kernel, groups, orbitals, row_blocks, col_blocks, stage, first, len(after)
        ),
        grid_spec=pltpu.PrefetchScalarGridSpec(
            num_scalar_prefetch=2,
            grid=(),
            in_specs=[in_hbm] * (not first) + [in_any] * (len(flat) + len(after)),
            out_specs=[in_hbm, pl.BlockSpec(memory_space=pltpu.VMEM)],
            scratch_shapes=[
                pltpu.VMEM((room, row_blocks + col_blocks, padded, BLK), jnp.bfloat16),
                pltpu.VMEM((rows, cols), jnp.float32),
                pltpu.VMEM((row_tile * BLK, row_tile * BLK), jnp.bfloat16),
                pltpu.SMEM((2 * orbitals + row_tiles,), jnp.int32),
                pltpu.SemaphoreType.DMA((room,)),
                pltpu.SemaphoreType.DMA((row_tiles,)),
                pltpu.SemaphoreType.DMA((row_tiles,)),
            ],
        ),
        out_shape=[
            jax.ShapeDtypeStruct((rows, cols), jnp.float32),
            jax.ShapeDtypeStruct((8, 128), jnp.float32),
        ],
        input_output_aliases={} if first else {2: 0},
        compiler_params=pltpu.CompilerParams(
            vmem_limit_bytes=2 * room * padded * (rows + cols) + 4 * rows * cols + 3 * MIB
        ),
        cost_estimate=pl.CostEstimate(
            flops=2 * rows * cols * total_aux * OBLK * orbitals,
            bytes_accessed=4 * rows * cols,
            transcendentals=0,
        ),
        name="product",
    )(loc, meta, *([] if first else [held]), *flat, *after)


def rounds(size, add, table, own):
    first = [(0, 1), (1, 0), (2, 3), (3, 2)]
    second = []
    for aux in range(4):
        here, there = aux * 4, (aux ^ 1) * 4
        second += [(here, there), (here + 1, here + 2), (here + 2, here + 1), (here + 3, there + 3)]
    across = [(0, 2), (2, 0), (1, 3), (3, 1)]

    def to_core(held):
        return lax.ppermute(held, "aux", first)

    moved, crossed, passed = [], [], []
    core_own = to_core(own)
    total, done = None, []
    for turn in range(ROUNDS + 1):
        chunks = []
        if turn < ROUNDS:
            arrived = moved[-2:] + crossed[-1:]
            chunks = gather(turn, size, table, [own] + moved, arrived, done)
        if turn > 0:
            if turn < ROUNDS:
                passed.append(to_core(chunks[-1]))
            else:
                passed.append(to_core(lax.optimization_barrier((crossed[-1], done[0]))[0]))
            near = [[(own, 0), (core_own, 0)]]
            for index, held in enumerate(moved):
                near.append([(held, 0), (passed[index // 2], index % 2 * size)])
            far = [
                [(held, 0), (passed[index], 2 * size if index < HOPS else 0)]
                for index, held in enumerate(crossed)
            ]
            total, token = add(table[3 * PLACES:6 * PLACES], [near, far], total, chunks[:1], turn - 1)
            done = [token]
        if turn < HOPS:
            moved.append(lax.ppermute(chunks[0], "occ", first))
            moved.append(lax.ppermute(chunks[1], ("aux", "occ"), second))
        if turn < ROUNDS:
            crossed.append(lax.ppermute(chunks[2 if turn < HOPS else 0], "aux", across))
    return total


def on_device(shape, factors, block_mask, block_lists):
    aux_count, occ_count = shape["aux"], shape["occ"]
    own_orbitals, slots = block_lists.shape
    aux, occ = lax.axis_index("aux"), lax.axis_index("occ")
    row_blocks, col_blocks = NB // aux_count, NB // occ_count
    meta = jnp.stack([aux * row_blocks, occ * col_blocks]).astype(jnp.int32)

    def add(loc, sources, held, after, stage):
        return product(loc, meta, sources, held, after, stage, NOB, row_blocks, col_blocks)

    kept = block_mask.T > 0
    own = pick(factors, block_lists)
    if aux_count == 4 and occ_count == 4 and shape["parts"] == 2:
        mask = as_number(kept).reshape(1, PLACES)
        other = lax.ppermute(mask, "parts", [(0, 1), (1, 0)])
        where = jnp.stack([aux, occ]).astype(jnp.int32)
        table = plan(where, jnp.concatenate([mask, other]), slots)
        return lax.switch(
            table[6, 0],
            [functools.partial(rounds, size, add) for size in LEVELS],
            table.reshape(-1),
            own,
        )
    everything = lax.all_gather(lax.all_gather(own, "aux"), "occ")
    sources = [[(everything[z, a], 0) for a in range(aux_count)] for z in range(occ_count)]
    earlier = jnp.arange(NB)[None, :] < jnp.arange(NB)[:, None]
    rank = jnp.sum(kept[:, None, :] & earlier[None], axis=2, dtype=jnp.int32)
    orbital = jnp.arange(NOB, dtype=jnp.int32)[:, None]
    start = orbital // own_orbitals * STRIDE + orbital % own_orbitals * slots
    loc = jnp.concatenate([
        jnp.where(kept, rank + start, -1).reshape(-1), jnp.zeros(PLACES, jnp.int32)
    ])
    return add(loc, [sources], None, [], 0)[0]


def solution(mesh):
    placed = (P(("parts", "aux"), "occ", None), P("parts", None), P(("parts", "occ"), None))
    return jax.shard_map(
        functools.partial(on_device, dict(mesh.shape)),
        mesh=mesh,
        in_specs=placed,
        out_specs=P(("parts", "aux"), "occ"),
        check_vma=False,
    )
```

```python
import functools

import jax
import jax.numpy as jnp
from jax import lax
from jax.experimental import pallas as pl
from jax.experimental.pallas import tpu as pltpu
from jax.sharding import PartitionSpec as P

BLK = 128
OBLK = 112
NB = 48
NOB = 8
PLACES = NOB * NB
STRIDE = 64
ROUNDS = 5
HOPS = ROUNDS - 1
LEVELS = (14, 16, 18, 22, 48)
MIB = 1024 * 1024


def pick_kernel(lists, factors, items):
    orbitals, slots = lists.shape

    def step(slot, carry):
        for orbital in range(orbitals):
            block = jnp.maximum(lists[orbital, slot], 0)
            columns = pl.ds(pl.multiple_of(block * BLK, BLK), BLK)
            rows = slice(orbital * OBLK, (orbital + 1) * OBLK)
            items[orbital * slots + slot] = factors[0, rows, columns]
        return carry

    lax.fori_loop(0, slots, step, 0)


def pick(factors, block_lists):
    orbitals, slots = block_lists.shape
    count = orbitals * slots
    return pl.pallas_call(
        pick_kernel,
        grid_spec=pltpu.PrefetchScalarGridSpec(
            num_scalar_prefetch=1,
            grid=(),
            in_specs=[pl.BlockSpec(memory_space=pltpu.VMEM)],
            out_specs=pl.BlockSpec(memory_space=pltpu.VMEM),
        ),
        out_shape=jax.ShapeDtypeStruct((count, OBLK, BLK), factors.dtype),
        compiler_params=pltpu.CompilerParams(vmem_limit_bytes=16 * MIB),
        cost_estimate=pl.CostEstimate(
            flops=0, bytes_accessed=4 * count * OBLK * BLK, transcendentals=0
        ),
        name="pick",
    )(block_lists, factors)


def as_number(condition):
    return jnp.where(condition, 1.0, 0.0)


def place_facts(shape, axis):
    place = lax.broadcasted_iota(jnp.int32, shape, axis).astype(jnp.float32)
    orbital = jnp.floor((place + 0.5) / NB)
    block = place - NB * orbital
    quarter = jnp.floor((block + 0.5) / (NB // 4))
    return place, orbital, quarter, jnp.floor((quarter + 0.5) / 2), jnp.floor((orbital + 0.5) / 2)


def plan_kernel(where, lists, masks, factors, out, items, loaded, sem):
    load = pltpu.make_async_copy(factors, loaded, sem)
    load.start()
    slots = lists.shape[1]
    levels = 8
    rows = 2 * levels
    wide = (rows, PLACES)
    _, orbital, quarter, half, origin = place_facts(wide, 1)
    row = lax.broadcasted_iota(jnp.int32, wide, 0)
    kept = jnp.where(row < levels, masks[0:1, :], masks[1:2, :])
    capacity = jnp.zeros(wide, jnp.float32)
    for index, size in enumerate(LEVELS + LEVELS[-1:] * (levels - len(LEVELS))):
        capacity = jnp.where((row == index) | (row == index + levels), float(size), capacity)

    square = (PLACES, PLACES)
    down_place, down_orbital, _, _, _ = place_facts(square, 0)
    over_place, over_orbital, _, _, _ = place_facts(square, 1)
    same = as_number(down_orbital == over_orbital)
    before = as_number(down_place < over_place)
    within = (same * before).astype(jnp.bfloat16)
    same, before = same.astype(jnp.bfloat16), before.astype(jnp.bfloat16)

    def times(parts, matrix):
        stacked = jnp.concatenate(parts, axis=0).astype(jnp.bfloat16)
        product = jnp.dot(stacked, matrix, preferred_element_type=jnp.float32)
        return [product[index * rows:(index + 1) * rows] for index in range(len(parts))]

    touching = times([kept * as_number(quarter == z) for z in range(4)], same)
    need = [kept * as_number(touch > 0) for touch in touching]
    zero = jnp.zeros(wide, jnp.float32)

    def union(parts):
        best = zero
        for part in parts:
            best = jnp.maximum(best, part)
        return best

    x_need = []
    for x in range(2):
        touched = as_number(touching[2 * x] + touching[2 * x + 1] > 0)
        here = as_number(half == x)
        x_need.append([
            need[z] * jnp.maximum(here, as_number(quarter == z) * touched) for z in range(4)
        ])
    mine = [kept * as_number(origin == z) for z in range(4)]
    need_up = [union(need[z + 1:]) for z in range(4)]
    far_up = [union(need[z + 2:]) for z in range(4)]
    need_down = [union(need[:z]) for z in range(4)]
    far_down = [union(need[:max(z - 1, 0)]) for z in range(4)]
    up = [mine[z] * need_up[z] for z in range(4)]
    down = [mine[z] * need_down[z] for z in range(4)]
    cross = [[mine[z] * x_need[x][z] for z in range(4)] for x in range(2)]
    up_code, down_code = [zero] * 4, [zero] * 4
    cross_code = [[zero] * 4, [zero] * 4]

    for turn in range(ROUNDS):
        parts = []
        if turn < HOPS:
            for z in range(3):
                parts += [up[z] * far_up[z], up[z] - up[z] * far_up[z]]
                parts += [down[z + 1] * far_down[z + 1], down[z + 1] - down[z + 1] * far_down[z + 1]]
        parts += [cross[x][z] for x in range(2) for z in range(4)]
        ranks = iter(zip(parts, times(parts, before)))

        def taken(pairs):
            rank, total = zero, 0.0
            chosen = zero
            for part, counted in pairs:
                rank = rank + part * (counted + total)
                total = total + jnp.sum(part, axis=1, keepdims=True)
                chosen = chosen + part
            chosen = chosen * as_number(rank < capacity)
            return chosen, chosen * (rank + float(turn * STRIDE + 1))

        up_sent, down_sent = [], []
        if turn < HOPS:
            for z in range(3):
                sent, code = taken([next(ranks), next(ranks)])
                up_sent.append(sent)
                up_code[z] = up_code[z] + code
                up[z] = up[z] - sent
                sent, code = taken([next(ranks), next(ranks)])
                down_sent.append(sent)
                down_code[z + 1] = down_code[z + 1] + code
                down[z + 1] = down[z + 1] - sent
        for x in range(2):
            for z in range(4):
                sent, code = taken([next(ranks)])
                cross_code[x][z] = cross_code[x][z] + code
                cross[x][z] = cross[x][z] - sent
        if turn < HOPS:
            for z in range(3):
                up[z + 1] = up[z + 1] + up_sent[z] * need_up[z + 1]
                down[z] = down[z] + down_sent[z] * need_down[z]
                for x in range(2):
                    cross[x][z + 1] = cross[x][z + 1] + up_sent[z] * x_need[x][z + 1]
                    cross[x][z] = cross[x][z] + down_sent[z] * x_need[x][z]

    left = zero
    for part in up + down + cross[0] + cross[1]:
        left = left + part
    left = jnp.sum(left, axis=1, keepdims=True)
    left = left[:levels] + left[levels:]
    order = lax.broadcasted_iota(jnp.int32, (levels, 1), 0).astype(jnp.float32)
    level = jnp.min(jnp.where(left > 0, float(len(LEVELS) - 1), order), axis=0, keepdims=True)
    level_row = as_number(
        lax.broadcasted_iota(jnp.int32, (levels, PLACES), 0).astype(jnp.float32) == level
    )
    me_x, me_z = where[0] // 2, where[1]
    odd = lax.rem(me_z, 2).astype(jnp.float32)

    def at(parts, z):
        total = jnp.zeros((levels, PLACES), jnp.float32)
        for index, part in enumerate(parts):
            total = total + jnp.where(z == index, 1.0, 0.0) * part[:levels]
        return jnp.sum(total * level_row, axis=0, keepdims=True)

    cross_here = [jnp.where(me_x == 0, cross_code[0][z], cross_code[1][z]) for z in range(4)]
    cross_there = [jnp.where(me_x == 0, cross_code[1][z], cross_code[0][z]) for z in range(4)]
    def turn_of(code):
        return jnp.floor((code - 0.5) / STRIDE)

    got_up, got_down = at(up_code, me_z - 1), at(down_code, me_z + 1)
    got_cross = at(cross_here, me_z)
    inner = jnp.dot(kept.astype(jnp.bfloat16), within, preferred_element_type=jnp.float32)[0:1]
    one_orbital, one_origin = orbital[0:1], origin[0:1]
    slot = inner + slots * (one_orbital - 2 * one_origin)
    owned = kept[0:1] * as_number(one_origin == me_z.astype(jnp.float32))
    held = (
        owned * (slot + 1)
        + as_number(got_up > 0) * (got_up + STRIDE * (2 - odd + turn_of(got_up)))
        + as_number(got_down > 0) * (got_down + STRIDE * (1 + odd + turn_of(got_down)))
        - 1
    )
    crossed = got_cross - 1
    near = jnp.maximum(
        as_number(quarter[0:1] == where[0].astype(jnp.float32)),
        as_number(quarter[0:1] == me_z.astype(jnp.float32)),
    )
    arrival = jnp.maximum(
        as_number(got_up + got_down > 0) * turn_of(got_up + got_down),
        as_number(got_cross > 0) * turn_of(got_cross),
    )
    lane = lax.broadcasted_iota(jnp.int32, (1, PLACES), 1)
    stage = jnp.zeros((1, PLACES), jnp.float32)
    for index in range(NOB):
        inside = as_number(one_orbital == float(index)) * near * kept[0:1]
        stage = jnp.where(
            lane == index, jnp.max(arrival * inside, axis=1, keepdims=True), stage
        )

    buffer = jnp.floor((held + 0.5) / STRIDE)
    tall = (PLACES, PLACES)
    target = lax.broadcasted_iota(jnp.int32, tall, 0).astype(jnp.float32) + 1
    pair = jnp.concatenate([buffer, held - STRIDE * buffer] + [jnp.zeros_like(held)] * 6, axis=0)
    sends = []
    sent_up, sent_down = at(up_code, me_z), at(down_code, me_z)
    for sent in (
        jnp.where(odd > 0, sent_down, sent_up),
        jnp.where(odd > 0, sent_up, sent_down),
        at(cross_there, me_z),
    ):
        chosen = as_number(target == sent).astype(jnp.bfloat16)
        both = lax.dot_general(
            pair.astype(jnp.bfloat16), chosen, (((1,), (1,)), ((), ())),
            preferred_element_type=jnp.float32,
        )
        sends.append(both[0:1] * STRIDE + both[1:2])
    flat = level + jnp.zeros((1, PLACES), jnp.float32)
    result = jnp.concatenate(sends + [held, crossed, stage, flat, flat], axis=0)
    out[...] = result.astype(jnp.int32)
    load.wait()
    pick_kernel(lists, loaded, items)


def plan(where, masks, factors, block_lists):
    orbitals, slots = block_lists.shape
    in_vmem = pl.BlockSpec(memory_space=pltpu.VMEM)
    return pl.pallas_call(
        plan_kernel,
        grid_spec=pltpu.PrefetchScalarGridSpec(
            num_scalar_prefetch=2,
            grid=(),
            in_specs=[in_vmem, pl.BlockSpec(memory_space=pltpu.HBM)],
            out_specs=[in_vmem, in_vmem],
            scratch_shapes=[pltpu.VMEM(factors.shape, factors.dtype), pltpu.SemaphoreType.DMA(())],
        ),
        out_shape=[
            jax.ShapeDtypeStruct((8, PLACES), jnp.int32),
            jax.ShapeDtypeStruct((orbitals * slots, OBLK, BLK), factors.dtype),
        ],
        compiler_params=pltpu.CompilerParams(vmem_limit_bytes=16 * MIB),
        name="plan",
    )(where, block_lists, masks, factors)


def branch(which, low, high, run):
    if high - low == 1:
        run(low)
        return
    middle = (low + high) // 2

    @pl.when(which < middle)
    def _():
        branch(which, low, middle, run)

    @pl.when(which >= middle)
    def _():
        branch(which, middle, high, run)


def gather_kernel(turn, held, streams, passed, table, *refs):
    buffers, refs = refs[:held], refs[held:]
    arrived, outs = refs[:passed], refs[len(refs) - streams - (passed > 0):]
    size = outs[0].shape[0]

    def step(index, carry):
        for stream in range(streams):
            row = stream if streams == 3 else 2
            code = table[row * PLACES + turn * STRIDE + index]

            def run(n, stream=stream, code=code):
                outs[stream][index] = buffers[n][lax.rem(code, STRIDE)]

            branch(code // STRIDE, 0, held, run)
        for place in range(passed):
            outs[streams][place * size + index] = arrived[place][index]
        return carry

    lax.fori_loop(0, size, step, 0)


def gather(turn, size, table, buffers, arrived, after):
    streams = 3 if turn < HOPS else 1
    dtype = buffers[0].dtype
    shapes = [jax.ShapeDtypeStruct((size, OBLK, BLK), dtype)] * streams
    if arrived:
        shapes.append(jax.ShapeDtypeStruct((size * len(arrived), OBLK, BLK), dtype))
    in_vmem = pl.BlockSpec(memory_space=pltpu.VMEM)
    return pl.pallas_call(
        functools.partial(gather_kernel, turn, len(buffers), streams, len(arrived)),
        grid_spec=pltpu.PrefetchScalarGridSpec(
            num_scalar_prefetch=1,
            grid=(),
            in_specs=[in_vmem] * (len(buffers) + len(arrived))
            + [pl.BlockSpec(memory_space=pl.ANY)] * len(after),
            out_specs=[in_vmem] * len(shapes),
        ),
        out_shape=shapes,
        compiler_params=pltpu.CompilerParams(
            vmem_limit_bytes=2 * sum(array.size for array in [*buffers, *arrived, *shapes]) + 4 * MIB
        ),
        cost_estimate=pl.CostEstimate(
            flops=0, bytes_accessed=4 * streams * size * OBLK * BLK, transcendentals=0
        ),
        name="gather",
    )(table, *buffers, *arrived, *after)


def relay_kernel(source, token, out):
    out[...] = source[...]


def relay(source, token):
    in_vmem = pl.BlockSpec(memory_space=pltpu.VMEM)
    return pl.pallas_call(
        relay_kernel,
        in_specs=[in_vmem, pl.BlockSpec(memory_space=pl.ANY)],
        out_specs=in_vmem,
        out_shape=jax.ShapeDtypeStruct(source.shape, source.dtype),
        compiler_params=pltpu.CompilerParams(vmem_limit_bytes=16 * MIB),
        name="relay",
    )(source, token)


def product_kernel(
    groups, orbitals, row_blocks, col_blocks, stage, first, extra, resident, loc, meta, *refs
):
    flat = iter(refs)
    before = None if first else next(flat)
    sources = [
        [[(next(flat), offset) for offset in offsets] for offsets in buffers] for buffers in groups
    ]
    for _ in range(extra):
        next(flat)
    out, done, items, acc, unit, state, in_sems, acc_sems, out_sems = flat
    group_aux = [len(buffers[0]) for buffers in groups]
    row_tile = 2 if row_blocks % 2 == 0 else 1
    col_tile = 4 if col_blocks % 4 == 0 else 3 if col_blocks % 3 == 0 else 1
    col_tiles = col_blocks // col_tile
    first_row, first_col = meta[0], meta[1]
    room, blocks = items.shape[:2]
    depth = sum(group_aux) * OBLK
    padded = items.shape[2]
    height, width = row_tile * BLK, col_tile * BLK
    row_tiles = row_blocks // row_tile
    met_at, columns_at = orbitals, orbitals + row_tiles

    def code_of(group, orbital, block):
        return loc[group * PLACES + orbital * NB + block]

    def any_kept(orbital, start, count):
        best = code_of(0, orbital, start)
        for step in range(1, count):
            best = jnp.maximum(best, code_of(0, orbital, start + step))
        return best >= 0

    def whole_block(block):
        return jnp.where(block < row_blocks, first_row + block, first_col + block - row_blocks)

    def span_of(tile):
        return pl.ds(pl.multiple_of(tile * height, height), height)

    def entering(tile):
        return pltpu.make_async_copy(before.at[span_of(tile)], acc.at[span_of(tile)], acc_sems.at[tile])

    def leaving(tile):
        return pltpu.make_async_copy(acc.at[span_of(tile)], out.at[span_of(tile)], out_sems.at[tile])

    def survey(orbital, count):
        wanted = jnp.logical_and(
            loc[len(groups) * PLACES + orbital] == stage,
            jnp.logical_and(
                any_kept(orbital, first_row, row_blocks), any_kept(orbital, first_col, col_blocks)
            ),
        )

        @pl.when(wanted)
        def _():
            state[count] = orbital
            columns = jnp.int32(0)
            for col in range(col_tiles):
                held = any_kept(orbital, first_col + col * col_tile, col_tile)
                columns = columns + jnp.where(held, 1 << col, 0)
            state[columns_at + count] = columns
            for tile in range(row_tiles):
                held = any_kept(orbital, first_row + tile * row_tile, row_tile)
                state[met_at + tile] = state[met_at + tile] + jnp.where(held, 1 << count, 0)

        return count + jnp.where(wanted, 1, 0)

    for tile in range(row_tiles):
        state[met_at + tile] = 0
    count = lax.fori_loop(0, orbitals, survey, jnp.int32(0))
    done[...] = jnp.zeros(done.shape, done.dtype)

    def fetch(begin):
        def one(slot, carry):
            orbital = state[begin + slot]

            def step(block, carry):
                code = code_of(0, orbital, whole_block(block))

                @pl.when(code >= 0)
                def _():
                    if padded > depth:
                        items[slot, block, depth:] = jnp.zeros((padded - depth, BLK), items.dtype)
                    start_aux = 0
                    for group, buffers in enumerate(sources):
                        place = code_of(group, orbital, whole_block(block))

                        def run(n, buffers=buffers, place=place, start_aux=start_aux):
                            for aux, (buffer, offset) in enumerate(buffers[n]):
                                index = lax.rem(place, STRIDE) + offset
                                span = pl.ds((start_aux + aux) * OBLK, OBLK)
                                if resident:
                                    items[slot, block, span] = buffer[index]
                                else:
                                    pltpu.make_async_copy(
                                        buffer.at[index], items.at[slot, block, span], in_sems.at[slot]
                                    ).start()

                        branch(place // STRIDE, 0, len(buffers), run)
                        start_aux += group_aux[group]

                @pl.when(code < 0)
                def _():
                    items[slot, block] = jnp.zeros((padded, BLK), items.dtype)

                return carry

            return lax.fori_loop(0, blocks, step, carry)

        lax.fori_loop(0, jnp.minimum(count - begin, room), one, 0)

    def landed(begin):
        def one(slot, carry):
            orbital = state[begin + slot]

            def step(block, carry):
                @pl.when(code_of(0, orbital, whole_block(block)) >= 0)
                def _():
                    whole = items.at[slot, block, pl.ds(0, depth)]
                    pltpu.make_async_copy(whole, whole, in_sems.at[slot]).wait()

                return carry

            return lax.fori_loop(0, blocks, step, carry)

        lax.fori_loop(0, jnp.minimum(count - begin, room), one, 0)

    def multiply(begin, tile):
        rows = span_of(tile)

        def one(slot, carry):
            @pl.when(lax.rem(lax.shift_right_logical(state[met_at + tile], begin + slot), 2) == 1)
            def _():
                left = jnp.concatenate(
                    [items[slot, tile * row_tile + step] for step in range(row_tile)], axis=1
                )
                turned = lax.dot_general(
                    unit[...], left, (((1,), (1,)), ((), ())), preferred_element_type=jnp.float32
                ).astype(left.dtype)
                columns = state[columns_at + begin + slot]

                def column(col, carry):
                    @pl.when(lax.rem(lax.shift_right_logical(columns, col), 2) == 1)
                    def _():
                        right = jnp.concatenate(
                            [items[slot, row_blocks + col * col_tile + step] for step in range(col_tile)],
                            axis=1,
                        )
                        span = pl.ds(pl.multiple_of(col * width, width), width)
                        acc[rows, span] += jnp.dot(turned, right, preferred_element_type=jnp.float32)

                    return carry

                lax.fori_loop(0, col_tiles, column, 0)

            return carry

        lax.fori_loop(0, jnp.minimum(count - begin, room), one, 0)

    fetch(0)
    if first:
        def clear(tile, carry):
            acc[span_of(tile)] = jnp.zeros((height, acc.shape[1]), acc.dtype)
            return carry
    else:
        def clear(tile, carry):
            @pl.when(state[met_at + tile] > 0)
            def _():
                entering(tile).start()
            return carry

    lax.fori_loop(0, row_tiles, clear, 0)
    across = lax.broadcasted_iota(jnp.int32, unit.shape, 1)
    unit[...] = as_number(lax.broadcasted_iota(jnp.int32, unit.shape, 0) == across).astype(unit.dtype)
    passes = (count + room - 1) // room
    if first:
        passes = jnp.maximum(passes, 1)

    def one_pass(turn, carry):
        begin = turn * room

        @pl.when(turn > 0)
        def _():
            fetch(begin)

        if not resident:
            landed(begin)

        def row_step(tile, carry):
            touched = jnp.logical_or(first, state[met_at + tile] > 0)

            @pl.when(touched)
            def _():
                if not first:
                    @pl.when(turn == 0)
                    def _():
                        entering(tile).wait()
                multiply(begin, tile)

                @pl.when(turn == passes - 1)
                def _():
                    leaving(tile).start()

            return carry

        lax.fori_loop(0, row_tiles, row_step, 0)
        return carry

    lax.fori_loop(0, passes, one_pass, 0)

    def row_end(tile, carry):
        @pl.when(jnp.logical_or(first, state[met_at + tile] > 0))
        def _():
            leaving(tile).wait()

        return carry

    lax.fori_loop(0, row_tiles, row_end, 0)


def product(loc, meta, sources, held, after, stage, resident, orbitals, row_blocks, col_blocks):
    groups = [[[offset for _, offset in refs] for refs in group] for group in sources]
    flat = [array for group in sources for refs in group for array, _ in refs]
    total_aux = sum(len(group[0]) for group in sources)
    rows, cols = row_blocks * BLK, col_blocks * BLK
    row_tile = 2 if row_blocks % 2 == 0 else 1
    row_tiles = row_blocks // row_tile
    padded = -(-total_aux * OBLK // 256) * 256
    room = 2
    first = held is None
    in_hbm = pl.BlockSpec(memory_space=pltpu.HBM)
    in_any = pl.BlockSpec(memory_space=pl.ANY)
    return pl.pallas_call(
        functools.partial(
            product_kernel, groups, orbitals, row_blocks, col_blocks, stage, first, len(after), resident
        ),
        grid_spec=pltpu.PrefetchScalarGridSpec(
            num_scalar_prefetch=2,
            grid=(),
            in_specs=[in_hbm] * (not first)
            + [pl.BlockSpec(memory_space=pltpu.VMEM) if resident else in_any] * len(flat)
            + [in_any] * len(after),
            out_specs=[in_hbm, pl.BlockSpec(memory_space=pltpu.VMEM)],
            scratch_shapes=[
                pltpu.VMEM((room, row_blocks + col_blocks, padded, BLK), jnp.bfloat16),
                pltpu.VMEM((rows, cols), jnp.float32),
                pltpu.VMEM((row_tile * BLK, row_tile * BLK), jnp.bfloat16),
                pltpu.SMEM((2 * orbitals + row_tiles,), jnp.int32),
                pltpu.SemaphoreType.DMA((room,)),
                pltpu.SemaphoreType.DMA((row_tiles,)),
                pltpu.SemaphoreType.DMA((row_tiles,)),
            ],
        ),
        out_shape=[
            jax.ShapeDtypeStruct((rows, cols), jnp.float32),
            jax.ShapeDtypeStruct((8, 128), jnp.float32),
        ],
        input_output_aliases={} if first else {2: 0},
        compiler_params=pltpu.CompilerParams(
            vmem_limit_bytes=2 * room * padded * (rows + cols)
            + 4 * rows * cols
            + (sum(2 * array.size for array in flat) if resident else 0)
            + 3 * MIB
        ),
        cost_estimate=pl.CostEstimate(
            flops=2 * rows * cols * total_aux * OBLK * orbitals,
            bytes_accessed=4 * rows * cols,
            transcendentals=0,
        ),
        name="product",
    )(loc, meta, *([] if first else [held]), *flat, *after)


def rounds(size, add, table, own):
    first = [(0, 1), (1, 0), (2, 3), (3, 2)]
    second = []
    for aux in range(4):
        here, there = aux * 4, (aux ^ 1) * 4
        second += [(here, there), (here + 1, here + 2), (here + 2, here + 1), (here + 3, there + 3)]
    across = [(0, 2), (2, 0), (1, 3), (3, 1)]

    def to_core(held):
        return lax.ppermute(held, "aux", first)

    moved, crossed, passed = [], [], []
    core_own = to_core(own)
    total, done = None, []
    for turn in range(ROUNDS + 1):
        chunks = []
        if turn < ROUNDS:
            arrived = moved[-2:] + crossed[-1:]
            chunks = gather(turn, size, table, [own] + moved, arrived, done)
        if turn > 0:
            if turn < ROUNDS:
                passed.append(to_core(chunks[-1]))
            else:
                passed.append(to_core(relay(crossed[-1], done[0])))
            near = [[(own, 0), (core_own, 0)]]
            for index, held in enumerate(moved):
                near.append([(held, 0), (passed[index // 2], index % 2 * size)])
            far = [
                [(held, 0), (passed[index], 2 * size if index < HOPS else 0)]
                for index, held in enumerate(crossed)
            ]
            total, token = add(
                table[3 * PLACES:6 * PLACES], [near, far], total, chunks[:1], turn - 1, size <= 24
            )
            done = [token]
        if turn < HOPS:
            moved.append(lax.ppermute(chunks[0], "occ", first))
            moved.append(lax.ppermute(chunks[1], ("aux", "occ"), second))
        if turn < ROUNDS:
            crossed.append(lax.ppermute(chunks[2 if turn < HOPS else 0], "aux", across))
    return total


def on_device(shape, factors, block_mask, block_lists):
    aux_count, occ_count = shape["aux"], shape["occ"]
    own_orbitals, slots = block_lists.shape
    aux, occ = lax.axis_index("aux"), lax.axis_index("occ")
    row_blocks, col_blocks = NB // aux_count, NB // occ_count
    meta = jnp.stack([aux * row_blocks, occ * col_blocks]).astype(jnp.int32)

    def add(loc, sources, held, after, stage, resident=False):
        return product(
            loc, meta, sources, held, after, stage, resident, NOB, row_blocks, col_blocks
        )

    kept = block_mask.T > 0
    if aux_count == 4 and occ_count == 4 and shape["parts"] == 2:
        mask = as_number(kept).reshape(1, PLACES)
        other = lax.ppermute(mask, "parts", [(0, 1), (1, 0)])
        where = jnp.stack([aux, occ]).astype(jnp.int32)
        table, own = plan(where, jnp.concatenate([mask, other]), factors, block_lists)
        return lax.switch(
            table[6, 0],
            [functools.partial(rounds, size, add) for size in LEVELS],
            table.reshape(-1),
            own,
        )
    own = pick(factors, block_lists)
    everything = lax.all_gather(lax.all_gather(own, "aux"), "occ")
    sources = [[(everything[z, a], 0) for a in range(aux_count)] for z in range(occ_count)]
    earlier = jnp.arange(NB)[None, :] < jnp.arange(NB)[:, None]
    rank = jnp.sum(kept[:, None, :] & earlier[None], axis=2, dtype=jnp.int32)
    orbital = jnp.arange(NOB, dtype=jnp.int32)[:, None]
    start = orbital // own_orbitals * STRIDE + orbital % own_orbitals * slots
    loc = jnp.concatenate([
        jnp.where(kept, rank + start, -1).reshape(-1), jnp.zeros(PLACES, jnp.int32)
    ])
    return add(loc, [sources], None, [], 0)[0]


def solution(mesh):
    placed = (P(("parts", "aux"), "occ", None), P("parts", None), P(("parts", "occ"), None))
    return jax.shard_map(
        functools.partial(on_device, dict(mesh.shape)),
        mesh=mesh,
        in_specs=placed,
        out_specs=P(("parts", "aux"), "occ"),
        check_vma=False,
    )
```

```python
import functools

import jax
import jax.numpy as jnp
from jax import lax
from jax.experimental import pallas as pl
from jax.experimental.pallas import tpu as pltpu
from jax.sharding import PartitionSpec as P

BLK = 128
OBLK = 112
NB = 48
NOB = 8
PLACES = NOB * NB
STRIDE = 64
ROUNDS = 5
HOPS = ROUNDS - 1
LEVELS = (14, 16, 18, 22, 48)
MIB = 1024 * 1024


def pick_kernel(lists, factors, *refs):
    items = refs[-1]
    orbitals, slots = lists.shape

    def step(slot, carry):
        for orbital in range(orbitals):
            block = jnp.maximum(lists[orbital, slot], 0)
            columns = pl.ds(pl.multiple_of(block * BLK, BLK), BLK)
            rows = slice(orbital * OBLK, (orbital + 1) * OBLK)
            items[orbital * slots + slot] = factors[0, rows, columns]
        return carry

    lax.fori_loop(0, slots, step, 0)


def pick(factors, block_lists, after=()):
    orbitals, slots = block_lists.shape
    count = orbitals * slots
    return pl.pallas_call(
        pick_kernel,
        grid_spec=pltpu.PrefetchScalarGridSpec(
            num_scalar_prefetch=1,
            grid=(),
            in_specs=[pl.BlockSpec(memory_space=pltpu.VMEM)]
            + [pl.BlockSpec(memory_space=pl.ANY)] * len(after),
            out_specs=pl.BlockSpec(memory_space=pltpu.VMEM),
        ),
        out_shape=jax.ShapeDtypeStruct((count, OBLK, BLK), factors.dtype),
        compiler_params=pltpu.CompilerParams(vmem_limit_bytes=16 * MIB),
        cost_estimate=pl.CostEstimate(
            flops=0, bytes_accessed=4 * count * OBLK * BLK, transcendentals=0
        ),
        name="pick",
    )(block_lists, factors, *after)


def as_number(condition):
    return jnp.where(condition, 1.0, 0.0)


def place_facts(shape, axis):
    place = lax.broadcasted_iota(jnp.int32, shape, axis).astype(jnp.float32)
    orbital = jnp.floor((place + 0.5) / NB)
    block = place - NB * orbital
    quarter = jnp.floor((block + 0.5) / (NB // 4))
    return place, orbital, quarter, jnp.floor((quarter + 0.5) / 2), jnp.floor((orbital + 0.5) / 2)


def plan_kernel(slots, where, masks, out):
    levels = 8
    rows = 2 * levels
    wide = (rows, PLACES)
    _, orbital, quarter, half, origin = place_facts(wide, 1)
    row = lax.broadcasted_iota(jnp.int32, wide, 0)
    kept = jnp.where(row < levels, masks[0:1, :], masks[1:2, :])
    capacity = jnp.zeros(wide, jnp.float32)
    for index, size in enumerate(LEVELS + LEVELS[-1:] * (levels - len(LEVELS))):
        capacity = jnp.where((row == index) | (row == index + levels), float(size), capacity)

    square = (PLACES, PLACES)
    down_place, down_orbital, _, _, _ = place_facts(square, 0)
    over_place, over_orbital, _, _, _ = place_facts(square, 1)
    same = as_number(down_orbital == over_orbital)
    before = as_number(down_place < over_place)
    within = (same * before).astype(jnp.bfloat16)
    same, before = same.astype(jnp.bfloat16), before.astype(jnp.bfloat16)

    def times(parts, matrix):
        stacked = jnp.concatenate(parts, axis=0).astype(jnp.bfloat16)
        product = jnp.dot(stacked, matrix, preferred_element_type=jnp.float32)
        return [product[index * rows:(index + 1) * rows] for index in range(len(parts))]

    touching = times([kept * as_number(quarter == z) for z in range(4)], same)
    need = [kept * as_number(touch > 0) for touch in touching]
    zero = jnp.zeros(wide, jnp.float32)

    def union(parts):
        best = zero
        for part in parts:
            best = jnp.maximum(best, part)
        return best

    x_need = []
    for x in range(2):
        touched = as_number(touching[2 * x] + touching[2 * x + 1] > 0)
        here = as_number(half == x)
        x_need.append([
            need[z] * jnp.maximum(here, as_number(quarter == z) * touched) for z in range(4)
        ])
    mine = [kept * as_number(origin == z) for z in range(4)]
    need_up = [union(need[z + 1:]) for z in range(4)]
    far_up = [union(need[z + 2:]) for z in range(4)]
    need_down = [union(need[:z]) for z in range(4)]
    far_down = [union(need[:max(z - 1, 0)]) for z in range(4)]
    up = [mine[z] * need_up[z] for z in range(4)]
    down = [mine[z] * need_down[z] for z in range(4)]
    cross = [[mine[z] * x_need[x][z] for z in range(4)] for x in range(2)]
    up_code, down_code = [zero] * 4, [zero] * 4
    cross_code = [[zero] * 4, [zero] * 4]

    for turn in range(ROUNDS):
        parts = []
        if turn < HOPS:
            for z in range(3):
                parts += [up[z] * far_up[z], up[z] - up[z] * far_up[z]]
                parts += [down[z + 1] * far_down[z + 1], down[z + 1] - down[z + 1] * far_down[z + 1]]
        parts += [cross[x][z] for x in range(2) for z in range(4)]
        ranks = iter(zip(parts, times(parts, before)))

        def taken(pairs):
            rank, total = zero, 0.0
            chosen = zero
            for part, counted in pairs:
                rank = rank + part * (counted + total)
                total = total + jnp.sum(part, axis=1, keepdims=True)
                chosen = chosen + part
            chosen = chosen * as_number(rank < capacity)
            return chosen, chosen * (rank + float(turn * STRIDE + 1))

        up_sent, down_sent = [], []
        if turn < HOPS:
            for z in range(3):
                sent, code = taken([next(ranks), next(ranks)])
                up_sent.append(sent)
                up_code[z] = up_code[z] + code
                up[z] = up[z] - sent
                sent, code = taken([next(ranks), next(ranks)])
                down_sent.append(sent)
                down_code[z + 1] = down_code[z + 1] + code
                down[z + 1] = down[z + 1] - sent
        for x in range(2):
            for z in range(4):
                sent, code = taken([next(ranks)])
                cross_code[x][z] = cross_code[x][z] + code
                cross[x][z] = cross[x][z] - sent
        if turn < HOPS:
            for z in range(3):
                up[z + 1] = up[z + 1] + up_sent[z] * need_up[z + 1]
                down[z] = down[z] + down_sent[z] * need_down[z]
                for x in range(2):
                    cross[x][z + 1] = cross[x][z + 1] + up_sent[z] * x_need[x][z + 1]
                    cross[x][z] = cross[x][z] + down_sent[z] * x_need[x][z]

    left = zero
    for part in up + down + cross[0] + cross[1]:
        left = left + part
    left = jnp.sum(left, axis=1, keepdims=True)
    left = left[:levels] + left[levels:]
    order = lax.broadcasted_iota(jnp.int32, (levels, 1), 0).astype(jnp.float32)
    level = jnp.min(jnp.where(left > 0, float(len(LEVELS) - 1), order), axis=0, keepdims=True)
    level_row = as_number(
        lax.broadcasted_iota(jnp.int32, (levels, PLACES), 0).astype(jnp.float32) == level
    )
    me_x, me_z = where[0] // 2, where[1]
    odd = lax.rem(me_z, 2).astype(jnp.float32)

    def at(parts, z):
        total = jnp.zeros((levels, PLACES), jnp.float32)
        for index, part in enumerate(parts):
            total = total + jnp.where(z == index, 1.0, 0.0) * part[:levels]
        return jnp.sum(total * level_row, axis=0, keepdims=True)

    cross_here = [jnp.where(me_x == 0, cross_code[0][z], cross_code[1][z]) for z in range(4)]
    cross_there = [jnp.where(me_x == 0, cross_code[1][z], cross_code[0][z]) for z in range(4)]
    def turn_of(code):
        return jnp.floor((code - 0.5) / STRIDE)

    got_up, got_down = at(up_code, me_z - 1), at(down_code, me_z + 1)
    got_cross = at(cross_here, me_z)
    inner = jnp.dot(kept.astype(jnp.bfloat16), within, preferred_element_type=jnp.float32)[0:1]
    one_orbital, one_origin = orbital[0:1], origin[0:1]
    slot = inner + slots * (one_orbital - 2 * one_origin)
    owned = kept[0:1] * as_number(one_origin == me_z.astype(jnp.float32))
    held = (
        owned * (slot + 1)
        + as_number(got_up > 0) * (got_up + STRIDE * (2 - odd + turn_of(got_up)))
        + as_number(got_down > 0) * (got_down + STRIDE * (1 + odd + turn_of(got_down)))
        - 1
    )
    crossed = got_cross - 1
    near = jnp.maximum(
        as_number(quarter[0:1] == where[0].astype(jnp.float32)),
        as_number(quarter[0:1] == me_z.astype(jnp.float32)),
    )
    arrival = jnp.maximum(
        as_number(got_up + got_down > 0) * turn_of(got_up + got_down),
        as_number(got_cross > 0) * turn_of(got_cross),
    )
    lane = lax.broadcasted_iota(jnp.int32, (1, PLACES), 1)
    stage = jnp.zeros((1, PLACES), jnp.float32)
    for index in range(NOB):
        inside = as_number(one_orbital == float(index)) * near * kept[0:1]
        stage = jnp.where(
            lane == index, jnp.max(arrival * inside, axis=1, keepdims=True), stage
        )

    buffer = jnp.floor((held + 0.5) / STRIDE)
    tall = (PLACES, PLACES)
    target = lax.broadcasted_iota(jnp.int32, tall, 0).astype(jnp.float32) + 1
    pair = jnp.concatenate([buffer, held - STRIDE * buffer] + [jnp.zeros_like(held)] * 6, axis=0)
    sends = []
    sent_up, sent_down = at(up_code, me_z), at(down_code, me_z)
    for sent in (
        jnp.where(odd > 0, sent_down, sent_up),
        jnp.where(odd > 0, sent_up, sent_down),
        at(cross_there, me_z),
    ):
        chosen = as_number(target == sent).astype(jnp.bfloat16)
        both = lax.dot_general(
            pair.astype(jnp.bfloat16), chosen, (((1,), (1,)), ((), ())),
            preferred_element_type=jnp.float32,
        )
        sends.append(both[0:1] * STRIDE + both[1:2])
    flat = level + jnp.zeros((1, PLACES), jnp.float32)
    result = jnp.concatenate(sends + [held, crossed, stage, flat, flat], axis=0)
    out[...] = result.astype(jnp.int32)


def plan(where, masks, slots):
    in_vmem = pl.BlockSpec(memory_space=pltpu.VMEM)
    return pl.pallas_call(
        functools.partial(plan_kernel, slots),
        grid_spec=pltpu.PrefetchScalarGridSpec(
            num_scalar_prefetch=1, grid=(), in_specs=[in_vmem], out_specs=in_vmem
        ),
        out_shape=jax.ShapeDtypeStruct((8, PLACES), jnp.int32),
        compiler_params=pltpu.CompilerParams(vmem_limit_bytes=16 * MIB),
        name="plan",
    )(where, masks)


def branch(which, low, high, run):
    if high - low == 1:
        run(low)
        return
    middle = (low + high) // 2

    @pl.when(which < middle)
    def _():
        branch(which, low, middle, run)

    @pl.when(which >= middle)
    def _():
        branch(which, middle, high, run)


def gather_kernel(turn, held, streams, passed, table, *refs):
    buffers, refs = refs[:held], refs[held:]
    arrived, outs = refs[:passed], refs[len(refs) - streams - (passed > 0):]
    size = outs[0].shape[0]

    def step(index, carry):
        for stream in range(streams):
            row = stream if streams == 3 else 2
            code = table[row * PLACES + turn * STRIDE + index]

            def run(n, stream=stream, code=code):
                outs[stream][index] = buffers[n][code & (STRIDE - 1)]

            branch(lax.shift_right_logical(code, 6), 0, held, run)
        for place in range(passed):
            outs[streams][place * size + index] = arrived[place][index]
        return carry

    lax.fori_loop(0, size, step, 0, unroll=2)


def gather(turn, size, table, buffers, arrived, after):
    streams = 3 if turn < HOPS else 1
    dtype = buffers[0].dtype
    shapes = [jax.ShapeDtypeStruct((size, OBLK, BLK), dtype)] * streams
    if arrived:
        shapes.append(jax.ShapeDtypeStruct((size * len(arrived), OBLK, BLK), dtype))
    in_vmem = pl.BlockSpec(memory_space=pltpu.VMEM)
    return pl.pallas_call(
        functools.partial(gather_kernel, turn, len(buffers), streams, len(arrived)),
        grid_spec=pltpu.PrefetchScalarGridSpec(
            num_scalar_prefetch=1,
            grid=(),
            in_specs=[in_vmem] * (len(buffers) + len(arrived))
            + [pl.BlockSpec(memory_space=pl.ANY)] * len(after),
            out_specs=[in_vmem] * len(shapes),
        ),
        out_shape=shapes,
        compiler_params=pltpu.CompilerParams(
            vmem_limit_bytes=2 * sum(array.size for array in [*buffers, *arrived, *shapes]) + 4 * MIB
        ),
        cost_estimate=pl.CostEstimate(
            flops=0, bytes_accessed=4 * streams * size * OBLK * BLK, transcendentals=0
        ),
        name="gather",
    )(table, *buffers, *arrived, *after)


def relay_kernel(source, token, out):
    out[...] = source[...]


def relay(source, token):
    in_vmem = pl.BlockSpec(memory_space=pltpu.VMEM)
    return pl.pallas_call(
        relay_kernel,
        in_specs=[in_vmem, pl.BlockSpec(memory_space=pl.ANY)],
        out_specs=in_vmem,
        out_shape=jax.ShapeDtypeStruct(source.shape, source.dtype),
        compiler_params=pltpu.CompilerParams(vmem_limit_bytes=16 * MIB),
        name="relay",
    )(source, token)


def product_kernel(
    groups, orbitals, row_blocks, col_blocks, stages, first, extra, loc, meta, *refs
):
    flat = iter(refs)
    before = None if first else next(flat)
    sources = [
        [[(next(flat), offset) for offset in offsets] for offsets in buffers] for buffers in groups
    ]
    for _ in range(extra):
        next(flat)
    out, done, items, acc, unit, state, in_sems, acc_sems, out_sems = flat
    group_aux = [len(buffers[0]) for buffers in groups]
    row_tile, col_tile = tile_of(row_blocks), tile_of(col_blocks)
    step_tile = unit.shape[0] // BLK
    col_tiles = col_blocks // col_tile
    first_row, first_col = meta[0], meta[1]
    room = items.shape[0]
    blocks, first_right = row_blocks + col_blocks, row_blocks
    if row_blocks == col_blocks:
        alike = first_row == first_col
        blocks = jnp.where(alike, row_blocks, blocks)
        first_right = jnp.where(alike, 0, first_right)
    depth = sum(group_aux) * OBLK
    padded = items.shape[2]
    height, width = row_tile * BLK, col_tile * BLK
    row_tiles = row_blocks // row_tile
    met_at, columns_at = orbitals, orbitals + row_tiles

    def code_of(group, orbital, block):
        return loc[group * PLACES + orbital * NB + block]

    def any_kept(orbital, start, count):
        best = code_of(0, orbital, start)
        for step in range(1, count):
            best = jnp.maximum(best, code_of(0, orbital, start + step))
        return best >= 0

    def whole_block(block):
        return jnp.where(block < row_blocks, first_row + block, first_col + block - row_blocks)

    def span_of(tile):
        return pl.ds(pl.multiple_of(tile * height, height), height)

    def entering(tile):
        return pltpu.make_async_copy(before.at[span_of(tile)], acc.at[span_of(tile)], acc_sems.at[tile])

    def leaving(tile):
        return pltpu.make_async_copy(acc.at[span_of(tile)], out.at[span_of(tile)], out_sems.at[tile])

    def survey(orbital, count):
        stage = loc[len(groups) * PLACES + orbital]
        wanted = jnp.logical_and(
            jnp.logical_and(stage >= stages[0], stage <= stages[1]),
            jnp.logical_and(
                any_kept(orbital, first_row, row_blocks), any_kept(orbital, first_col, col_blocks)
            ),
        )

        @pl.when(wanted)
        def _():
            state[count] = orbital
            columns = jnp.int32(0)
            for col in range(col_tiles):
                held = any_kept(orbital, first_col + col * col_tile, col_tile)
                columns = columns + jnp.where(held, 1 << col, 0)
            state[columns_at + count] = columns
            for tile in range(row_tiles):
                held = any_kept(orbital, first_row + tile * row_tile, row_tile)
                state[met_at + tile] = state[met_at + tile] + jnp.where(held, 1 << count, 0)

        return count + jnp.where(wanted, 1, 0)

    for tile in range(row_tiles):
        state[met_at + tile] = 0
    count = lax.fori_loop(0, orbitals, survey, jnp.int32(0))
    done[...] = jnp.zeros(done.shape, done.dtype)

    def fetch(begin):
        def one(slot, carry):
            orbital = state[begin + slot]

            def step(block, carry):
                code = code_of(0, orbital, whole_block(block))

                @pl.when(code >= 0)
                def _():
                    if padded > depth:
                        items[slot, block, depth:] = jnp.zeros((padded - depth, BLK), items.dtype)
                    start_aux = 0
                    for group, buffers in enumerate(sources):
                        place = code_of(group, orbital, whole_block(block))

                        def run(n, buffers=buffers, place=place, start_aux=start_aux):
                            for aux, (buffer, offset) in enumerate(buffers[n]):
                                pltpu.make_async_copy(
                                    buffer.at[(place & (STRIDE - 1)) + offset],
                                    items.at[slot, block, pl.ds((start_aux + aux) * OBLK, OBLK)],
                                    in_sems.at[slot],
                                ).start()

                        branch(lax.shift_right_logical(place, 6), 0, len(buffers), run)
                        start_aux += group_aux[group]

                @pl.when(code < 0)
                def _():
                    items[slot, block] = jnp.zeros((padded, BLK), items.dtype)

                return carry

            return lax.fori_loop(0, blocks, step, carry)

        lax.fori_loop(0, jnp.minimum(count - begin, room), one, 0)

    def landed(begin):
        def one(slot, carry):
            orbital = state[begin + slot]

            def step(block, carry):
                @pl.when(code_of(0, orbital, whole_block(block)) >= 0)
                def _():
                    whole = items.at[slot, block, pl.ds(0, depth)]
                    pltpu.make_async_copy(whole, whole, in_sems.at[slot]).wait()

                return carry

            return lax.fori_loop(0, blocks, step, carry)

        lax.fori_loop(0, jnp.minimum(count - begin, room), one, 0)

    def multiply(begin, tile):
        rows = span_of(tile)

        def one(slot, carry):
            @pl.when(lax.rem(lax.shift_right_logical(state[met_at + tile], begin + slot), 2) == 1)
            def _():
                turned = []
                for start in range(0, row_tile, step_tile):
                    left = jnp.concatenate(
                        [items[slot, tile * row_tile + start + step] for step in range(step_tile)],
                        axis=1,
                    )
                    turned.append(lax.dot_general(
                        unit[...], left, (((1,), (1,)), ((), ())), preferred_element_type=jnp.float32
                    ).astype(left.dtype))
                turned = jnp.concatenate(turned, axis=0)
                columns = state[columns_at + begin + slot]

                def column(col, carry):
                    @pl.when(lax.rem(lax.shift_right_logical(columns, col), 2) == 1)
                    def _():
                        right = jnp.concatenate(
                            [items[slot, first_right + col * col_tile + step] for step in range(col_tile)],
                            axis=1,
                        )
                        span = pl.ds(pl.multiple_of(col * width, width), width)
                        acc[rows, span] += jnp.dot(turned, right, preferred_element_type=jnp.float32)

                    return carry

                lax.fori_loop(0, col_tiles, column, 0)

            return carry

        lax.fori_loop(0, jnp.minimum(count - begin, room), one, 0)

    fetch(0)
    if first:
        def clear(tile, carry):
            acc[span_of(tile)] = jnp.zeros((height, acc.shape[1]), acc.dtype)
            return carry
    else:
        def clear(tile, carry):
            @pl.when(state[met_at + tile] > 0)
            def _():
                entering(tile).start()
            return carry

    lax.fori_loop(0, row_tiles, clear, 0)
    across = lax.broadcasted_iota(jnp.int32, unit.shape, 1)
    unit[...] = as_number(lax.broadcasted_iota(jnp.int32, unit.shape, 0) == across).astype(unit.dtype)
    passes = (count + room - 1) // room
    if first:
        passes = jnp.maximum(passes, 1)

    def one_pass(turn, carry):
        begin = turn * room

        @pl.when(turn > 0)
        def _():
            fetch(begin)

        landed(begin)

        def row_step(tile, carry):
            touched = jnp.logical_or(first, state[met_at + tile] > 0)

            @pl.when(touched)
            def _():
                if not first:
                    @pl.when(turn == 0)
                    def _():
                        entering(tile).wait()
                multiply(begin, tile)

                @pl.when(turn == passes - 1)
                def _():
                    leaving(tile).start()

            return carry

        lax.fori_loop(0, row_tiles, row_step, 0)
        return carry

    lax.fori_loop(0, passes, one_pass, 0)

    def row_end(tile, carry):
        @pl.when(jnp.logical_or(first, state[met_at + tile] > 0))
        def _():
            leaving(tile).wait()

        return carry

    lax.fori_loop(0, row_tiles, row_end, 0)


def tile_of(blocks):
    return 4 if blocks % 4 == 0 else 3 if blocks % 3 == 0 else 1


def product(loc, meta, sources, held, after, stages, orbitals, row_blocks, col_blocks):
    groups = [[[offset for _, offset in refs] for refs in group] for group in sources]
    flat = [array for group in sources for refs in group for array, _ in refs]
    total_aux = sum(len(group[0]) for group in sources)
    rows, cols = row_blocks * BLK, col_blocks * BLK
    row_tile = tile_of(row_blocks)
    step_tile = 2 if row_tile % 2 == 0 else row_tile
    row_tiles = row_blocks // row_tile
    padded = -(-total_aux * OBLK // 256) * 256
    room = 2
    first = held is None
    in_hbm = pl.BlockSpec(memory_space=pltpu.HBM)
    in_any = pl.BlockSpec(memory_space=pl.ANY)
    return pl.pallas_call(
        functools.partial(
            product_kernel, groups, orbitals, row_blocks, col_blocks, stages, first, len(after)
        ),
        grid_spec=pltpu.PrefetchScalarGridSpec(
            num_scalar_prefetch=2,
            grid=(),
            in_specs=[in_hbm] * (not first)
            + [in_any] * (len(flat) + len(after)),
            out_specs=[in_hbm, pl.BlockSpec(memory_space=pltpu.VMEM)],
            scratch_shapes=[
                pltpu.VMEM((room, row_blocks + col_blocks, padded, BLK), jnp.bfloat16),
                pltpu.VMEM((rows, cols), jnp.float32),
                pltpu.VMEM((step_tile * BLK, step_tile * BLK), jnp.bfloat16),
                pltpu.SMEM((2 * orbitals + row_tiles,), jnp.int32),
                pltpu.SemaphoreType.DMA((room,)),
                pltpu.SemaphoreType.DMA((row_tiles,)),
                pltpu.SemaphoreType.DMA((row_tiles,)),
            ],
        ),
        out_shape=[
            jax.ShapeDtypeStruct((rows, cols), jnp.float32),
            jax.ShapeDtypeStruct((8, 128), jnp.float32),
        ],
        input_output_aliases={} if first else {2: 0},
        compiler_params=pltpu.CompilerParams(
            vmem_limit_bytes=2 * room * padded * (rows + cols) + 4 * rows * cols + 4 * MIB
        ),
        cost_estimate=pl.CostEstimate(
            flops=2 * rows * cols * total_aux * OBLK * orbitals,
            bytes_accessed=4 * rows * cols,
            transcendentals=0,
        ),
        name="product",
    )(loc, meta, *([] if first else [held]), *flat, *after)


def rounds(size, add, table, own):
    first = [(0, 1), (1, 0), (2, 3), (3, 2)]
    second = []
    for aux in range(4):
        here, there = aux * 4, (aux ^ 1) * 4
        second += [(here, there), (here + 1, here + 2), (here + 2, here + 1), (here + 3, there + 3)]
    across = [(0, 2), (2, 0), (1, 3), (3, 1)]

    def to_core(held):
        return lax.ppermute(held, "aux", first)

    moved, crossed, passed = [], [], []
    core_own = to_core(own)
    total, done = None, []
    calls = {2: (0, 1), 3: (2, 2), 4: (3, 3), 5: (4, 4)}
    if size == LEVELS[-1]:
        calls = {ROUNDS: (0, HOPS)}
    for turn in range(ROUNDS + 1):
        chunks = []
        if turn < ROUNDS:
            arrived = moved[-2:] + crossed[-1:]
            chunks = gather(turn, size, table, [own] + moved, arrived, done)
        if turn > 0:
            if turn < ROUNDS:
                passed.append(to_core(chunks[-1]))
            elif done:
                passed.append(to_core(relay(crossed[-1], done[0])))
            else:
                passed.append(to_core(crossed[-1]))
        if turn in calls:
            near = [[(own, 0), (core_own, 0)]]
            for index, held in enumerate(moved):
                near.append([(held, 0), (passed[index // 2], index % 2 * size)])
            far = [
                [(held, 0), (passed[index], 2 * size if index < HOPS else 0)]
                for index, held in enumerate(crossed)
            ]
            total, token = add(
                table[3 * PLACES:6 * PLACES], [near, far], total, chunks[:1], calls[turn]
            )
            done = [token]
        if turn < HOPS:
            moved.append(lax.ppermute(chunks[0], "occ", first))
            moved.append(lax.ppermute(chunks[1], ("aux", "occ"), second))
        if turn < ROUNDS:
            crossed.append(lax.ppermute(chunks[2 if turn < HOPS else 0], "aux", across))
    return total


def on_device(shape, factors, block_mask, block_lists):
    aux_count, occ_count = shape["aux"], shape["occ"]
    own_orbitals, slots = block_lists.shape
    aux, occ = lax.axis_index("aux"), lax.axis_index("occ")
    row_blocks, col_blocks = NB // aux_count, NB // occ_count
    meta = jnp.stack([aux * row_blocks, occ * col_blocks]).astype(jnp.int32)

    def add(loc, sources, held, after, stages):
        return product(loc, meta, sources, held, after, stages, NOB, row_blocks, col_blocks)

    kept = block_mask.T > 0
    if aux_count == 4 and occ_count == 4 and shape["parts"] == 2:
        mask = as_number(kept).reshape(1, PLACES)
        other = lax.ppermute(mask, "parts", [(0, 1), (1, 0)])
        where = jnp.stack([aux, occ]).astype(jnp.int32)
        table = plan(where, jnp.concatenate([mask, other]), slots)
        own = pick(factors, block_lists, [table])
        return lax.switch(
            table[6, 0],
            [functools.partial(rounds, size, add) for size in LEVELS],
            table.reshape(-1),
            own,
        )
    own = pick(factors, block_lists)
    everything = lax.all_gather(lax.all_gather(own, "aux"), "occ")
    sources = [[(everything[z, a], 0) for a in range(aux_count)] for z in range(occ_count)]
    earlier = jnp.arange(NB)[None, :] < jnp.arange(NB)[:, None]
    rank = jnp.sum(kept[:, None, :] & earlier[None], axis=2, dtype=jnp.int32)
    orbital = jnp.arange(NOB, dtype=jnp.int32)[:, None]
    start = orbital // own_orbitals * STRIDE + orbital % own_orbitals * slots
    loc = jnp.concatenate([
        jnp.where(kept, rank + start, -1).reshape(-1), jnp.zeros(PLACES, jnp.int32)
    ])
    return add(loc, [sources], None, [], (0, 0))[0]


def solution(mesh):
    placed = (P(("parts", "aux"), "occ", None), P("parts", None), P(("parts", "occ"), None))
    return jax.shard_map(
        functools.partial(on_device, dict(mesh.shape)),
        mesh=mesh,
        in_specs=placed,
        out_specs=P(("parts", "aux"), "occ"),
        check_vma=False,
    )
```

```python
import functools
import math

import jax
import jax.numpy as jnp
from jax import lax
from jax.experimental import pallas as pl
from jax.experimental.pallas import tpu as pltpu
from jax.sharding import PartitionSpec as P

BLK = 128
OBLK = 112
NB = 48
NOB = 8
PLACES = NOB * NB
STRIDE = 64
ROUNDS = 5
HOPS = ROUNDS - 1
LEVELS = (16, 18, 21, 48)
MIB = 1024 * 1024


def pick_kernel(lists, factors, *refs):
    items = refs[-1]
    orbitals, slots = lists.shape

    def step(slot, carry):
        for orbital in range(orbitals):
            block = jnp.maximum(lists[orbital, slot], 0)
            columns = pl.ds(pl.multiple_of(block * BLK, BLK), BLK)
            rows = slice(orbital * OBLK, (orbital + 1) * OBLK)
            items[orbital * slots + slot] = factors[0, rows, columns]
        return carry

    lax.fori_loop(0, slots, step, 0)


def pick(factors, block_lists, after=()):
    orbitals, slots = block_lists.shape
    count = orbitals * slots
    return pl.pallas_call(
        pick_kernel,
        grid_spec=pltpu.PrefetchScalarGridSpec(
            num_scalar_prefetch=1,
            grid=(),
            in_specs=[pl.BlockSpec(memory_space=pltpu.VMEM)]
            + [pl.BlockSpec(memory_space=pl.ANY)] * len(after),
            out_specs=pl.BlockSpec(memory_space=pltpu.VMEM),
        ),
        out_shape=jax.ShapeDtypeStruct((count, OBLK, BLK), factors.dtype),
        compiler_params=pltpu.CompilerParams(vmem_limit_bytes=16 * MIB),
        cost_estimate=pl.CostEstimate(
            flops=0, bytes_accessed=4 * count * OBLK * BLK, transcendentals=0
        ),
        name="pick",
    )(block_lists, factors, *after)


def as_number(condition):
    return jnp.where(condition, 1.0, 0.0)


def place_facts(shape, axis):
    place = lax.broadcasted_iota(jnp.int32, shape, axis).astype(jnp.float32)
    orbital = jnp.floor((place + 0.5) / NB)
    block = place - NB * orbital
    quarter = jnp.floor((block + 0.5) / (NB // 4))
    return place, orbital, quarter, jnp.floor((quarter + 0.5) / 2), jnp.floor((orbital + 0.5) / 2)


def plan_kernel(slots, where, masks, out):
    levels = 8
    rows = 2 * levels
    wide = (rows, PLACES)
    _, orbital, quarter, half, origin = place_facts(wide, 1)
    row = lax.broadcasted_iota(jnp.int32, wide, 0)
    kept = jnp.where(row < levels, masks[0:1, :], masks[1:2, :])
    capacity = jnp.zeros(wide, jnp.float32)
    for index, size in enumerate(LEVELS + LEVELS[-1:] * (levels - len(LEVELS))):
        capacity = jnp.where((row == index) | (row == index + levels), float(size), capacity)

    square = (PLACES, PLACES)
    down_place, down_orbital, _, _, _ = place_facts(square, 0)
    over_place, over_orbital, _, _, _ = place_facts(square, 1)
    same = as_number(down_orbital == over_orbital)
    before = as_number(down_place < over_place)
    within = (same * before).astype(jnp.bfloat16)
    same, before = same.astype(jnp.bfloat16), before.astype(jnp.bfloat16)

    def times(parts, matrix):
        stacked = jnp.concatenate(parts, axis=0).astype(jnp.bfloat16)
        product = jnp.dot(stacked, matrix, preferred_element_type=jnp.float32)
        return [product[index * rows:(index + 1) * rows] for index in range(len(parts))]

    touching = times([kept * as_number(quarter == z) for z in range(4)], same)
    need = [kept * as_number(touch > 0) for touch in touching]
    zero = jnp.zeros(wide, jnp.float32)

    def union(parts):
        best = zero
        for part in parts:
            best = jnp.maximum(best, part)
        return best

    x_need = []
    for x in range(2):
        touched = as_number(touching[2 * x] + touching[2 * x + 1] > 0)
        here = as_number(half == x)
        x_need.append([
            need[z] * jnp.maximum(here, as_number(quarter == z) * touched) for z in range(4)
        ])
    mine = [kept * as_number(origin == z) for z in range(4)]
    need_up = [union(need[z + 1:]) for z in range(4)]
    far_up = [union(need[z + 2:]) for z in range(4)]
    need_down = [union(need[:z]) for z in range(4)]
    far_down = [union(need[:max(z - 1, 0)]) for z in range(4)]
    up = [mine[z] * need_up[z] for z in range(4)]
    down = [mine[z] * need_down[z] for z in range(4)]
    cross = [[mine[z] * x_need[x][z] for z in range(4)] for x in range(2)]
    up_code, down_code = [zero] * 4, [zero] * 4
    cross_code = [[zero] * 4, [zero] * 4]

    for turn in range(ROUNDS):
        parts = []
        if turn < HOPS:
            for z in range(3):
                parts += [up[z] * far_up[z], up[z] - up[z] * far_up[z]]
                parts += [down[z + 1] * far_down[z + 1], down[z + 1] - down[z + 1] * far_down[z + 1]]
        parts += [cross[x][z] for x in range(2) for z in range(4)]
        ranks = iter(zip(parts, times(parts, before)))

        def taken(pairs):
            rank, total = zero, 0.0
            chosen = zero
            for part, counted in pairs:
                rank = rank + part * (counted + total)
                total = total + jnp.sum(part, axis=1, keepdims=True)
                chosen = chosen + part
            chosen = chosen * as_number(rank < capacity)
            return chosen, chosen * (rank + float(turn * STRIDE + 1))

        up_sent, down_sent = [], []
        if turn < HOPS:
            for z in range(3):
                sent, code = taken([next(ranks), next(ranks)])
                up_sent.append(sent)
                up_code[z] = up_code[z] + code
                up[z] = up[z] - sent
                sent, code = taken([next(ranks), next(ranks)])
                down_sent.append(sent)
                down_code[z + 1] = down_code[z + 1] + code
                down[z + 1] = down[z + 1] - sent
        for x in range(2):
            for z in range(4):
                sent, code = taken([next(ranks)])
                cross_code[x][z] = cross_code[x][z] + code
                cross[x][z] = cross[x][z] - sent
        if turn < HOPS:
            for z in range(3):
                up[z + 1] = up[z + 1] + up_sent[z] * need_up[z + 1]
                down[z] = down[z] + down_sent[z] * need_down[z]
                for x in range(2):
                    cross[x][z + 1] = cross[x][z + 1] + up_sent[z] * x_need[x][z + 1]
                    cross[x][z] = cross[x][z] + down_sent[z] * x_need[x][z]

    left = zero
    for part in up + down + cross[0] + cross[1]:
        left = left + part
    left = jnp.sum(left, axis=1, keepdims=True)
    left = left[:levels] + left[levels:]
    order = lax.broadcasted_iota(jnp.int32, (levels, 1), 0).astype(jnp.float32)
    level = jnp.min(jnp.where(left > 0, float(len(LEVELS) - 1), order), axis=0, keepdims=True)
    level_row = as_number(
        lax.broadcasted_iota(jnp.int32, (levels, PLACES), 0).astype(jnp.float32) == level
    )
    me_x, me_z = where[0] // 2, where[1]
    odd = lax.rem(me_z, 2).astype(jnp.float32)

    def at(parts, z):
        total = jnp.zeros((levels, PLACES), jnp.float32)
        for index, part in enumerate(parts):
            total = total + jnp.where(z == index, 1.0, 0.0) * part[:levels]
        return jnp.sum(total * level_row, axis=0, keepdims=True)

    cross_here = [jnp.where(me_x == 0, cross_code[0][z], cross_code[1][z]) for z in range(4)]
    cross_there = [jnp.where(me_x == 0, cross_code[1][z], cross_code[0][z]) for z in range(4)]
    def turn_of(code):
        return jnp.floor((code - 0.5) / STRIDE)

    got_up, got_down = at(up_code, me_z - 1), at(down_code, me_z + 1)
    got_cross = at(cross_here, me_z)
    inner = jnp.dot(kept.astype(jnp.bfloat16), within, preferred_element_type=jnp.float32)[0:1]
    one_orbital, one_origin = orbital[0:1], origin[0:1]
    slot = inner + slots * (one_orbital - 2 * one_origin)
    owned = kept[0:1] * as_number(one_origin == me_z.astype(jnp.float32))
    held = (
        owned * (slot + 1)
        + as_number(got_up > 0) * (got_up + STRIDE * (2 - odd + turn_of(got_up)))
        + as_number(got_down > 0) * (got_down + STRIDE * (1 + odd + turn_of(got_down)))
        - 1
    )
    crossed = got_cross - 1
    near = jnp.maximum(
        as_number(quarter[0:1] == where[0].astype(jnp.float32)),
        as_number(quarter[0:1] == me_z.astype(jnp.float32)),
    )
    arrival = jnp.maximum(
        as_number(got_up + got_down > 0) * turn_of(got_up + got_down),
        as_number(got_cross > 0) * turn_of(got_cross),
    )
    lane = lax.broadcasted_iota(jnp.int32, (1, PLACES), 1)
    stage = jnp.zeros((1, PLACES), jnp.float32)
    for index in range(NOB):
        inside = as_number(one_orbital == float(index)) * near * kept[0:1]
        stage = jnp.where(
            lane == index, jnp.max(arrival * inside, axis=1, keepdims=True), stage
        )

    buffer = jnp.floor((held + 0.5) / STRIDE)
    tall = (PLACES, PLACES)
    target = lax.broadcasted_iota(jnp.int32, tall, 0).astype(jnp.float32) + 1
    pair = jnp.concatenate([buffer, held - STRIDE * buffer] + [jnp.zeros_like(held)] * 6, axis=0)
    sends = []
    sent_up, sent_down = at(up_code, me_z), at(down_code, me_z)
    for sent in (
        jnp.where(odd > 0, sent_down, sent_up),
        jnp.where(odd > 0, sent_up, sent_down),
        at(cross_there, me_z),
    ):
        chosen = as_number(target == sent).astype(jnp.bfloat16)
        both = lax.dot_general(
            pair.astype(jnp.bfloat16), chosen, (((1,), (1,)), ((), ())),
            preferred_element_type=jnp.float32,
        )
        sends.append(both[0:1] * STRIDE + both[1:2])
    flat = level + jnp.zeros((1, PLACES), jnp.float32)
    result = jnp.concatenate(sends + [held, crossed, stage, flat, flat], axis=0)
    out[...] = result.astype(jnp.int32)


def plan(where, masks, slots):
    in_vmem = pl.BlockSpec(memory_space=pltpu.VMEM)
    return pl.pallas_call(
        functools.partial(plan_kernel, slots),
        grid_spec=pltpu.PrefetchScalarGridSpec(
            num_scalar_prefetch=1, grid=(), in_specs=[in_vmem], out_specs=in_vmem
        ),
        out_shape=jax.ShapeDtypeStruct((8, PLACES), jnp.int32),
        compiler_params=pltpu.CompilerParams(vmem_limit_bytes=16 * MIB),
        name="plan",
    )(where, masks)


def branch(which, low, high, run):
    if high - low == 1:
        run(low)
        return
    middle = (low + high) // 2

    @pl.when(which < middle)
    def _():
        branch(which, low, middle, run)

    @pl.when(which >= middle)
    def _():
        branch(which, middle, high, run)


def gather_kernel(turn, held, streams, passed, table, *refs):
    buffers, refs = refs[:held], refs[held:]
    arrived, outs = refs[:passed], refs[len(refs) - len(streams) - (passed > 0):]
    size = outs[0].shape[0]

    def step(index, carry):
        for stream, out in zip(streams, outs):
            code = table[stream * PLACES + turn * STRIDE + index]

            def run(n, out=out, code=code):
                out[index] = buffers[n][code & (STRIDE - 1)]

            branch(lax.shift_right_logical(code, 6), 0, held, run)
        for place in range(passed):
            outs[-1][place * size + index] = arrived[place][index]
        return carry

    lax.fori_loop(0, size, step, 0)


def gather(turn, size, table, buffers, streams, arrived, after):
    dtype = buffers[0].dtype
    shapes = [jax.ShapeDtypeStruct((size, OBLK, BLK), dtype) for _ in streams]
    if arrived:
        shapes.append(jax.ShapeDtypeStruct((size * len(arrived), OBLK, BLK), dtype))
    in_vmem = pl.BlockSpec(memory_space=pltpu.VMEM)
    return pl.pallas_call(
        functools.partial(gather_kernel, turn, len(buffers), streams, len(arrived)),
        grid_spec=pltpu.PrefetchScalarGridSpec(
            num_scalar_prefetch=1,
            grid=(),
            in_specs=[in_vmem] * (len(buffers) + len(arrived))
            + [pl.BlockSpec(memory_space=pl.ANY)] * len(after),
            out_specs=[in_vmem] * len(shapes),
        ),
        out_shape=shapes,
        compiler_params=pltpu.CompilerParams(
            vmem_limit_bytes=2 * sum(array.size for array in [*buffers, *arrived, *shapes]) + 4 * MIB
        ),
        cost_estimate=pl.CostEstimate(
            flops=0, bytes_accessed=4 * len(streams) * size * OBLK * BLK, transcendentals=0
        ),
        name="gather",
    )(table, *buffers, *arrived, *after)


def relay_kernel(source, token, out):
    out[...] = source[...]


def relay(source, token):
    in_vmem = pl.BlockSpec(memory_space=pltpu.VMEM)
    return pl.pallas_call(
        relay_kernel,
        in_specs=[in_vmem, pl.BlockSpec(memory_space=pl.ANY)],
        out_specs=in_vmem,
        out_shape=jax.ShapeDtypeStruct(source.shape, source.dtype),
        compiler_params=pltpu.CompilerParams(vmem_limit_bytes=16 * MIB),
        name="relay",
    )(source, token)


def product_kernel(
    groups, orbitals, row_blocks, col_blocks, stages, first, extra, loc, meta, *refs
):
    flat = iter(refs)
    before = None if first else next(flat)
    sources = [
        [[(next(flat), offset) for offset in offsets] for offsets in buffers] for buffers in groups
    ]
    for _ in range(extra):
        next(flat)
    out, done, items, acc, unit, state, in_sems, acc_sems, out_sems = flat
    group_aux = [len(buffers[0]) for buffers in groups]
    row_tile, col_tile = tile_of(row_blocks), tile_of(col_blocks)
    step_tile = unit.shape[0] // BLK
    col_tiles = col_blocks // col_tile
    first_row, first_col = meta[0], meta[1]
    room = items.shape[0]
    quad = math.gcd(row_blocks, col_blocks, 4)
    if quad == 1:
        quad = math.gcd(row_blocks, col_blocks)
    blocks, first_right = row_blocks + col_blocks, row_blocks
    if row_blocks == col_blocks:
        alike = first_row == first_col
        blocks = jnp.where(alike, row_blocks, blocks)
        first_right = jnp.where(alike, 0, first_right)
    depth = sum(group_aux) * OBLK
    padded = items.shape[2]
    height, width = row_tile * BLK, col_tile * BLK
    row_tiles = row_blocks // row_tile
    met_at, columns_at = orbitals, orbitals + row_tiles

    def code_of(group, orbital, block):
        return loc[group * PLACES + orbital * NB + block]

    def any_kept(orbital, start, count):
        best = code_of(0, orbital, start)
        for step in range(1, count):
            best = jnp.maximum(best, code_of(0, orbital, start + step))
        return best >= 0

    def whole_block(block):
        return jnp.where(block < row_blocks, first_row + block, first_col + block - row_blocks)

    def span_of(tile):
        return pl.ds(pl.multiple_of(tile * height, height), height)

    def entering(tile):
        return pltpu.make_async_copy(before.at[span_of(tile)], acc.at[span_of(tile)], acc_sems.at[tile])

    def leaving(tile):
        return pltpu.make_async_copy(acc.at[span_of(tile)], out.at[span_of(tile)], out_sems.at[tile])

    def survey(orbital, count):
        stage = loc[len(groups) * PLACES + orbital]
        wanted = jnp.logical_and(stage >= stages[0], stage <= stages[1])
        state[columns_at + count] = 0

        @pl.when(wanted)
        def _():
            @pl.when(any_kept(orbital, first_row, row_blocks))
            def _():
                columns = jnp.int32(0)
                for col in range(col_tiles):
                    held = any_kept(orbital, first_col + col * col_tile, col_tile)
                    columns = columns + jnp.where(held, 1 << col, 0)
                state[columns_at + count] = columns

        wanted = state[columns_at + count] > 0

        @pl.when(wanted)
        def _():
            state[count] = orbital
            for tile in range(row_tiles):
                held = any_kept(orbital, first_row + tile * row_tile, row_tile)
                state[met_at + tile] = state[met_at + tile] + jnp.where(held, 1 << count, 0)

        return count + jnp.where(wanted, 1, 0)

    for tile in range(row_tiles):
        state[met_at + tile] = 0
    count = lax.fori_loop(0, orbitals, survey, jnp.int32(0))
    done[...] = jnp.zeros(done.shape, done.dtype)

    def fetch(begin):
        def one(slot, carry):
            orbital = state[begin + slot]

            def load(block, run):
                start_aux = 0
                for group, buffers in enumerate(sources):
                    place = code_of(group, orbital, whole_block(block))

                    def copy(n, buffers=buffers, place=place, start_aux=start_aux):
                        for aux, (buffer, offset) in enumerate(buffers[n]):
                            pltpu.make_async_copy(
                                buffer.at[pl.ds((place & (STRIDE - 1)) + offset, run)],
                                items.at[
                                    slot, pl.ds(block, run), pl.ds((start_aux + aux) * OBLK, OBLK)
                                ],
                                in_sems.at[slot],
                            ).start()

                    branch(lax.shift_right_logical(place, 6), 0, len(buffers), copy)
                    start_aux += group_aux[group]
                if padded > depth:
                    items[slot, pl.ds(block, run), depth:] = jnp.zeros(
                        (run, padded - depth, BLK), items.dtype
                    )

            def step(part, carry):
                block = part * quad
                in_row = code_of(0, orbital, whole_block(block)) >= 0
                for group in range(len(groups)):
                    low = code_of(group, orbital, whole_block(block))
                    high = code_of(group, orbital, whole_block(block) + quad - 1)
                    in_row = jnp.logical_and(in_row, high - low == quad - 1)

                @pl.when(in_row)
                def _():
                    load(block, quad)

                @pl.when(jnp.logical_not(in_row))
                def _():
                    def single(inner, carry):
                        held = code_of(0, orbital, whole_block(block + inner)) >= 0

                        @pl.when(held)
                        def _():
                            load(block + inner, 1)

                        @pl.when(jnp.logical_not(held))
                        def _():
                            items[slot, block + inner] = jnp.zeros((padded, BLK), items.dtype)

                        return carry

                    lax.fori_loop(0, quad, single, 0)

                return carry

            return lax.fori_loop(0, blocks // quad, step, carry)

        lax.fori_loop(0, jnp.minimum(count - begin, room), one, 0)

    def landed(begin):
        def one(slot, carry):
            orbital = state[begin + slot]

            def step(block, carry):
                @pl.when(code_of(0, orbital, whole_block(block)) >= 0)
                def _():
                    whole = items.at[slot, block, pl.ds(0, depth)]
                    pltpu.make_async_copy(whole, whole, in_sems.at[slot]).wait()

                return carry

            return lax.fori_loop(0, blocks, step, carry)

        lax.fori_loop(0, jnp.minimum(count - begin, room), one, 0)

    def multiply(begin, tile):
        rows = span_of(tile)

        def one(slot, carry):
            @pl.when(lax.rem(lax.shift_right_logical(state[met_at + tile], begin + slot), 2) == 1)
            def _():
                turned = []
                for start in range(0, row_tile, step_tile):
                    left = jnp.concatenate(
                        [items[slot, tile * row_tile + start + step] for step in range(step_tile)],
                        axis=1,
                    )
                    turned.append(lax.dot_general(
                        unit[...], left, (((1,), (1,)), ((), ())), preferred_element_type=jnp.float32
                    ).astype(left.dtype))
                turned = jnp.concatenate(turned, axis=0)
                columns = state[columns_at + begin + slot]

                def column(col, carry):
                    @pl.when(lax.rem(lax.shift_right_logical(columns, col), 2) == 1)
                    def _():
                        right = jnp.concatenate(
                            [items[slot, first_right + col * col_tile + step] for step in range(col_tile)],
                            axis=1,
                        )
                        span = pl.ds(pl.multiple_of(col * width, width), width)
                        acc[rows, span] += jnp.dot(turned, right, preferred_element_type=jnp.float32)

                    return carry

                lax.fori_loop(0, col_tiles, column, 0)

            return carry

        lax.fori_loop(0, jnp.minimum(count - begin, room), one, 0)

    fetch(0)
    if first:
        def clear(tile, carry):
            acc[span_of(tile)] = jnp.zeros((height, acc.shape[1]), acc.dtype)
            return carry
    else:
        def clear(tile, carry):
            @pl.when(state[met_at + tile] > 0)
            def _():
                entering(tile).start()
            return carry

    lax.fori_loop(0, row_tiles, clear, 0)
    across = lax.broadcasted_iota(jnp.int32, unit.shape, 1)
    unit[...] = as_number(lax.broadcasted_iota(jnp.int32, unit.shape, 0) == across).astype(unit.dtype)
    passes = (count + room - 1) // room
    if first:
        passes = jnp.maximum(passes, 1)

    def one_pass(turn, carry):
        begin = turn * room

        @pl.when(turn > 0)
        def _():
            fetch(begin)

        landed(begin)

        def row_step(tile, carry):
            touched = jnp.logical_or(first, state[met_at + tile] > 0)

            @pl.when(touched)
            def _():
                if not first:
                    @pl.when(turn == 0)
                    def _():
                        entering(tile).wait()
                multiply(begin, tile)

                @pl.when(turn == passes - 1)
                def _():
                    leaving(tile).start()

            return carry

        lax.fori_loop(0, row_tiles, row_step, 0)
        return carry

    lax.fori_loop(0, passes, one_pass, 0)

    def row_end(tile, carry):
        @pl.when(jnp.logical_or(first, state[met_at + tile] > 0))
        def _():
            leaving(tile).wait()

        return carry

    lax.fori_loop(0, row_tiles, row_end, 0)


def tile_of(blocks):
    return 4 if blocks % 4 == 0 else 3 if blocks % 3 == 0 else 1


def product(loc, meta, sources, held, after, stages, orbitals, row_blocks, col_blocks):
    groups = [[[offset for _, offset in refs] for refs in group] for group in sources]
    flat = [array for group in sources for refs in group for array, _ in refs]
    total_aux = sum(len(group[0]) for group in sources)
    rows, cols = row_blocks * BLK, col_blocks * BLK
    row_tile = tile_of(row_blocks)
    step_tile = 2 if row_tile % 2 == 0 else row_tile
    row_tiles = row_blocks // row_tile
    padded = -(-total_aux * OBLK // 256) * 256
    room = 2
    first = held is None
    in_hbm = pl.BlockSpec(memory_space=pltpu.HBM)
    in_any = pl.BlockSpec(memory_space=pl.ANY)
    return pl.pallas_call(
        functools.partial(
            product_kernel, groups, orbitals, row_blocks, col_blocks, stages, first, len(after)
        ),
        grid_spec=pltpu.PrefetchScalarGridSpec(
            num_scalar_prefetch=2,
            grid=(),
            in_specs=[in_hbm] * (not first)
            + [in_any] * (len(flat) + len(after)),
            out_specs=[in_hbm, pl.BlockSpec(memory_space=pltpu.VMEM)],
            scratch_shapes=[
                pltpu.VMEM((room, row_blocks + col_blocks, padded, BLK), jnp.bfloat16),
                pltpu.VMEM((rows, cols), jnp.float32),
                pltpu.VMEM((step_tile * BLK, step_tile * BLK), jnp.bfloat16),
                pltpu.SMEM((2 * orbitals + row_tiles + 1,), jnp.int32),
                pltpu.SemaphoreType.DMA((room,)),
                pltpu.SemaphoreType.DMA((row_tiles,)),
                pltpu.SemaphoreType.DMA((row_tiles,)),
            ],
        ),
        out_shape=[
            jax.ShapeDtypeStruct((rows, cols), jnp.float32),
            jax.ShapeDtypeStruct((8, 128), jnp.float32),
        ],
        input_output_aliases={} if first else {2: 0},
        compiler_params=pltpu.CompilerParams(
            vmem_limit_bytes=2 * room * padded * (rows + cols) + 4 * rows * cols + 4 * MIB
        ),
        cost_estimate=pl.CostEstimate(
            flops=2 * rows * cols * total_aux * OBLK * orbitals,
            bytes_accessed=4 * rows * cols,
            transcendentals=0,
        ),
        name="product",
    )(loc, meta, *([] if first else [held]), *flat, *after)


def rounds(size, add, table, own):
    first = [(0, 1), (1, 0), (2, 3), (3, 2)]
    second = []
    for aux in range(4):
        here, there = aux * 4, (aux ^ 1) * 4
        second += [(here, there), (here + 1, here + 2), (here + 2, here + 1), (here + 3, there + 3)]
    across = [(0, 2), (2, 0), (1, 3), (3, 1)]

    def to_core(held):
        return lax.ppermute(held, "aux", first)

    moved, crossed, passed = [], [], []
    core_own = to_core(own)
    total, done = None, []
    calls = {2: (0, 1), 3: (2, 2), 4: (3, 3), 5: (4, 4)}
    if size == LEVELS[-1]:
        calls = {ROUNDS: (0, HOPS)}
    for turn in range(ROUNDS + 1):
        chunks = []
        if turn < ROUNDS:
            streams = (0, 1, 2) if turn < HOPS else (2,)
            arrived = moved[-2:] + crossed[-1:]
            chunks = gather(turn, size, table, [own] + moved, streams, arrived, done)
        if turn > 0:
            if turn < ROUNDS:
                passed.append(to_core(chunks[-1]))
            elif done:
                passed.append(to_core(relay(crossed[-1], done[0])))
            else:
                passed.append(to_core(crossed[-1]))
        if turn in calls:
            near = [[(own, 0), (core_own, 0)]]
            for index, held in enumerate(moved):
                near.append([(held, 0), (passed[index // 2], index % 2 * size)])
            far = [
                [(held, 0), (passed[index], 2 * size if index < HOPS else 0)]
                for index, held in enumerate(crossed)
            ]
            total, token = add(
                table[3 * PLACES:6 * PLACES], [near, far], total, chunks[:1], calls[turn]
            )
            done = [token]
        if turn < HOPS:
            moved.append(lax.ppermute(chunks[0], "occ", first))
            moved.append(lax.ppermute(chunks[1], ("aux", "occ"), second))
        if turn < ROUNDS:
            crossed.append(lax.ppermute(chunks[2 if turn < HOPS else 0], "aux", across))
    return total


def on_device(shape, factors, block_mask, block_lists):
    aux_count, occ_count = shape["aux"], shape["occ"]
    own_orbitals, slots = block_lists.shape
    aux, occ = lax.axis_index("aux"), lax.axis_index("occ")
    row_blocks, col_blocks = NB // aux_count, NB // occ_count
    meta = jnp.stack([aux * row_blocks, occ * col_blocks]).astype(jnp.int32)

    def add(loc, sources, held, after, stages):
        return product(loc, meta, sources, held, after, stages, NOB, row_blocks, col_blocks)

    kept = block_mask.T > 0
    if aux_count == 4 and occ_count == 4 and shape["parts"] == 2:
        mask = as_number(kept).reshape(1, PLACES)
        other = lax.ppermute(mask, "parts", [(0, 1), (1, 0)])
        where = jnp.stack([aux, occ]).astype(jnp.int32)
        table = plan(where, jnp.concatenate([mask, other]), slots)
        own = pick(factors, block_lists, [table])
        return lax.switch(
            table[6, 0],
            [functools.partial(rounds, size, add) for size in LEVELS],
            table.reshape(-1),
            own,
        )
    own = pick(factors, block_lists)
    everything = lax.all_gather(lax.all_gather(own, "aux"), "occ")
    sources = [[(everything[z, a], 0) for a in range(aux_count)] for z in range(occ_count)]
    earlier = jnp.arange(NB)[None, :] < jnp.arange(NB)[:, None]
    rank = jnp.sum(kept[:, None, :] & earlier[None], axis=2, dtype=jnp.int32)
    orbital = jnp.arange(NOB, dtype=jnp.int32)[:, None]
    start = orbital // own_orbitals * STRIDE + orbital % own_orbitals * slots
    loc = jnp.concatenate([
        jnp.where(kept, rank + start, -1).reshape(-1), jnp.zeros(PLACES, jnp.int32)
    ])
    return add(loc, [sources], None, [], (0, 0))[0]


def solution(mesh):
    placed = (P(("parts", "aux"), "occ", None), P("parts", None), P(("parts", "occ"), None))
    return jax.shard_map(
        functools.partial(on_device, dict(mesh.shape)),
        mesh=mesh,
        in_specs=placed,
        out_specs=P(("parts", "aux"), "occ"),
        check_vma=False,
    )
```

```python
import functools
import math

import jax
import jax.numpy as jnp
from jax import lax
from jax.experimental import pallas as pl
from jax.experimental.pallas import tpu as pltpu
from jax.sharding import PartitionSpec as P

BLK = 128
OBLK = 112
NB = 48
NOB = 8
PLACES = NOB * NB
STRIDE = 64
ROUNDS = 5
HOPS = ROUNDS - 1
LEVELS = (15, 18, 21, 48)
RUN = 3
MIB = 1024 * 1024


def pick_kernel(lists, factors, *refs):
    items = refs[-1]
    orbitals, slots = lists.shape

    def step(slot, carry):
        for orbital in range(orbitals):
            block = jnp.maximum(lists[orbital, slot], 0)
            columns = pl.ds(pl.multiple_of(block * BLK, BLK), BLK)
            rows = slice(orbital * OBLK, (orbital + 1) * OBLK)
            items[orbital * slots + slot] = factors[0, rows, columns]
        return carry

    lax.fori_loop(0, slots, step, 0)


def pick(factors, block_lists, after=()):
    orbitals, slots = block_lists.shape
    count = orbitals * slots
    return pl.pallas_call(
        pick_kernel,
        grid_spec=pltpu.PrefetchScalarGridSpec(
            num_scalar_prefetch=1,
            grid=(),
            in_specs=[pl.BlockSpec(memory_space=pltpu.VMEM)]
            + [pl.BlockSpec(memory_space=pl.ANY)] * len(after),
            out_specs=pl.BlockSpec(memory_space=pltpu.VMEM),
        ),
        out_shape=jax.ShapeDtypeStruct((count, OBLK, BLK), factors.dtype),
        compiler_params=pltpu.CompilerParams(vmem_limit_bytes=16 * MIB),
        cost_estimate=pl.CostEstimate(
            flops=0, bytes_accessed=4 * count * OBLK * BLK, transcendentals=0
        ),
        name="pick",
    )(block_lists, factors, *after)


def as_number(condition):
    return jnp.where(condition, 1.0, 0.0)


def place_facts(shape, axis):
    place = lax.broadcasted_iota(jnp.int32, shape, axis).astype(jnp.float32)
    orbital = jnp.floor((place + 0.5) / NB)
    block = place - NB * orbital
    quarter = jnp.floor((block + 0.5) / (NB // 4))
    return place, orbital, quarter, jnp.floor((quarter + 0.5) / 2), jnp.floor((orbital + 0.5) / 2)


def plan_kernel(slots, where, masks, out):
    levels = 8
    rows = 2 * levels
    wide = (rows, PLACES)
    _, orbital, quarter, half, origin = place_facts(wide, 1)
    row = lax.broadcasted_iota(jnp.int32, wide, 0)
    kept = jnp.where(row < levels, masks[0:1, :], masks[1:2, :])
    capacity = jnp.zeros(wide, jnp.float32)
    for index, size in enumerate(LEVELS + LEVELS[-1:] * (levels - len(LEVELS))):
        capacity = jnp.where((row == index) | (row == index + levels), float(size), capacity)

    square = (PLACES, PLACES)
    down_place, down_orbital, _, _, _ = place_facts(square, 0)
    over_place, over_orbital, _, _, _ = place_facts(square, 1)
    same = as_number(down_orbital == over_orbital)
    before = as_number(down_place < over_place)
    within = (same * before).astype(jnp.bfloat16)
    same, before = same.astype(jnp.bfloat16), before.astype(jnp.bfloat16)

    def times(parts, matrix):
        stacked = jnp.concatenate(parts, axis=0).astype(jnp.bfloat16)
        product = jnp.dot(stacked, matrix, preferred_element_type=jnp.float32)
        return [product[index * rows:(index + 1) * rows] for index in range(len(parts))]

    touching = times([kept * as_number(quarter == z) for z in range(4)], same)
    need = [kept * as_number(touch > 0) for touch in touching]
    zero = jnp.zeros(wide, jnp.float32)

    def union(parts):
        best = zero
        for part in parts:
            best = jnp.maximum(best, part)
        return best

    x_need = []
    for x in range(2):
        touched = as_number(touching[2 * x] + touching[2 * x + 1] > 0)
        here = as_number(half == x)
        x_need.append([
            need[z] * jnp.maximum(here, as_number(quarter == z) * touched) for z in range(4)
        ])
    mine = [kept * as_number(origin == z) for z in range(4)]
    need_up = [union(need[z + 1:]) for z in range(4)]
    far_up = [union(need[z + 2:]) for z in range(4)]
    need_down = [union(need[:z]) for z in range(4)]
    far_down = [union(need[:max(z - 1, 0)]) for z in range(4)]
    up = [mine[z] * need_up[z] for z in range(4)]
    down = [mine[z] * need_down[z] for z in range(4)]
    cross = [[mine[z] * x_need[x][z] for z in range(4)] for x in range(2)]
    up_code, down_code = [zero] * 4, [zero] * 4
    cross_code = [[zero] * 4, [zero] * 4]

    for turn in range(ROUNDS):
        parts = []
        if turn < HOPS:
            for z in range(3):
                parts += [up[z] * far_up[z], up[z] - up[z] * far_up[z]]
                parts += [down[z + 1] * far_down[z + 1], down[z + 1] - down[z + 1] * far_down[z + 1]]
        parts += [cross[x][z] for x in range(2) for z in range(4)]
        ranks = iter(zip(parts, times(parts, before)))

        def taken(pairs):
            rank, total = zero, 0.0
            chosen = zero
            for part, counted in pairs:
                rank = rank + part * (counted + total)
                total = total + jnp.sum(part, axis=1, keepdims=True)
                chosen = chosen + part
            chosen = chosen * as_number(rank < capacity)
            return chosen, chosen * (rank + float(turn * STRIDE + 1))

        up_sent, down_sent = [], []
        if turn < HOPS:
            for z in range(3):
                sent, code = taken([next(ranks), next(ranks)])
                up_sent.append(sent)
                up_code[z] = up_code[z] + code
                up[z] = up[z] - sent
                sent, code = taken([next(ranks), next(ranks)])
                down_sent.append(sent)
                down_code[z + 1] = down_code[z + 1] + code
                down[z + 1] = down[z + 1] - sent
        for x in range(2):
            for z in range(4):
                sent, code = taken([next(ranks)])
                cross_code[x][z] = cross_code[x][z] + code
                cross[x][z] = cross[x][z] - sent
        if turn < HOPS:
            for z in range(3):
                up[z + 1] = up[z + 1] + up_sent[z] * need_up[z + 1]
                down[z] = down[z] + down_sent[z] * need_down[z]
                for x in range(2):
                    cross[x][z + 1] = cross[x][z + 1] + up_sent[z] * x_need[x][z + 1]
                    cross[x][z] = cross[x][z] + down_sent[z] * x_need[x][z]

    left = zero
    for part in up + down + cross[0] + cross[1]:
        left = left + part
    left = jnp.sum(left, axis=1, keepdims=True)
    left = left[:levels] + left[levels:]
    order = lax.broadcasted_iota(jnp.int32, (levels, 1), 0).astype(jnp.float32)
    level = jnp.min(jnp.where(left > 0, float(len(LEVELS) - 1), order), axis=0, keepdims=True)
    level_row = as_number(
        lax.broadcasted_iota(jnp.int32, (levels, PLACES), 0).astype(jnp.float32) == level
    )
    me_x, me_z = where[0] // 2, where[1]
    odd = lax.rem(me_z, 2).astype(jnp.float32)

    def at(parts, z):
        total = jnp.zeros((levels, PLACES), jnp.float32)
        for index, part in enumerate(parts):
            total = total + jnp.where(z == index, 1.0, 0.0) * part[:levels]
        return jnp.sum(total * level_row, axis=0, keepdims=True)

    cross_here = [jnp.where(me_x == 0, cross_code[0][z], cross_code[1][z]) for z in range(4)]
    cross_there = [jnp.where(me_x == 0, cross_code[1][z], cross_code[0][z]) for z in range(4)]
    def turn_of(code):
        return jnp.floor((code - 0.5) / STRIDE)

    got_up, got_down = at(up_code, me_z - 1), at(down_code, me_z + 1)
    got_cross = at(cross_here, me_z)
    inner = jnp.dot(kept.astype(jnp.bfloat16), within, preferred_element_type=jnp.float32)[0:1]
    one_orbital, one_origin = orbital[0:1], origin[0:1]
    slot = inner + slots * (one_orbital - 2 * one_origin)
    owned = kept[0:1] * as_number(one_origin == me_z.astype(jnp.float32))
    held = (
        owned * (slot + 1)
        + as_number(got_up > 0) * (got_up + STRIDE * (2 - odd + turn_of(got_up)))
        + as_number(got_down > 0) * (got_down + STRIDE * (1 + odd + turn_of(got_down)))
        - 1
    )
    crossed = got_cross - 1
    near = jnp.maximum(
        as_number(quarter[0:1] == where[0].astype(jnp.float32)),
        as_number(quarter[0:1] == me_z.astype(jnp.float32)),
    )
    arrival = jnp.maximum(
        as_number(got_up + got_down > 0) * turn_of(got_up + got_down),
        as_number(got_cross > 0) * turn_of(got_cross),
    )
    lane = lax.broadcasted_iota(jnp.int32, (1, PLACES), 1)
    stage = jnp.zeros((1, PLACES), jnp.float32)
    for index in range(NOB):
        inside = as_number(one_orbital == float(index)) * near * kept[0:1]
        stage = jnp.where(
            lane == index, jnp.max(arrival * inside, axis=1, keepdims=True), stage
        )

    buffer = jnp.floor((held + 0.5) / STRIDE)
    tall = (PLACES, PLACES)
    target = lax.broadcasted_iota(jnp.int32, tall, 0).astype(jnp.float32) + 1
    blank = jnp.zeros_like(held)
    pair = jnp.concatenate([buffer, held - STRIDE * buffer, blank + 1] + [blank] * 5, axis=0)
    position = lax.broadcasted_iota(jnp.int32, (1, PLACES), 1).astype(jnp.float32)
    spare = position - STRIDE * jnp.floor((position + 0.5) / STRIDE)
    sends = []
    sent_up, sent_down = at(up_code, me_z), at(down_code, me_z)
    for sent in (
        jnp.where(odd > 0, sent_down, sent_up),
        jnp.where(odd > 0, sent_up, sent_down),
        at(cross_there, me_z),
    ):
        chosen = as_number(target == sent).astype(jnp.bfloat16)
        both = lax.dot_general(
            pair.astype(jnp.bfloat16), chosen, (((1,), (1,)), ((), ())),
            preferred_element_type=jnp.float32,
        )
        filled = both[0:1] * STRIDE + both[1:2]
        sends.append(jnp.where(both[2:3] > 0, filled, spare))
    flat = level + jnp.zeros((1, PLACES), jnp.float32)
    result = jnp.concatenate(sends + [held, crossed, stage, flat, flat], axis=0)
    out[...] = result.astype(jnp.int32)


def plan(where, masks, slots):
    in_vmem = pl.BlockSpec(memory_space=pltpu.VMEM)
    return pl.pallas_call(
        functools.partial(plan_kernel, slots),
        grid_spec=pltpu.PrefetchScalarGridSpec(
            num_scalar_prefetch=1, grid=(), in_specs=[in_vmem], out_specs=in_vmem
        ),
        out_shape=jax.ShapeDtypeStruct((8, PLACES), jnp.int32),
        compiler_params=pltpu.CompilerParams(vmem_limit_bytes=16 * MIB),
        name="plan",
    )(where, masks)


def branch(which, low, high, run):
    if high - low == 1:
        run(low)
        return
    middle = (low + high) // 2

    @pl.when(which < middle)
    def _():
        branch(which, low, middle, run)

    @pl.when(which >= middle)
    def _():
        branch(which, middle, high, run)


def gather_kernel(turn, held, streams, passed, table, *refs):
    buffers, refs = refs[:held], refs[held:]
    arrived, sems = refs[:passed], refs[-1]
    outs = refs[len(refs) - 1 - len(streams) - (passed > 0):-1]
    size = outs[0].shape[0]
    for place in range(passed):
        span = pl.ds(place * size, size)
        pltpu.make_async_copy(arrived[place], outs[-1].at[span], sems.at[len(outs) - 1]).start()

    def load(stream, at, code, run):
        def copy(n):
            pltpu.make_async_copy(
                buffers[n].at[pl.ds(code & (STRIDE - 1), run)],
                outs[stream].at[pl.ds(at, run)],
                sems.at[stream],
            ).start()

        branch(lax.shift_right_logical(code, 6), 0, held, copy)

    def step(part, carry):
        at = part * RUN
        for index, stream in enumerate(streams):
            start = stream * PLACES + turn * STRIDE + at
            codes = [table[start + inner] for inner in range(RUN)]
            in_row = codes[1] - codes[0] == 1
            for inner in range(2, RUN):
                in_row = jnp.logical_and(in_row, codes[inner] - codes[inner - 1] == 1)

            @pl.when(in_row)
            def _(index=index, codes=codes):
                load(index, at, codes[0], RUN)

            @pl.when(jnp.logical_not(in_row))
            def _(index=index, start=start):
                def single(inner, carry):
                    load(index, at + inner, table[start + inner], 1)
                    return carry

                lax.fori_loop(0, RUN, single, 0)

        return carry

    lax.fori_loop(0, size // RUN, step, 0)
    for index, out in enumerate(outs):
        pltpu.make_async_copy(out, out, sems.at[index]).wait()


def gather(turn, size, table, buffers, streams, arrived, after):
    dtype = buffers[0].dtype
    shapes = [jax.ShapeDtypeStruct((size, OBLK, BLK), dtype) for _ in streams]
    if arrived:
        shapes.append(jax.ShapeDtypeStruct((size * len(arrived), OBLK, BLK), dtype))
    return pl.pallas_call(
        functools.partial(gather_kernel, turn, len(buffers), streams, len(arrived)),
        grid_spec=pltpu.PrefetchScalarGridSpec(
            num_scalar_prefetch=1,
            grid=(),
            in_specs=[pl.BlockSpec(memory_space=pl.ANY)] * (len(buffers) + len(arrived) + len(after)),
            out_specs=[pl.BlockSpec(memory_space=pltpu.VMEM)] * len(shapes),
            scratch_shapes=[pltpu.SemaphoreType.DMA((len(shapes),))],
        ),
        out_shape=shapes,
        compiler_params=pltpu.CompilerParams(
            vmem_limit_bytes=2 * sum(array.size for array in shapes) + 2 * MIB
        ),
        cost_estimate=pl.CostEstimate(
            flops=0, bytes_accessed=4 * len(streams) * size * OBLK * BLK, transcendentals=0
        ),
        name="gather",
    )(table, *buffers, *arrived, *after)


def relay_kernel(source, token, out):
    out[...] = source[...]


def relay(source, token):
    in_vmem = pl.BlockSpec(memory_space=pltpu.VMEM)
    return pl.pallas_call(
        relay_kernel,
        in_specs=[in_vmem, pl.BlockSpec(memory_space=pl.ANY)],
        out_specs=in_vmem,
        out_shape=jax.ShapeDtypeStruct(source.shape, source.dtype),
        compiler_params=pltpu.CompilerParams(vmem_limit_bytes=16 * MIB),
        name="relay",
    )(source, token)


def product_kernel(
    groups, orbitals, row_blocks, col_blocks, stages, first, extra, loc, meta, *refs
):
    flat = iter(refs)
    before = None if first else next(flat)
    sources = [
        [[(next(flat), offset) for offset in offsets] for offsets in buffers] for buffers in groups
    ]
    for _ in range(extra):
        next(flat)
    out, done, items, acc, unit, state, in_sems, acc_sems, out_sems = flat
    group_aux = [len(buffers[0]) for buffers in groups]
    row_tile, col_tile = tile_of(row_blocks), tile_of(col_blocks)
    step_tile = unit.shape[0] // BLK
    col_tiles = col_blocks // col_tile
    first_row, first_col = meta[0], meta[1]
    room = items.shape[0]
    quad = math.gcd(row_blocks, col_blocks, 4)
    if quad == 1:
        quad = math.gcd(row_blocks, col_blocks)
    blocks, first_right = row_blocks + col_blocks, row_blocks
    if row_blocks == col_blocks:
        alike = first_row == first_col
        blocks = jnp.where(alike, row_blocks, blocks)
        first_right = jnp.where(alike, 0, first_right)
    depth = sum(group_aux) * OBLK
    padded = items.shape[2]
    height, width = row_tile * BLK, col_tile * BLK
    row_tiles = row_blocks // row_tile
    met_at, columns_at = orbitals, orbitals + row_tiles

    def code_of(group, orbital, block):
        return loc[group * PLACES + orbital * NB + block]

    def any_kept(orbital, start, count):
        best = code_of(0, orbital, start)
        for step in range(1, count):
            best = jnp.maximum(best, code_of(0, orbital, start + step))
        return best >= 0

    def whole_block(block):
        return jnp.where(block < row_blocks, first_row + block, first_col + block - row_blocks)

    def span_of(tile):
        return pl.ds(pl.multiple_of(tile * height, height), height)

    def entering(tile):
        return pltpu.make_async_copy(before.at[span_of(tile)], acc.at[span_of(tile)], acc_sems.at[tile])

    def leaving(tile):
        return pltpu.make_async_copy(acc.at[span_of(tile)], out.at[span_of(tile)], out_sems.at[tile])

    def survey(orbital, count):
        stage = loc[len(groups) * PLACES + orbital]
        wanted = jnp.logical_and(stage >= stages[0], stage <= stages[1])
        state[columns_at + count] = 0

        @pl.when(wanted)
        def _():
            @pl.when(any_kept(orbital, first_row, row_blocks))
            def _():
                columns = jnp.int32(0)
                for col in range(col_tiles):
                    held = any_kept(orbital, first_col + col * col_tile, col_tile)
                    columns = columns + jnp.where(held, 1 << col, 0)
                state[columns_at + count] = columns

        wanted = state[columns_at + count] > 0

        @pl.when(wanted)
        def _():
            state[count] = orbital
            for tile in range(row_tiles):
                held = any_kept(orbital, first_row + tile * row_tile, row_tile)
                state[met_at + tile] = state[met_at + tile] + jnp.where(held, 1 << count, 0)

        return count + jnp.where(wanted, 1, 0)

    for tile in range(row_tiles):
        state[met_at + tile] = 0
    count = lax.fori_loop(0, orbitals, survey, jnp.int32(0))
    done[...] = jnp.zeros(done.shape, done.dtype)

    def fetch(begin):
        def one(slot, carry):
            orbital = state[begin + slot]

            def load(block, run):
                start_aux = 0
                for group, buffers in enumerate(sources):
                    place = code_of(group, orbital, whole_block(block))

                    def copy(n, buffers=buffers, place=place, start_aux=start_aux):
                        for aux, (buffer, offset) in enumerate(buffers[n]):
                            pltpu.make_async_copy(
                                buffer.at[pl.ds((place & (STRIDE - 1)) + offset, run)],
                                items.at[
                                    slot, pl.ds(block, run), pl.ds((start_aux + aux) * OBLK, OBLK)
                                ],
                                in_sems.at[slot],
                            ).start()

                    branch(lax.shift_right_logical(place, 6), 0, len(buffers), copy)
                    start_aux += group_aux[group]
                if padded > depth:
                    items[slot, pl.ds(block, run), depth:] = jnp.zeros(
                        (run, padded - depth, BLK), items.dtype
                    )

            def step(part, carry):
                block = part * quad
                in_row = code_of(0, orbital, whole_block(block)) >= 0
                for group in range(len(groups)):
                    low = code_of(group, orbital, whole_block(block))
                    high = code_of(group, orbital, whole_block(block) + quad - 1)
                    in_row = jnp.logical_and(in_row, high - low == quad - 1)

                @pl.when(in_row)
                def _():
                    load(block, quad)

                @pl.when(jnp.logical_not(in_row))
                def _():
                    def single(inner, carry):
                        held = code_of(0, orbital, whole_block(block + inner)) >= 0

                        @pl.when(held)
                        def _():
                            load(block + inner, 1)

                        @pl.when(jnp.logical_not(held))
                        def _():
                            items[slot, block + inner] = jnp.zeros((padded, BLK), items.dtype)

                        return carry

                    lax.fori_loop(0, quad, single, 0)

                return carry

            return lax.fori_loop(0, blocks // quad, step, carry)

        lax.fori_loop(0, jnp.minimum(count - begin, room), one, 0)

    def landed(begin):
        def one(slot, carry):
            orbital = state[begin + slot]

            def step(block, carry):
                @pl.when(code_of(0, orbital, whole_block(block)) >= 0)
                def _():
                    whole = items.at[slot, block, pl.ds(0, depth)]
                    pltpu.make_async_copy(whole, whole, in_sems.at[slot]).wait()

                return carry

            return lax.fori_loop(0, blocks, step, carry)

        lax.fori_loop(0, jnp.minimum(count - begin, room), one, 0)

    def multiply(begin, tile):
        rows = span_of(tile)

        def one(slot, carry):
            @pl.when(lax.rem(lax.shift_right_logical(state[met_at + tile], begin + slot), 2) == 1)
            def _():
                turned = []
                for start in range(0, row_tile, step_tile):
                    left = jnp.concatenate(
                        [items[slot, tile * row_tile + start + step] for step in range(step_tile)],
                        axis=1,
                    )
                    turned.append(lax.dot_general(
                        unit[...], left, (((1,), (1,)), ((), ())), preferred_element_type=jnp.float32
                    ).astype(left.dtype))
                turned = jnp.concatenate(turned, axis=0)
                columns = state[columns_at + begin + slot]

                def column(col, carry):
                    @pl.when(lax.rem(lax.shift_right_logical(columns, col), 2) == 1)
                    def _():
                        right = jnp.concatenate(
                            [items[slot, first_right + col * col_tile + step] for step in range(col_tile)],
                            axis=1,
                        )
                        span = pl.ds(pl.multiple_of(col * width, width), width)
                        acc[rows, span] += jnp.dot(turned, right, preferred_element_type=jnp.float32)

                    return carry

                lax.fori_loop(0, col_tiles, column, 0)

            return carry

        lax.fori_loop(0, jnp.minimum(count - begin, room), one, 0)

    fetch(0)
    if first:
        def clear(tile, carry):
            acc[span_of(tile)] = jnp.zeros((height, acc.shape[1]), acc.dtype)
            return carry
    else:
        def clear(tile, carry):
            @pl.when(state[met_at + tile] > 0)
            def _():
                entering(tile).start()
            return carry

    lax.fori_loop(0, row_tiles, clear, 0)
    across = lax.broadcasted_iota(jnp.int32, unit.shape, 1)
    unit[...] = as_number(lax.broadcasted_iota(jnp.int32, unit.shape, 0) == across).astype(unit.dtype)
    passes = (count + room - 1) // room
    if first:
        passes = jnp.maximum(passes, 1)

    def one_pass(turn, carry):
        begin = turn * room

        @pl.when(turn > 0)
        def _():
            fetch(begin)

        landed(begin)

        def row_step(tile, carry):
            touched = jnp.logical_or(first, state[met_at + tile] > 0)

            @pl.when(touched)
            def _():
                if not first:
                    @pl.when(turn == 0)
                    def _():
                        entering(tile).wait()
                multiply(begin, tile)

                @pl.when(turn == passes - 1)
                def _():
                    leaving(tile).start()

            return carry

        lax.fori_loop(0, row_tiles, row_step, 0)
        return carry

    lax.fori_loop(0, passes, one_pass, 0)

    def row_end(tile, carry):
        @pl.when(jnp.logical_or(first, state[met_at + tile] > 0))
        def _():
            leaving(tile).wait()

        return carry

    lax.fori_loop(0, row_tiles, row_end, 0)


def tile_of(blocks):
    return 4 if blocks % 4 == 0 else 3 if blocks % 3 == 0 else 1


def product(loc, meta, sources, held, after, stages, orbitals, row_blocks, col_blocks):
    groups = [[[offset for _, offset in refs] for refs in group] for group in sources]
    flat = [array for group in sources for refs in group for array, _ in refs]
    total_aux = sum(len(group[0]) for group in sources)
    rows, cols = row_blocks * BLK, col_blocks * BLK
    row_tile = tile_of(row_blocks)
    step_tile = 2 if row_tile % 2 == 0 else row_tile
    row_tiles = row_blocks // row_tile
    padded = -(-total_aux * OBLK // 256) * 256
    room = 2
    first = held is None
    in_hbm = pl.BlockSpec(memory_space=pltpu.HBM)
    in_any = pl.BlockSpec(memory_space=pl.ANY)
    return pl.pallas_call(
        functools.partial(
            product_kernel, groups, orbitals, row_blocks, col_blocks, stages, first, len(after)
        ),
        grid_spec=pltpu.PrefetchScalarGridSpec(
            num_scalar_prefetch=2,
            grid=(),
            in_specs=[in_hbm] * (not first)
            + [in_any] * (len(flat) + len(after)),
            out_specs=[in_hbm, pl.BlockSpec(memory_space=pltpu.VMEM)],
            scratch_shapes=[
                pltpu.VMEM((room, row_blocks + col_blocks, padded, BLK), jnp.bfloat16),
                pltpu.VMEM((rows, cols), jnp.float32),
                pltpu.VMEM((step_tile * BLK, step_tile * BLK), jnp.bfloat16),
                pltpu.SMEM((2 * orbitals + row_tiles + 1,), jnp.int32),
                pltpu.SemaphoreType.DMA((room,)),
                pltpu.SemaphoreType.DMA((row_tiles,)),
                pltpu.SemaphoreType.DMA((row_tiles,)),
            ],
        ),
        out_shape=[
            jax.ShapeDtypeStruct((rows, cols), jnp.float32),
            jax.ShapeDtypeStruct((8, 128), jnp.float32),
        ],
        input_output_aliases={} if first else {2: 0},
        compiler_params=pltpu.CompilerParams(
            vmem_limit_bytes=2 * room * padded * (rows + cols) + 4 * rows * cols + 4 * MIB
        ),
        cost_estimate=pl.CostEstimate(
            flops=2 * rows * cols * total_aux * OBLK * orbitals,
            bytes_accessed=4 * rows * cols,
            transcendentals=0,
        ),
        name="product",
    )(loc, meta, *([] if first else [held]), *flat, *after)


def rounds(size, add, table, own):
    first = [(0, 1), (1, 0), (2, 3), (3, 2)]
    second = []
    for aux in range(4):
        here, there = aux * 4, (aux ^ 1) * 4
        second += [(here, there), (here + 1, here + 2), (here + 2, here + 1), (here + 3, there + 3)]
    across = [(0, 2), (2, 0), (1, 3), (3, 1)]

    def to_core(held):
        return lax.ppermute(held, "aux", first)

    moved, crossed, passed = [], [], []
    core_own = to_core(own)
    total, done = None, []
    calls = {2: (0, 1), 3: (2, 2), 4: (3, 3), 5: (4, 4)}
    if size == LEVELS[-1]:
        calls = {ROUNDS: (0, HOPS)}
    for turn in range(ROUNDS + 1):
        chunks = []
        if turn < ROUNDS:
            streams = (0, 1, 2) if turn < HOPS else (2,)
            arrived = moved[-2:] + crossed[-1:]
            chunks = gather(turn, size, table, [own] + moved, streams, arrived, done)
        if turn > 0:
            if turn < ROUNDS:
                passed.append(to_core(chunks[-1]))
            elif done:
                passed.append(to_core(relay(crossed[-1], done[0])))
            else:
                passed.append(to_core(crossed[-1]))
        if turn in calls:
            near = [[(own, 0), (core_own, 0)]]
            for index, held in enumerate(moved):
                near.append([(held, 0), (passed[index // 2], index % 2 * size)])
            far = [
                [(held, 0), (passed[index], 2 * size if index < HOPS else 0)]
                for index, held in enumerate(crossed)
            ]
            total, token = add(
                table[3 * PLACES:6 * PLACES], [near, far], total, chunks[:1], calls[turn]
            )
            done = [token]
        if turn < HOPS:
            moved.append(lax.ppermute(chunks[0], "occ", first))
            moved.append(lax.ppermute(chunks[1], ("aux", "occ"), second))
        if turn < ROUNDS:
            crossed.append(lax.ppermute(chunks[2 if turn < HOPS else 0], "aux", across))
    return total


def on_device(shape, factors, block_mask, block_lists):
    aux_count, occ_count = shape["aux"], shape["occ"]
    own_orbitals, slots = block_lists.shape
    aux, occ = lax.axis_index("aux"), lax.axis_index("occ")
    row_blocks, col_blocks = NB // aux_count, NB // occ_count
    meta = jnp.stack([aux * row_blocks, occ * col_blocks]).astype(jnp.int32)

    def add(loc, sources, held, after, stages):
        return product(loc, meta, sources, held, after, stages, NOB, row_blocks, col_blocks)

    kept = block_mask.T > 0
    if aux_count == 4 and occ_count == 4 and shape["parts"] == 2:
        mask = as_number(kept).reshape(1, PLACES)
        other = lax.ppermute(mask, "parts", [(0, 1), (1, 0)])
        where = jnp.stack([aux, occ]).astype(jnp.int32)
        table = plan(where, jnp.concatenate([mask, other]), slots)
        own = pick(factors, block_lists)
        return lax.switch(
            table[6, 0],
            [functools.partial(rounds, size, add) for size in LEVELS],
            table.reshape(-1),
            own,
        )
    own = pick(factors, block_lists)
    everything = lax.all_gather(lax.all_gather(own, "aux"), "occ")
    sources = [[(everything[z, a], 0) for a in range(aux_count)] for z in range(occ_count)]
    earlier = jnp.arange(NB)[None, :] < jnp.arange(NB)[:, None]
    rank = jnp.sum(kept[:, None, :] & earlier[None], axis=2, dtype=jnp.int32)
    orbital = jnp.arange(NOB, dtype=jnp.int32)[:, None]
    start = orbital // own_orbitals * STRIDE + orbital % own_orbitals * slots
    loc = jnp.concatenate([
        jnp.where(kept, rank + start, -1).reshape(-1), jnp.zeros(PLACES, jnp.int32)
    ])
    return add(loc, [sources], None, [], (0, 0))[0]


def solution(mesh):
    placed = (P(("parts", "aux"), "occ", None), P("parts", None), P(("parts", "occ"), None))
    return jax.shard_map(
        functools.partial(on_device, dict(mesh.shape)),
        mesh=mesh,
        in_specs=placed,
        out_specs=P(("parts", "aux"), "occ"),
        check_vma=False,
    )
```

```python
import functools
import math

import jax
import jax.numpy as jnp
from jax import lax
from jax.experimental import pallas as pl
from jax.experimental.pallas import tpu as pltpu
from jax.sharding import PartitionSpec as P

BLK = 128
OBLK = 112
NB = 48
NOB = 8
PLACES = NOB * NB
STRIDE = 64
ROUNDS = 5
HOPS = ROUNDS - 1
LEVELS = (15, 18, 21, 48)
RUN = 3
MIB = 1024 * 1024


def pick_kernel(lists, factors, *refs):
    items = refs[-1]
    orbitals, slots = lists.shape

    def step(slot, carry):
        for orbital in range(orbitals):
            block = jnp.maximum(lists[orbital, slot], 0)
            columns = pl.ds(pl.multiple_of(block * BLK, BLK), BLK)
            rows = slice(orbital * OBLK, (orbital + 1) * OBLK)
            items[orbital * slots + slot] = factors[0, rows, columns]
        return carry

    lax.fori_loop(0, slots, step, 0)


def pick(factors, block_lists, after=()):
    orbitals, slots = block_lists.shape
    count = orbitals * slots
    return pl.pallas_call(
        pick_kernel,
        grid_spec=pltpu.PrefetchScalarGridSpec(
            num_scalar_prefetch=1,
            grid=(),
            in_specs=[pl.BlockSpec(memory_space=pltpu.VMEM)]
            + [pl.BlockSpec(memory_space=pl.ANY)] * len(after),
            out_specs=pl.BlockSpec(memory_space=pltpu.VMEM),
        ),
        out_shape=jax.ShapeDtypeStruct((count, OBLK, BLK), factors.dtype),
        compiler_params=pltpu.CompilerParams(vmem_limit_bytes=16 * MIB),
        cost_estimate=pl.CostEstimate(
            flops=0, bytes_accessed=4 * count * OBLK * BLK, transcendentals=0
        ),
        name="pick",
    )(block_lists, factors, *after)


def as_number(condition):
    return jnp.where(condition, 1.0, 0.0)


def place_facts(shape, axis):
    place = lax.broadcasted_iota(jnp.int32, shape, axis).astype(jnp.float32)
    orbital = jnp.floor((place + 0.5) / NB)
    block = place - NB * orbital
    quarter = jnp.floor((block + 0.5) / (NB // 4))
    return place, orbital, quarter, jnp.floor((quarter + 0.5) / 2), jnp.floor((orbital + 0.5) / 2)


def plan_kernel(slots, where, masks, out):
    rows = levels = 8
    wide = (rows, PLACES)
    _, orbital, quarter, half, origin = place_facts(wide, 1)
    row = lax.broadcasted_iota(jnp.int32, wide, 0)
    kept = jnp.broadcast_to(masks[...], wide)
    capacity = jnp.zeros(wide, jnp.float32)
    for index, size in enumerate(LEVELS + LEVELS[-1:] * (levels - len(LEVELS))):
        capacity = jnp.where(row == index, float(size), capacity)

    square = (PLACES, PLACES)
    down_place, down_orbital, _, _, _ = place_facts(square, 0)
    over_place, over_orbital, _, _, _ = place_facts(square, 1)
    same = as_number(down_orbital == over_orbital)
    before = as_number(down_place < over_place)
    within = (same * before).astype(jnp.bfloat16)
    same, before = same.astype(jnp.bfloat16), before.astype(jnp.bfloat16)

    def times(parts, matrix):
        stacked = jnp.concatenate(parts, axis=0).astype(jnp.bfloat16)
        product = jnp.dot(stacked, matrix, preferred_element_type=jnp.float32)
        return [product[index * rows:(index + 1) * rows] for index in range(len(parts))]

    touching = times([kept * as_number(quarter == z) for z in range(4)], same)
    need = [kept * as_number(touch > 0) for touch in touching]
    zero = jnp.zeros(wide, jnp.float32)

    def union(parts):
        best = zero
        for part in parts:
            best = jnp.maximum(best, part)
        return best

    x_need = []
    for x in range(2):
        touched = as_number(touching[2 * x] + touching[2 * x + 1] > 0)
        here = as_number(half == x)
        x_need.append([
            need[z] * jnp.maximum(here, as_number(quarter == z) * touched) for z in range(4)
        ])
    mine = [kept * as_number(origin == z) for z in range(4)]
    need_up = [union(need[z + 1:]) for z in range(4)]
    far_up = [union(need[z + 2:]) for z in range(4)]
    need_down = [union(need[:z]) for z in range(4)]
    far_down = [union(need[:max(z - 1, 0)]) for z in range(4)]
    up = [mine[z] * need_up[z] for z in range(4)]
    down = [mine[z] * need_down[z] for z in range(4)]
    cross = [[mine[z] * x_need[x][z] for z in range(4)] for x in range(2)]
    up_code, down_code = [zero] * 4, [zero] * 4
    cross_code = [[zero] * 4, [zero] * 4]

    for turn in range(ROUNDS):
        parts = []
        if turn < HOPS:
            for z in range(3):
                parts += [up[z] * far_up[z], up[z] - up[z] * far_up[z]]
                parts += [down[z + 1] * far_down[z + 1], down[z + 1] - down[z + 1] * far_down[z + 1]]
        parts += [cross[x][z] for x in range(2) for z in range(4)]
        ranks = iter(zip(parts, times(parts, before)))

        def taken(pairs):
            rank, total = zero, 0.0
            chosen = zero
            for part, counted in pairs:
                rank = rank + part * (counted + total)
                total = total + jnp.sum(part, axis=1, keepdims=True)
                chosen = chosen + part
            chosen = chosen * as_number(rank < capacity)
            return chosen, chosen * (rank + float(turn * STRIDE + 1))

        up_sent, down_sent = [], []
        if turn < HOPS:
            for z in range(3):
                sent, code = taken([next(ranks), next(ranks)])
                up_sent.append(sent)
                up_code[z] = up_code[z] + code
                up[z] = up[z] - sent
                sent, code = taken([next(ranks), next(ranks)])
                down_sent.append(sent)
                down_code[z + 1] = down_code[z + 1] + code
                down[z + 1] = down[z + 1] - sent
        for x in range(2):
            for z in range(4):
                sent, code = taken([next(ranks)])
                cross_code[x][z] = cross_code[x][z] + code
                cross[x][z] = cross[x][z] - sent
        if turn < HOPS:
            for z in range(3):
                up[z + 1] = up[z + 1] + up_sent[z] * need_up[z + 1]
                down[z] = down[z] + down_sent[z] * need_down[z]
                for x in range(2):
                    cross[x][z + 1] = cross[x][z + 1] + up_sent[z] * x_need[x][z + 1]
                    cross[x][z] = cross[x][z] + down_sent[z] * x_need[x][z]

    left = zero
    for part in up + down + cross[0] + cross[1]:
        left = left + part
    left = jnp.sum(left, axis=1, keepdims=True)
    order = lax.broadcasted_iota(jnp.int32, (levels, 1), 0).astype(jnp.float32)
    level = jnp.min(jnp.where(left > 0, float(len(LEVELS) - 1), order), axis=0, keepdims=True)
    level_row = as_number(
        lax.broadcasted_iota(jnp.int32, (levels, PLACES), 0).astype(jnp.float32) == level
    )
    me_x, me_z = where[0] // 2, where[1]
    odd = lax.rem(me_z, 2).astype(jnp.float32)

    def at(parts, z):
        total = jnp.zeros((levels, PLACES), jnp.float32)
        for index, part in enumerate(parts):
            total = total + jnp.where(z == index, 1.0, 0.0) * part[:levels]
        return jnp.sum(total * level_row, axis=0, keepdims=True)

    cross_here = [jnp.where(me_x == 0, cross_code[0][z], cross_code[1][z]) for z in range(4)]
    cross_there = [jnp.where(me_x == 0, cross_code[1][z], cross_code[0][z]) for z in range(4)]
    def turn_of(code):
        return jnp.floor((code - 0.5) / STRIDE)

    got_up, got_down = at(up_code, me_z - 1), at(down_code, me_z + 1)
    got_cross = at(cross_here, me_z)
    inner = jnp.dot(kept.astype(jnp.bfloat16), within, preferred_element_type=jnp.float32)[0:1]
    one_orbital, one_origin = orbital[0:1], origin[0:1]
    slot = inner + slots * (one_orbital - 2 * one_origin)
    owned = kept[0:1] * as_number(one_origin == me_z.astype(jnp.float32))
    held = (
        owned * (slot + 1)
        + as_number(got_up > 0) * (got_up + STRIDE * (2 - odd + turn_of(got_up)))
        + as_number(got_down > 0) * (got_down + STRIDE * (1 + odd + turn_of(got_down)))
        - 1
    )
    crossed = got_cross - 1
    near = jnp.maximum(
        as_number(quarter[0:1] == where[0].astype(jnp.float32)),
        as_number(quarter[0:1] == me_z.astype(jnp.float32)),
    )
    arrival = jnp.maximum(
        as_number(got_up + got_down > 0) * turn_of(got_up + got_down),
        as_number(got_cross > 0) * turn_of(got_cross),
    )
    lane = lax.broadcasted_iota(jnp.int32, (1, PLACES), 1)
    stage = jnp.zeros((1, PLACES), jnp.float32)
    for index in range(NOB):
        inside = as_number(one_orbital == float(index)) * near * kept[0:1]
        stage = jnp.where(
            lane == index, jnp.max(arrival * inside, axis=1, keepdims=True), stage
        )

    buffer = jnp.floor((held + 0.5) / STRIDE)
    tall = (PLACES, PLACES)
    target = lax.broadcasted_iota(jnp.int32, tall, 0).astype(jnp.float32) + 1
    blank = jnp.zeros_like(held)
    pair = jnp.concatenate([buffer, held - STRIDE * buffer, blank + 1] + [blank] * 5, axis=0)
    position = lax.broadcasted_iota(jnp.int32, (1, PLACES), 1).astype(jnp.float32)
    spare = position - STRIDE * jnp.floor((position + 0.5) / STRIDE)
    sends = []
    sent_up, sent_down = at(up_code, me_z), at(down_code, me_z)
    for sent in (
        jnp.where(odd > 0, sent_down, sent_up),
        jnp.where(odd > 0, sent_up, sent_down),
        at(cross_there, me_z),
    ):
        chosen = as_number(target == sent).astype(jnp.bfloat16)
        both = lax.dot_general(
            pair.astype(jnp.bfloat16), chosen, (((1,), (1,)), ((), ())),
            preferred_element_type=jnp.float32,
        )
        filled = both[0:1] * STRIDE + both[1:2]
        sends.append(jnp.where(both[2:3] > 0, filled, spare))
    flat = level + jnp.zeros((1, PLACES), jnp.float32)
    result = jnp.concatenate(sends + [held, crossed, stage, flat, flat], axis=0)
    out[...] = result.astype(jnp.int32)


def plan(where, masks, slots):
    in_vmem = pl.BlockSpec(memory_space=pltpu.VMEM)
    return pl.pallas_call(
        functools.partial(plan_kernel, slots),
        grid_spec=pltpu.PrefetchScalarGridSpec(
            num_scalar_prefetch=1, grid=(), in_specs=[in_vmem], out_specs=in_vmem
        ),
        out_shape=jax.ShapeDtypeStruct((8, PLACES), jnp.int32),
        compiler_params=pltpu.CompilerParams(vmem_limit_bytes=16 * MIB),
        name="plan",
    )(where, masks)


def branch(which, low, high, run):
    if high - low == 1:
        run(low)
        return
    middle = (low + high) // 2

    @pl.when(which < middle)
    def _():
        branch(which, low, middle, run)

    @pl.when(which >= middle)
    def _():
        branch(which, middle, high, run)


def gather_kernel(turn, held, streams, passed, table, *refs):
    buffers, refs = refs[:held], refs[held:]
    arrived, sems = refs[:passed], refs[-1]
    outs = refs[len(refs) - 1 - len(streams) - (passed > 0):-1]
    size = outs[0].shape[0]
    for place in range(passed):
        span = pl.ds(place * size, size)
        pltpu.make_async_copy(arrived[place], outs[-1].at[span], sems.at[len(outs) - 1]).start()

    def load(stream, at, code, run):
        def copy(n):
            pltpu.make_async_copy(
                buffers[n].at[pl.ds(code & (STRIDE - 1), run)],
                outs[stream].at[pl.ds(at, run)],
                sems.at[stream],
            ).start()

        branch(lax.shift_right_logical(code, 6), 0, held, copy)

    def step(part, carry):
        at = part * RUN
        for index, stream in enumerate(streams):
            start = stream * PLACES + turn * STRIDE + at
            codes = [table[start + inner] for inner in range(RUN)]
            in_row = codes[1] - codes[0] == 1
            for inner in range(2, RUN):
                in_row = jnp.logical_and(in_row, codes[inner] - codes[inner - 1] == 1)

            @pl.when(in_row)
            def _(index=index, codes=codes):
                load(index, at, codes[0], RUN)

            @pl.when(jnp.logical_not(in_row))
            def _(index=index, start=start):
                def single(inner, carry):
                    load(index, at + inner, table[start + inner], 1)
                    return carry

                lax.fori_loop(0, RUN, single, 0)

        return carry

    lax.fori_loop(0, size // RUN, step, 0)
    for index, out in enumerate(outs):
        pltpu.make_async_copy(out, out, sems.at[index]).wait()


def gather(turn, size, table, buffers, streams, arrived, after):
    dtype = buffers[0].dtype
    shapes = [jax.ShapeDtypeStruct((size, OBLK, BLK), dtype) for _ in streams]
    if arrived:
        shapes.append(jax.ShapeDtypeStruct((size * len(arrived), OBLK, BLK), dtype))
    return pl.pallas_call(
        functools.partial(gather_kernel, turn, len(buffers), streams, len(arrived)),
        grid_spec=pltpu.PrefetchScalarGridSpec(
            num_scalar_prefetch=1,
            grid=(),
            in_specs=[pl.BlockSpec(memory_space=pl.ANY)] * (len(buffers) + len(arrived) + len(after)),
            out_specs=[pl.BlockSpec(memory_space=pltpu.VMEM)] * len(shapes),
            scratch_shapes=[pltpu.SemaphoreType.DMA((len(shapes),))],
        ),
        out_shape=shapes,
        compiler_params=pltpu.CompilerParams(
            vmem_limit_bytes=2 * sum(array.size for array in shapes) + 2 * MIB
        ),
        cost_estimate=pl.CostEstimate(
            flops=0, bytes_accessed=4 * len(streams) * size * OBLK * BLK, transcendentals=0
        ),
        name="gather",
    )(table, *buffers, *arrived, *after)


def relay_kernel(source, token, out):
    out[...] = source[...]


def relay(source, token):
    in_vmem = pl.BlockSpec(memory_space=pltpu.VMEM)
    return pl.pallas_call(
        relay_kernel,
        in_specs=[in_vmem, pl.BlockSpec(memory_space=pl.ANY)],
        out_specs=in_vmem,
        out_shape=jax.ShapeDtypeStruct(source.shape, source.dtype),
        compiler_params=pltpu.CompilerParams(vmem_limit_bytes=16 * MIB),
        name="relay",
    )(source, token)


def product_kernel(
    groups, orbitals, row_blocks, col_blocks, stages, first, extra, loc, meta, *refs
):
    flat = iter(refs)
    before = None if first else next(flat)
    sources = [
        [[(next(flat), offset) for offset in offsets] for offsets in buffers] for buffers in groups
    ]
    for _ in range(extra):
        next(flat)
    out, done, items, acc, unit, state, in_sems, acc_sems, out_sems = flat
    group_aux = [len(buffers[0]) for buffers in groups]
    row_tile, col_tile = tile_of(row_blocks), tile_of(col_blocks)
    step_tile = unit.shape[0] // BLK
    col_tiles = col_blocks // col_tile
    first_row, first_col = meta[0], meta[1]
    room = items.shape[0]
    quad = math.gcd(row_blocks, col_blocks, 4)
    if quad == 1:
        quad = math.gcd(row_blocks, col_blocks)
    blocks, first_right = row_blocks + col_blocks, row_blocks
    if row_blocks == col_blocks:
        alike = first_row == first_col
        blocks = jnp.where(alike, row_blocks, blocks)
        first_right = jnp.where(alike, 0, first_right)
    depth = sum(group_aux) * OBLK
    padded = items.shape[2]
    height, width = row_tile * BLK, col_tile * BLK
    row_tiles = row_blocks // row_tile
    met_at, columns_at = orbitals, orbitals + row_tiles

    def code_of(group, orbital, block):
        return loc[group * PLACES + orbital * NB + block]

    def any_kept(orbital, start, count):
        best = code_of(0, orbital, start)
        for step in range(1, count):
            best = jnp.maximum(best, code_of(0, orbital, start + step))
        return best >= 0

    def whole_block(block):
        return jnp.where(block < row_blocks, first_row + block, first_col + block - row_blocks)

    def span_of(tile):
        return pl.ds(pl.multiple_of(tile * height, height), height)

    def entering(tile):
        return pltpu.make_async_copy(before.at[span_of(tile)], acc.at[span_of(tile)], acc_sems.at[tile])

    def leaving(tile):
        return pltpu.make_async_copy(acc.at[span_of(tile)], out.at[span_of(tile)], out_sems.at[tile])

    def survey(orbital, count):
        stage = loc[len(groups) * PLACES + orbital]
        wanted = jnp.logical_and(stage >= stages[0], stage <= stages[1])
        state[columns_at + count] = 0

        @pl.when(wanted)
        def _():
            @pl.when(any_kept(orbital, first_row, row_blocks))
            def _():
                columns = jnp.int32(0)
                for col in range(col_tiles):
                    held = any_kept(orbital, first_col + col * col_tile, col_tile)
                    columns = columns + jnp.where(held, 1 << col, 0)
                state[columns_at + count] = columns

        wanted = state[columns_at + count] > 0

        @pl.when(wanted)
        def _():
            state[count] = orbital
            for tile in range(row_tiles):
                held = any_kept(orbital, first_row + tile * row_tile, row_tile)
                state[met_at + tile] = state[met_at + tile] + jnp.where(held, 1 << count, 0)

        return count + jnp.where(wanted, 1, 0)

    for tile in range(row_tiles):
        state[met_at + tile] = 0
    count = lax.fori_loop(0, orbitals, survey, jnp.int32(0))
    done[...] = jnp.zeros(done.shape, done.dtype)

    def fetch(begin):
        def one(slot, carry):
            orbital = state[begin + slot]

            def load(block, run):
                start_aux = 0
                for group, buffers in enumerate(sources):
                    place = code_of(group, orbital, whole_block(block))

                    def copy(n, buffers=buffers, place=place, start_aux=start_aux):
                        for aux, (buffer, offset) in enumerate(buffers[n]):
                            pltpu.make_async_copy(
                                buffer.at[pl.ds((place & (STRIDE - 1)) + offset, run)],
                                items.at[
                                    slot, pl.ds(block, run), pl.ds((start_aux + aux) * OBLK, OBLK)
                                ],
                                in_sems.at[slot],
                            ).start()

                    branch(lax.shift_right_logical(place, 6), 0, len(buffers), copy)
                    start_aux += group_aux[group]
                if padded > depth:
                    items[slot, pl.ds(block, run), depth:] = jnp.zeros(
                        (run, padded - depth, BLK), items.dtype
                    )

            def step(part, carry):
                block = part * quad
                in_row = code_of(0, orbital, whole_block(block)) >= 0
                for group in range(len(groups)):
                    low = code_of(group, orbital, whole_block(block))
                    high = code_of(group, orbital, whole_block(block) + quad - 1)
                    in_row = jnp.logical_and(in_row, high - low == quad - 1)

                @pl.when(in_row)
                def _():
                    load(block, quad)

                @pl.when(jnp.logical_not(in_row))
                def _():
                    def single(inner, carry):
                        held = code_of(0, orbital, whole_block(block + inner)) >= 0

                        @pl.when(held)
                        def _():
                            load(block + inner, 1)

                        @pl.when(jnp.logical_not(held))
                        def _():
                            items[slot, block + inner] = jnp.zeros((padded, BLK), items.dtype)

                        return carry

                    lax.fori_loop(0, quad, single, 0)

                return carry

            return lax.fori_loop(0, blocks // quad, step, carry)

        lax.fori_loop(0, jnp.minimum(count - begin, room), one, 0)

    def landed(begin):
        def one(slot, carry):
            orbital = state[begin + slot]

            def step(block, carry):
                @pl.when(code_of(0, orbital, whole_block(block)) >= 0)
                def _():
                    whole = items.at[slot, block, pl.ds(0, depth)]
                    pltpu.make_async_copy(whole, whole, in_sems.at[slot]).wait()

                return carry

            return lax.fori_loop(0, blocks, step, carry)

        lax.fori_loop(0, jnp.minimum(count - begin, room), one, 0)

    def multiply(begin, tile):
        rows = span_of(tile)

        def one(slot, carry):
            @pl.when(lax.rem(lax.shift_right_logical(state[met_at + tile], begin + slot), 2) == 1)
            def _():
                turned = []
                for start in range(0, row_tile, step_tile):
                    left = jnp.concatenate(
                        [items[slot, tile * row_tile + start + step] for step in range(step_tile)],
                        axis=1,
                    )
                    turned.append(lax.dot_general(
                        unit[...], left, (((1,), (1,)), ((), ())), preferred_element_type=jnp.float32
                    ).astype(left.dtype))
                turned = jnp.concatenate(turned, axis=0)
                columns = state[columns_at + begin + slot]

                def column(col, carry):
                    @pl.when(lax.rem(lax.shift_right_logical(columns, col), 2) == 1)
                    def _():
                        right = jnp.concatenate(
                            [items[slot, first_right + col * col_tile + step] for step in range(col_tile)],
                            axis=1,
                        )
                        span = pl.ds(pl.multiple_of(col * width, width), width)
                        acc[rows, span] += jnp.dot(turned, right, preferred_element_type=jnp.float32)

                    return carry

                lax.fori_loop(0, col_tiles, column, 0)

            return carry

        lax.fori_loop(0, jnp.minimum(count - begin, room), one, 0)

    fetch(0)
    if first:
        def clear(tile, carry):
            acc[span_of(tile)] = jnp.zeros((height, acc.shape[1]), acc.dtype)
            return carry
    else:
        def clear(tile, carry):
            @pl.when(state[met_at + tile] > 0)
            def _():
                entering(tile).start()
            return carry

    lax.fori_loop(0, row_tiles, clear, 0)
    across = lax.broadcasted_iota(jnp.int32, unit.shape, 1)
    unit[...] = as_number(lax.broadcasted_iota(jnp.int32, unit.shape, 0) == across).astype(unit.dtype)
    passes = (count + room - 1) // room
    if first:
        passes = jnp.maximum(passes, 1)

    def one_pass(turn, carry):
        begin = turn * room

        @pl.when(turn > 0)
        def _():
            fetch(begin)

        landed(begin)

        def row_step(tile, carry):
            touched = jnp.logical_or(first, state[met_at + tile] > 0)

            @pl.when(touched)
            def _():
                if not first:
                    @pl.when(turn == 0)
                    def _():
                        entering(tile).wait()
                multiply(begin, tile)

                @pl.when(turn == passes - 1)
                def _():
                    leaving(tile).start()

            return carry

        lax.fori_loop(0, row_tiles, row_step, 0)
        return carry

    lax.fori_loop(0, passes, one_pass, 0)

    def row_end(tile, carry):
        @pl.when(jnp.logical_or(first, state[met_at + tile] > 0))
        def _():
            leaving(tile).wait()

        return carry

    lax.fori_loop(0, row_tiles, row_end, 0)


def tile_of(blocks):
    return 4 if blocks % 4 == 0 else 3 if blocks % 3 == 0 else 1


def product(loc, meta, sources, held, after, stages, orbitals, row_blocks, col_blocks):
    groups = [[[offset for _, offset in refs] for refs in group] for group in sources]
    flat = [array for group in sources for refs in group for array, _ in refs]
    total_aux = sum(len(group[0]) for group in sources)
    rows, cols = row_blocks * BLK, col_blocks * BLK
    row_tile = tile_of(row_blocks)
    step_tile = 2 if row_tile % 2 == 0 else row_tile
    row_tiles = row_blocks // row_tile
    padded = -(-total_aux * OBLK // 256) * 256
    room = 2
    first = held is None
    in_hbm = pl.BlockSpec(memory_space=pltpu.HBM)
    in_any = pl.BlockSpec(memory_space=pl.ANY)
    return pl.pallas_call(
        functools.partial(
            product_kernel, groups, orbitals, row_blocks, col_blocks, stages, first, len(after)
        ),
        grid_spec=pltpu.PrefetchScalarGridSpec(
            num_scalar_prefetch=2,
            grid=(),
            in_specs=[in_hbm] * (not first)
            + [in_any] * (len(flat) + len(after)),
            out_specs=[in_hbm, pl.BlockSpec(memory_space=pltpu.VMEM)],
            scratch_shapes=[
                pltpu.VMEM((room, row_blocks + col_blocks, padded, BLK), jnp.bfloat16),
                pltpu.VMEM((rows, cols), jnp.float32),
                pltpu.VMEM((step_tile * BLK, step_tile * BLK), jnp.bfloat16),
                pltpu.SMEM((2 * orbitals + row_tiles + 1,), jnp.int32),
                pltpu.SemaphoreType.DMA((room,)),
                pltpu.SemaphoreType.DMA((row_tiles,)),
                pltpu.SemaphoreType.DMA((row_tiles,)),
            ],
        ),
        out_shape=[
            jax.ShapeDtypeStruct((rows, cols), jnp.float32),
            jax.ShapeDtypeStruct((8, 128), jnp.float32),
        ],
        input_output_aliases={} if first else {2: 0},
        compiler_params=pltpu.CompilerParams(
            vmem_limit_bytes=2 * room * padded * (rows + cols) + 4 * rows * cols + 4 * MIB
        ),
        cost_estimate=pl.CostEstimate(
            flops=2 * rows * cols * total_aux * OBLK * orbitals,
            bytes_accessed=4 * rows * cols,
            transcendentals=0,
        ),
        name="product",
    )(loc, meta, *([] if first else [held]), *flat, *after)


def rounds(size, add, table, own):
    first = [(0, 1), (1, 0), (2, 3), (3, 2)]
    second = []
    for aux in range(4):
        here, there = aux * 4, (aux ^ 1) * 4
        second += [(here, there), (here + 1, here + 2), (here + 2, here + 1), (here + 3, there + 3)]
    across = [(0, 2), (2, 0), (1, 3), (3, 1)]

    def to_core(held):
        return lax.ppermute(held, "aux", first)

    moved, crossed, passed = [], [], []
    core_own = to_core(own)
    total, done = None, []
    calls = {2: (0, 1), 3: (2, 2), 4: (3, 3), 5: (4, 4)}
    if size == LEVELS[-1]:
        calls = {ROUNDS: (0, HOPS)}
    for turn in range(ROUNDS + 1):
        chunks = []
        if turn < ROUNDS:
            streams = (0, 1, 2) if turn < HOPS else (2,)
            arrived = moved[-2:] + crossed[-1:]
            chunks = gather(turn, size, table, [own] + moved, streams, arrived, done)
        if turn > 0:
            if turn < ROUNDS:
                passed.append(to_core(chunks[-1]))
            elif done:
                passed.append(to_core(relay(crossed[-1], done[0])))
            else:
                passed.append(to_core(crossed[-1]))
        if turn in calls:
            near = [[(own, 0), (core_own, 0)]]
            for index, held in enumerate(moved):
                near.append([(held, 0), (passed[index // 2], index % 2 * size)])
            far = [
                [(held, 0), (passed[index], 2 * size if index < HOPS else 0)]
                for index, held in enumerate(crossed)
            ]
            total, token = add(
                table[3 * PLACES:6 * PLACES], [near, far], total, chunks[:1], calls[turn]
            )
            done = [token]
        if turn < HOPS:
            moved.append(lax.ppermute(chunks[0], "occ", first))
            moved.append(lax.ppermute(chunks[1], ("aux", "occ"), second))
        if turn < ROUNDS:
            crossed.append(lax.ppermute(chunks[2 if turn < HOPS else 0], "aux", across))
    return total


def on_device(shape, factors, block_mask, block_lists):
    aux_count, occ_count = shape["aux"], shape["occ"]
    own_orbitals, slots = block_lists.shape
    aux, occ = lax.axis_index("aux"), lax.axis_index("occ")
    row_blocks, col_blocks = NB // aux_count, NB // occ_count
    meta = jnp.stack([aux * row_blocks, occ * col_blocks]).astype(jnp.int32)

    def add(loc, sources, held, after, stages):
        return product(loc, meta, sources, held, after, stages, NOB, row_blocks, col_blocks)

    kept = block_mask.T > 0
    if aux_count == 4 and occ_count == 4:
        mask = as_number(kept).reshape(1, PLACES)
        where = jnp.stack([aux, occ]).astype(jnp.int32)
        table = plan(where, mask, slots)
        own = pick(factors, block_lists)
        return lax.switch(
            table[6, 0],
            [functools.partial(rounds, size, add) for size in LEVELS],
            table.reshape(-1),
            own,
        )
    own = pick(factors, block_lists)
    everything = lax.all_gather(lax.all_gather(own, "aux"), "occ")
    sources = [[(everything[z, a], 0) for a in range(aux_count)] for z in range(occ_count)]
    earlier = jnp.arange(NB)[None, :] < jnp.arange(NB)[:, None]
    rank = jnp.sum(kept[:, None, :] & earlier[None], axis=2, dtype=jnp.int32)
    orbital = jnp.arange(NOB, dtype=jnp.int32)[:, None]
    start = orbital // own_orbitals * STRIDE + orbital % own_orbitals * slots
    loc = jnp.concatenate([
        jnp.where(kept, rank + start, -1).reshape(-1), jnp.zeros(PLACES, jnp.int32)
    ])
    return add(loc, [sources], None, [], (0, 0))[0]


def solution(mesh):
    placed = (P(("parts", "aux"), "occ", None), P("parts", None), P(("parts", "occ"), None))
    return jax.shard_map(
        functools.partial(on_device, dict(mesh.shape)),
        mesh=mesh,
        in_specs=placed,
        out_specs=P(("parts", "aux"), "occ"),
        check_vma=False,
    )
```

```python
import functools
import math

import jax
import jax.numpy as jnp
from jax import lax
from jax.experimental import pallas as pl
from jax.experimental.pallas import tpu as pltpu
from jax.sharding import PartitionSpec as P

BLK = 128
OBLK = 112
NB = 48
NOB = 8
PLACES = NOB * NB
STRIDE = 64
ROUNDS = 5
HOPS = ROUNDS - 1
LEVELS = (15, 18, 21, 48)
RUN = 3
MIB = 1024 * 1024


def pick_kernel(lists, factors, *refs):
    items = refs[-1]
    orbitals, slots = lists.shape

    def step(slot, carry):
        for orbital in range(orbitals):
            block = jnp.maximum(lists[orbital, slot], 0)
            columns = pl.ds(pl.multiple_of(block * BLK, BLK), BLK)
            rows = slice(orbital * OBLK, (orbital + 1) * OBLK)
            items[orbital * slots + slot] = factors[0, rows, columns]
        return carry

    lax.fori_loop(0, slots, step, 0)


def pick(factors, block_lists, after=()):
    orbitals, slots = block_lists.shape
    count = orbitals * slots
    return pl.pallas_call(
        pick_kernel,
        grid_spec=pltpu.PrefetchScalarGridSpec(
            num_scalar_prefetch=1,
            grid=(),
            in_specs=[pl.BlockSpec(memory_space=pltpu.VMEM)]
            + [pl.BlockSpec(memory_space=pl.ANY)] * len(after),
            out_specs=pl.BlockSpec(memory_space=pltpu.VMEM),
        ),
        out_shape=jax.ShapeDtypeStruct((count, OBLK, BLK), factors.dtype),
        compiler_params=pltpu.CompilerParams(vmem_limit_bytes=16 * MIB),
        cost_estimate=pl.CostEstimate(
            flops=0, bytes_accessed=4 * count * OBLK * BLK, transcendentals=0
        ),
        name="pick",
    )(block_lists, factors, *after)


def as_number(condition):
    return jnp.where(condition, 1.0, 0.0)


def place_facts(shape, axis):
    place = lax.broadcasted_iota(jnp.int32, shape, axis).astype(jnp.float32)
    orbital = jnp.floor((place + 0.5) / NB)
    block = place - NB * orbital
    quarter = jnp.floor((block + 0.5) / (NB // 4))
    return place, orbital, quarter, jnp.floor((quarter + 0.5) / 2), jnp.floor((orbital + 0.5) / 2)


def plan_kernel(slots, where, masks, out):
    rows = levels = 8
    wide = (rows, PLACES)
    _, orbital, quarter, half, origin = place_facts(wide, 1)
    row = lax.broadcasted_iota(jnp.int32, wide, 0)
    kept = jnp.broadcast_to(masks[...], wide)
    capacity = jnp.zeros(wide, jnp.float32)
    for index, size in enumerate(LEVELS + LEVELS[-1:] * (levels - len(LEVELS))):
        capacity = jnp.where(row == index, float(size), capacity)

    square = (PLACES, PLACES)
    down_place, down_orbital, _, _, _ = place_facts(square, 0)
    over_place, over_orbital, _, _, _ = place_facts(square, 1)
    same = as_number(down_orbital == over_orbital)
    before = as_number(down_place < over_place)
    within = (same * before).astype(jnp.bfloat16)
    same, before = same.astype(jnp.bfloat16), before.astype(jnp.bfloat16)

    def times(parts, matrix):
        stacked = jnp.concatenate(parts, axis=0).astype(jnp.bfloat16)
        product = jnp.dot(stacked, matrix, preferred_element_type=jnp.float32)
        return [product[index * rows:(index + 1) * rows] for index in range(len(parts))]

    touching = times([kept * as_number(quarter == z) for z in range(4)], same)
    need = [kept * as_number(touch > 0) for touch in touching]
    zero = jnp.zeros(wide, jnp.float32)

    def union(parts):
        best = zero
        for part in parts:
            best = jnp.maximum(best, part)
        return best

    x_need = []
    for x in range(2):
        touched = as_number(touching[2 * x] + touching[2 * x + 1] > 0)
        here = as_number(half == x)
        x_need.append([
            need[z] * jnp.maximum(here, as_number(quarter == z) * touched) for z in range(4)
        ])
    mine = [kept * as_number(origin == z) for z in range(4)]
    need_up = [union(need[z + 1:]) for z in range(4)]
    far_up = [union(need[z + 2:]) for z in range(4)]
    need_down = [union(need[:z]) for z in range(4)]
    far_down = [union(need[:max(z - 1, 0)]) for z in range(4)]
    up = [mine[z] * need_up[z] for z in range(4)]
    down = [mine[z] * need_down[z] for z in range(4)]
    cross = [[mine[z] * x_need[x][z] for z in range(4)] for x in range(2)]
    up_code, down_code = [zero] * 4, [zero] * 4
    cross_code = [[zero] * 4, [zero] * 4]

    for turn in range(ROUNDS):
        parts = []
        if turn < HOPS:
            for z in range(3):
                parts += [up[z] * far_up[z], up[z] - up[z] * far_up[z]]
                parts += [down[z + 1] * far_down[z + 1], down[z + 1] - down[z + 1] * far_down[z + 1]]
        parts += [cross[x][z] for x in range(2) for z in range(4)]
        ranks = iter(zip(parts, times(parts, before)))

        def taken(pairs):
            rank, total = zero, 0.0
            chosen = zero
            for part, counted in pairs:
                rank = rank + part * (counted + total)
                total = total + jnp.sum(part, axis=1, keepdims=True)
                chosen = chosen + part
            chosen = chosen * as_number(rank < capacity)
            return chosen, chosen * (rank + float(turn * STRIDE + 1))

        up_sent, down_sent = [], []
        if turn < HOPS:
            for z in range(3):
                sent, code = taken([next(ranks), next(ranks)])
                up_sent.append(sent)
                up_code[z] = up_code[z] + code
                up[z] = up[z] - sent
                sent, code = taken([next(ranks), next(ranks)])
                down_sent.append(sent)
                down_code[z + 1] = down_code[z + 1] + code
                down[z + 1] = down[z + 1] - sent
        for x in range(2):
            for z in range(4):
                sent, code = taken([next(ranks)])
                cross_code[x][z] = cross_code[x][z] + code
                cross[x][z] = cross[x][z] - sent
        if turn < HOPS:
            for z in range(3):
                up[z + 1] = up[z + 1] + up_sent[z] * need_up[z + 1]
                down[z] = down[z] + down_sent[z] * need_down[z]
                for x in range(2):
                    cross[x][z + 1] = cross[x][z + 1] + up_sent[z] * x_need[x][z + 1]
                    cross[x][z] = cross[x][z] + down_sent[z] * x_need[x][z]

    left = zero
    for part in up + down + cross[0] + cross[1]:
        left = left + part
    left = jnp.sum(left, axis=1, keepdims=True)
    order = lax.broadcasted_iota(jnp.int32, (levels, 1), 0).astype(jnp.float32)
    level = jnp.min(jnp.where(left > 0, float(len(LEVELS) - 1), order), axis=0, keepdims=True)
    level_row = as_number(
        lax.broadcasted_iota(jnp.int32, (levels, PLACES), 0).astype(jnp.float32) == level
    )
    me_x, me_z = where[0] // 2, where[1]
    odd = lax.rem(me_z, 2).astype(jnp.float32)

    def at(parts, z):
        total = jnp.zeros((levels, PLACES), jnp.float32)
        for index, part in enumerate(parts):
            total = total + jnp.where(z == index, 1.0, 0.0) * part[:levels]
        return jnp.sum(total * level_row, axis=0, keepdims=True)

    cross_here = [jnp.where(me_x == 0, cross_code[0][z], cross_code[1][z]) for z in range(4)]
    cross_there = [jnp.where(me_x == 0, cross_code[1][z], cross_code[0][z]) for z in range(4)]
    def turn_of(code):
        return jnp.floor((code - 0.5) / STRIDE)

    got_up, got_down = at(up_code, me_z - 1), at(down_code, me_z + 1)
    got_cross = at(cross_here, me_z)
    inner = jnp.dot(kept.astype(jnp.bfloat16), within, preferred_element_type=jnp.float32)[0:1]
    one_orbital, one_origin = orbital[0:1], origin[0:1]
    slot = inner + slots * (one_orbital - 2 * one_origin)
    owned = kept[0:1] * as_number(one_origin == me_z.astype(jnp.float32))
    held = (
        owned * (slot + 1)
        + as_number(got_up > 0) * (got_up + STRIDE * (2 - odd + turn_of(got_up)))
        + as_number(got_down > 0) * (got_down + STRIDE * (1 + odd + turn_of(got_down)))
        - 1
    )
    crossed = got_cross - 1
    near = jnp.maximum(
        as_number(quarter[0:1] == where[0].astype(jnp.float32)),
        as_number(quarter[0:1] == me_z.astype(jnp.float32)),
    )
    arrival = jnp.maximum(
        as_number(got_up + got_down > 0) * turn_of(got_up + got_down),
        as_number(got_cross > 0) * turn_of(got_cross),
    )
    lane = lax.broadcasted_iota(jnp.int32, (1, PLACES), 1)
    stage = jnp.zeros((1, PLACES), jnp.float32)
    for index in range(NOB):
        inside = as_number(one_orbital == float(index)) * near * kept[0:1]
        stage = jnp.where(
            lane == index, jnp.max(arrival * inside, axis=1, keepdims=True), stage
        )

    buffer = jnp.floor((held + 0.5) / STRIDE)
    tall = (PLACES, PLACES)
    target = lax.broadcasted_iota(jnp.int32, tall, 0).astype(jnp.float32) + 1
    blank = jnp.zeros_like(held)
    pair = jnp.concatenate([buffer, held - STRIDE * buffer, blank + 1] + [blank] * 5, axis=0)
    position = lax.broadcasted_iota(jnp.int32, (1, PLACES), 1).astype(jnp.float32)
    spare = position - STRIDE * jnp.floor((position + 0.5) / STRIDE)
    sends = []
    sent_up, sent_down = at(up_code, me_z), at(down_code, me_z)
    for sent in (
        jnp.where(odd > 0, sent_down, sent_up),
        jnp.where(odd > 0, sent_up, sent_down),
        at(cross_there, me_z),
    ):
        chosen = as_number(target == sent).astype(jnp.bfloat16)
        both = lax.dot_general(
            pair.astype(jnp.bfloat16), chosen, (((1,), (1,)), ((), ())),
            preferred_element_type=jnp.float32,
        )
        filled = both[0:1] * STRIDE + both[1:2]
        sends.append(jnp.where(both[2:3] > 0, filled, spare))
    flat = level + jnp.zeros((1, PLACES), jnp.float32)
    result = jnp.concatenate(sends + [held, crossed, stage, flat, flat], axis=0)
    out[...] = result.astype(jnp.int32)


def plan(where, masks, slots):
    in_vmem = pl.BlockSpec(memory_space=pltpu.VMEM)
    return pl.pallas_call(
        functools.partial(plan_kernel, slots),
        grid_spec=pltpu.PrefetchScalarGridSpec(
            num_scalar_prefetch=1, grid=(), in_specs=[in_vmem], out_specs=in_vmem
        ),
        out_shape=jax.ShapeDtypeStruct((8, PLACES), jnp.int32),
        compiler_params=pltpu.CompilerParams(vmem_limit_bytes=16 * MIB),
        name="plan",
    )(where, masks)


def branch(which, low, high, run):
    if high - low == 1:
        run(low)
        return
    middle = (low + high) // 2

    @pl.when(which < middle)
    def _():
        branch(which, low, middle, run)

    @pl.when(which >= middle)
    def _():
        branch(which, middle, high, run)


def gather_kernel(turn, held, streams, passed, table, *refs):
    buffers, sem = refs[:held], refs[-1]
    outs = refs[len(refs) - 1 - len(streams) - (passed > 0):-1]
    size = outs[0].shape[0]
    for place in range(passed):
        span = pl.ds(place * size, size)
        pltpu.make_async_copy(buffers[held - passed + place], outs[-1].at[span], sem).start()

    def load(stream, at, code, run):
        def copy(n):
            outs[stream][pl.ds(at, run)] = buffers[n][pl.ds(code & (STRIDE - 1), run)]

        branch(lax.shift_right_logical(code, 6), 0, held, copy)

    def step(part, carry):
        at = part * RUN
        for index, stream in enumerate(streams):
            start = stream * PLACES + turn * STRIDE + at
            codes = [table[start + inner] for inner in range(RUN)]
            in_row = codes[1] - codes[0] == 1
            for inner in range(2, RUN):
                in_row = jnp.logical_and(in_row, codes[inner] - codes[inner - 1] == 1)

            @pl.when(in_row)
            def _(index=index, codes=codes):
                load(index, at, codes[0], RUN)

            @pl.when(jnp.logical_not(in_row))
            def _(index=index, start=start):
                def single(inner, carry):
                    load(index, at + inner, table[start + inner], 1)
                    return carry

                lax.fori_loop(0, RUN, single, 0)

        return carry

    lax.fori_loop(0, size // RUN, step, 0)
    if passed:
        pltpu.make_async_copy(outs[-1], outs[-1], sem).wait()


def gather(turn, size, table, buffers, streams, passed, after):
    dtype = buffers[0].dtype
    shapes = [jax.ShapeDtypeStruct((size, OBLK, BLK), dtype) for _ in streams]
    if passed:
        shapes.append(jax.ShapeDtypeStruct((size * passed, OBLK, BLK), dtype))
    in_vmem = pl.BlockSpec(memory_space=pltpu.VMEM)
    return pl.pallas_call(
        functools.partial(gather_kernel, turn, len(buffers), streams, passed),
        grid_spec=pltpu.PrefetchScalarGridSpec(
            num_scalar_prefetch=1,
            grid=(),
            in_specs=[in_vmem] * len(buffers) + [pl.BlockSpec(memory_space=pl.ANY)] * len(after),
            out_specs=[in_vmem] * len(shapes),
            scratch_shapes=[pltpu.SemaphoreType.DMA(())],
        ),
        out_shape=shapes,
        compiler_params=pltpu.CompilerParams(
            vmem_limit_bytes=2 * sum(array.size for array in [*buffers, *shapes]) + 3 * MIB
        ),
        cost_estimate=pl.CostEstimate(
            flops=0, bytes_accessed=4 * len(streams) * size * OBLK * BLK, transcendentals=0
        ),
        name="gather",
    )(table, *buffers, *after)


def relay_kernel(source, token, out):
    pass


def relay(source, token):
    in_any = pl.BlockSpec(memory_space=pl.ANY)
    return pl.pallas_call(
        relay_kernel,
        in_specs=[in_any, in_any],
        out_specs=in_any,
        out_shape=jax.ShapeDtypeStruct(source.shape, source.dtype),
        input_output_aliases={0: 0},
        compiler_params=pltpu.CompilerParams(vmem_limit_bytes=2 * MIB),
        name="relay",
    )(source, token)


def product_kernel(
    groups, orbitals, row_blocks, col_blocks, stages, first, extra, loc, meta, *refs
):
    flat = iter(refs)
    before = None if first else next(flat)
    sources = [
        [[(next(flat), offset) for offset in offsets] for offsets in buffers] for buffers in groups
    ]
    for _ in range(extra):
        next(flat)
    out, done, items, acc, unit, state, in_sems, acc_sems, out_sems = flat
    group_aux = [len(buffers[0]) for buffers in groups]
    row_tile, col_tile = tile_of(row_blocks), tile_of(col_blocks)
    step_tile = unit.shape[0] // BLK
    col_tiles = col_blocks // col_tile
    first_row, first_col = meta[0], meta[1]
    room = items.shape[0]
    quad = math.gcd(row_blocks, col_blocks, 4)
    if quad == 1:
        quad = math.gcd(row_blocks, col_blocks)
    blocks, first_right = row_blocks + col_blocks, row_blocks
    if row_blocks == col_blocks:
        alike = first_row == first_col
        blocks = jnp.where(alike, row_blocks, blocks)
        first_right = jnp.where(alike, 0, first_right)
    depth = sum(group_aux) * OBLK
    padded = items.shape[2]
    height, width = row_tile * BLK, col_tile * BLK
    row_tiles = row_blocks // row_tile
    met_at, columns_at = orbitals, orbitals + row_tiles

    def code_of(group, orbital, block):
        return loc[group * PLACES + orbital * NB + block]

    def any_kept(orbital, start, count):
        best = code_of(0, orbital, start)
        for step in range(1, count):
            best = jnp.maximum(best, code_of(0, orbital, start + step))
        return best >= 0

    def whole_block(block):
        return jnp.where(block < row_blocks, first_row + block, first_col + block - row_blocks)

    def span_of(tile):
        return pl.ds(pl.multiple_of(tile * height, height), height)

    def entering(tile):
        return pltpu.make_async_copy(before.at[span_of(tile)], acc.at[span_of(tile)], acc_sems.at[tile])

    def leaving(tile):
        return pltpu.make_async_copy(acc.at[span_of(tile)], out.at[span_of(tile)], out_sems.at[tile])

    def survey(orbital, count):
        stage = loc[len(groups) * PLACES + orbital]
        wanted = jnp.logical_and(stage >= stages[0], stage <= stages[1])
        state[columns_at + count] = 0

        @pl.when(wanted)
        def _():
            @pl.when(any_kept(orbital, first_row, row_blocks))
            def _():
                columns = jnp.int32(0)
                for col in range(col_tiles):
                    held = any_kept(orbital, first_col + col * col_tile, col_tile)
                    columns = columns + jnp.where(held, 1 << col, 0)
                state[columns_at + count] = columns

        wanted = state[columns_at + count] > 0

        @pl.when(wanted)
        def _():
            state[count] = orbital
            for tile in range(row_tiles):
                held = any_kept(orbital, first_row + tile * row_tile, row_tile)
                state[met_at + tile] = state[met_at + tile] + jnp.where(held, 1 << count, 0)

        return count + jnp.where(wanted, 1, 0)

    for tile in range(row_tiles):
        state[met_at + tile] = 0
    count = lax.fori_loop(0, orbitals, survey, jnp.int32(0))
    done[...] = jnp.zeros(done.shape, done.dtype)

    def fetch(begin):
        def one(slot, carry):
            orbital = state[begin + slot]

            def load(block, run):
                start_aux = 0
                for group, buffers in enumerate(sources):
                    place = code_of(group, orbital, whole_block(block))

                    def copy(n, buffers=buffers, place=place, start_aux=start_aux):
                        for aux, (buffer, offset) in enumerate(buffers[n]):
                            pltpu.make_async_copy(
                                buffer.at[pl.ds((place & (STRIDE - 1)) + offset, run)],
                                items.at[
                                    slot, pl.ds(block, run), pl.ds((start_aux + aux) * OBLK, OBLK)
                                ],
                                in_sems.at[slot],
                            ).start()

                    branch(lax.shift_right_logical(place, 6), 0, len(buffers), copy)
                    start_aux += group_aux[group]
                if padded > depth:
                    items[slot, pl.ds(block, run), depth:] = jnp.zeros(
                        (run, padded - depth, BLK), items.dtype
                    )

            def step(part, carry):
                block = part * quad
                in_row = code_of(0, orbital, whole_block(block)) >= 0
                for group in range(len(groups)):
                    low = code_of(group, orbital, whole_block(block))
                    high = code_of(group, orbital, whole_block(block) + quad - 1)
                    in_row = jnp.logical_and(in_row, high - low == quad - 1)

                @pl.when(in_row)
                def _():
                    load(block, quad)

                @pl.when(jnp.logical_not(in_row))
                def _():
                    def single(inner, carry):
                        held = code_of(0, orbital, whole_block(block + inner)) >= 0

                        @pl.when(held)
                        def _():
                            load(block + inner, 1)

                        @pl.when(jnp.logical_not(held))
                        def _():
                            items[slot, block + inner] = jnp.zeros((padded, BLK), items.dtype)

                        return carry

                    lax.fori_loop(0, quad, single, 0)

                return carry

            return lax.fori_loop(0, blocks // quad, step, carry)

        lax.fori_loop(0, jnp.minimum(count - begin, room), one, 0)

    def landed(begin):
        def one(slot, carry):
            orbital = state[begin + slot]

            def step(block, carry):
                @pl.when(code_of(0, orbital, whole_block(block)) >= 0)
                def _():
                    whole = items.at[slot, block, pl.ds(0, depth)]
                    pltpu.make_async_copy(whole, whole, in_sems.at[slot]).wait()

                return carry

            return lax.fori_loop(0, blocks, step, carry)

        lax.fori_loop(0, jnp.minimum(count - begin, room), one, 0)

    def multiply(begin, tile):
        rows = span_of(tile)

        def one(slot, carry):
            @pl.when(lax.rem(lax.shift_right_logical(state[met_at + tile], begin + slot), 2) == 1)
            def _():
                turned = []
                for start in range(0, row_tile, step_tile):
                    left = jnp.concatenate(
                        [items[slot, tile * row_tile + start + step] for step in range(step_tile)],
                        axis=1,
                    )
                    turned.append(lax.dot_general(
                        unit[...], left, (((1,), (1,)), ((), ())), preferred_element_type=jnp.float32
                    ).astype(left.dtype))
                turned = jnp.concatenate(turned, axis=0)
                columns = state[columns_at + begin + slot]

                def column(col, carry):
                    @pl.when(lax.rem(lax.shift_right_logical(columns, col), 2) == 1)
                    def _():
                        right = jnp.concatenate(
                            [items[slot, first_right + col * col_tile + step] for step in range(col_tile)],
                            axis=1,
                        )
                        span = pl.ds(pl.multiple_of(col * width, width), width)
                        acc[rows, span] += jnp.dot(turned, right, preferred_element_type=jnp.float32)

                    return carry

                lax.fori_loop(0, col_tiles, column, 0)

            return carry

        lax.fori_loop(0, jnp.minimum(count - begin, room), one, 0)

    fetch(0)
    if first:
        def clear(tile, carry):
            acc[span_of(tile)] = jnp.zeros((height, acc.shape[1]), acc.dtype)
            return carry
    else:
        def clear(tile, carry):
            @pl.when(state[met_at + tile] > 0)
            def _():
                entering(tile).start()
            return carry

    lax.fori_loop(0, row_tiles, clear, 0)
    across = lax.broadcasted_iota(jnp.int32, unit.shape, 1)
    unit[...] = as_number(lax.broadcasted_iota(jnp.int32, unit.shape, 0) == across).astype(unit.dtype)
    passes = (count + room - 1) // room
    if first:
        passes = jnp.maximum(passes, 1)

    def one_pass(turn, carry):
        begin = turn * room

        @pl.when(turn > 0)
        def _():
            fetch(begin)

        landed(begin)

        def row_step(tile, carry):
            touched = jnp.logical_or(first, state[met_at + tile] > 0)

            @pl.when(touched)
            def _():
                if not first:
                    @pl.when(turn == 0)
                    def _():
                        entering(tile).wait()
                multiply(begin, tile)

                @pl.when(turn == passes - 1)
                def _():
                    leaving(tile).start()

            return carry

        lax.fori_loop(0, row_tiles, row_step, 0)
        return carry

    lax.fori_loop(0, passes, one_pass, 0)

    def row_end(tile, carry):
        @pl.when(jnp.logical_or(first, state[met_at + tile] > 0))
        def _():
            leaving(tile).wait()

        return carry

    lax.fori_loop(0, row_tiles, row_end, 0)


def tile_of(blocks):
    return 4 if blocks % 4 == 0 else 3 if blocks % 3 == 0 else 1


def product(loc, meta, sources, held, after, stages, orbitals, row_blocks, col_blocks):
    groups = [[[offset for _, offset in refs] for refs in group] for group in sources]
    flat = [array for group in sources for refs in group for array, _ in refs]
    total_aux = sum(len(group[0]) for group in sources)
    rows, cols = row_blocks * BLK, col_blocks * BLK
    row_tile = tile_of(row_blocks)
    step_tile = 2 if row_tile % 2 == 0 else row_tile
    row_tiles = row_blocks // row_tile
    padded = -(-total_aux * OBLK // 256) * 256
    room = 2
    first = held is None
    in_hbm = pl.BlockSpec(memory_space=pltpu.HBM)
    in_any = pl.BlockSpec(memory_space=pl.ANY)
    return pl.pallas_call(
        functools.partial(
            product_kernel, groups, orbitals, row_blocks, col_blocks, stages, first, len(after)
        ),
        grid_spec=pltpu.PrefetchScalarGridSpec(
            num_scalar_prefetch=2,
            grid=(),
            in_specs=[in_hbm] * (not first)
            + [in_any] * (len(flat) + len(after)),
            out_specs=[in_hbm, pl.BlockSpec(memory_space=pltpu.VMEM)],
            scratch_shapes=[
                pltpu.VMEM((room, row_blocks + col_blocks, padded, BLK), jnp.bfloat16),
                pltpu.VMEM((rows, cols), jnp.float32),
                pltpu.VMEM((step_tile * BLK, step_tile * BLK), jnp.bfloat16),
                pltpu.SMEM((2 * orbitals + row_tiles + 1,), jnp.int32),
                pltpu.SemaphoreType.DMA((room,)),
                pltpu.SemaphoreType.DMA((row_tiles,)),
                pltpu.SemaphoreType.DMA((row_tiles,)),
            ],
        ),
        out_shape=[
            jax.ShapeDtypeStruct((rows, cols), jnp.float32),
            jax.ShapeDtypeStruct((8, 128), jnp.float32),
        ],
        input_output_aliases={} if first else {2: 0},
        compiler_params=pltpu.CompilerParams(
            vmem_limit_bytes=2 * room * padded * (rows + cols) + 4 * rows * cols + 4 * MIB
        ),
        cost_estimate=pl.CostEstimate(
            flops=2 * rows * cols * total_aux * OBLK * orbitals,
            bytes_accessed=4 * rows * cols,
            transcendentals=0,
        ),
        name="product",
    )(loc, meta, *([] if first else [held]), *flat, *after)


def rounds(size, add, table, own):
    first = [(0, 1), (1, 0), (2, 3), (3, 2)]
    second = []
    for aux in range(4):
        here, there = aux * 4, (aux ^ 1) * 4
        second += [(here, there), (here + 1, here + 2), (here + 2, here + 1), (here + 3, there + 3)]
    across = [(0, 2), (2, 0), (1, 3), (3, 1)]

    def to_core(held):
        return lax.ppermute(held, "aux", first)

    moved, crossed, passed, core_crossed = [], [], [], []
    core_own = to_core(own)
    total, done = None, []
    calls = {2: (0, 1), 3: (2, 2), 4: (3, 3), 5: (4, 4)}
    if size == LEVELS[-1]:
        calls = {ROUNDS: (0, HOPS)}
    for turn in range(ROUNDS + 1):
        chunks = []
        if turn < ROUNDS:
            streams = (0, 1, 2) if turn < HOPS else (2,)
            after = crossed[-1:] + ([core_own] if turn == 1 else done)
            chunks = gather(turn, size, table, [own] + moved, streams, len(moved[-2:]), after)
        if turn > 0:
            if turn < ROUNDS:
                passed.append(to_core(chunks[-1]))
            crossed[-1] = relay(crossed[-1], (chunks or done or [own])[0])
            core_crossed.append(to_core(crossed[-1]))
        if turn in calls:
            near = [[(own, 0), (core_own, 0)]]
            for index, held in enumerate(moved):
                near.append([(held, 0), (passed[index // 2], index % 2 * size)])
            far = [[(held, 0), (other, 0)] for held, other in zip(crossed, core_crossed)]
            total, token = add(
                table[3 * PLACES:6 * PLACES], [near, far], total, chunks[:1], calls[turn]
            )
            done = [token]
        if turn < HOPS:
            moved.append(lax.ppermute(chunks[0], "occ", first))
            moved.append(lax.ppermute(chunks[1], ("aux", "occ"), second))
        if turn < ROUNDS:
            crossed.append(lax.ppermute(chunks[2 if turn < HOPS else 0], "aux", across))
    return total


def on_device(shape, factors, block_mask, block_lists):
    aux_count, occ_count = shape["aux"], shape["occ"]
    own_orbitals, slots = block_lists.shape
    aux, occ = lax.axis_index("aux"), lax.axis_index("occ")
    row_blocks, col_blocks = NB // aux_count, NB // occ_count
    meta = jnp.stack([aux * row_blocks, occ * col_blocks]).astype(jnp.int32)

    def add(loc, sources, held, after, stages):
        return product(loc, meta, sources, held, after, stages, NOB, row_blocks, col_blocks)

    kept = block_mask.T > 0
    if aux_count == 4 and occ_count == 4:
        mask = as_number(kept).reshape(1, PLACES)
        where = jnp.stack([aux, occ]).astype(jnp.int32)
        table = plan(where, mask, slots)
        own = pick(factors, block_lists)
        return lax.switch(
            table[6, 0],
            [functools.partial(rounds, size, add) for size in LEVELS],
            table.reshape(-1),
            own,
        )
    own = pick(factors, block_lists)
    everything = lax.all_gather(lax.all_gather(own, "aux"), "occ")
    sources = [[(everything[z, a], 0) for a in range(aux_count)] for z in range(occ_count)]
    earlier = jnp.arange(NB)[None, :] < jnp.arange(NB)[:, None]
    rank = jnp.sum(kept[:, None, :] & earlier[None], axis=2, dtype=jnp.int32)
    orbital = jnp.arange(NOB, dtype=jnp.int32)[:, None]
    start = orbital // own_orbitals * STRIDE + orbital % own_orbitals * slots
    loc = jnp.concatenate([
        jnp.where(kept, rank + start, -1).reshape(-1), jnp.zeros(PLACES, jnp.int32)
    ])
    return add(loc, [sources], None, [], (0, 0))[0]


def solution(mesh):
    placed = (P(("parts", "aux"), "occ", None), P("parts", None), P(("parts", "occ"), None))
    return jax.shard_map(
        functools.partial(on_device, dict(mesh.shape)),
        mesh=mesh,
        in_specs=placed,
        out_specs=P(("parts", "aux"), "occ"),
        check_vma=False,
    )
```

```python
import functools
import math

import jax
import jax.numpy as jnp
from jax import lax
from jax.experimental import pallas as pl
from jax.experimental.pallas import tpu as pltpu
from jax.sharding import PartitionSpec as P

BLK = 128
OBLK = 112
NB = 48
NOB = 8
PLACES = NOB * NB
STRIDE = 64
ROUNDS = 5
HOPS = ROUNDS - 1
LEVELS = (15, 18, 21, 48)
RUN = 3
MIB = 1024 * 1024


def pick_kernel(lists, factors, *refs):
    items = refs[-1]
    orbitals, slots = lists.shape

    def step(slot, carry):
        for orbital in range(orbitals):
            block = jnp.maximum(lists[orbital, slot], 0)
            columns = pl.ds(pl.multiple_of(block * BLK, BLK), BLK)
            rows = slice(orbital * OBLK, (orbital + 1) * OBLK)
            items[orbital * slots + slot] = factors[0, rows, columns]
        return carry

    lax.fori_loop(0, slots, step, 0)


def pick(factors, block_lists, after=()):
    orbitals, slots = block_lists.shape
    count = orbitals * slots
    return pl.pallas_call(
        pick_kernel,
        grid_spec=pltpu.PrefetchScalarGridSpec(
            num_scalar_prefetch=1,
            grid=(),
            in_specs=[pl.BlockSpec(memory_space=pltpu.VMEM)]
            + [pl.BlockSpec(memory_space=pl.ANY)] * len(after),
            out_specs=pl.BlockSpec(memory_space=pltpu.VMEM),
        ),
        out_shape=jax.ShapeDtypeStruct((count, OBLK, BLK), factors.dtype),
        compiler_params=pltpu.CompilerParams(vmem_limit_bytes=16 * MIB),
        cost_estimate=pl.CostEstimate(
            flops=0, bytes_accessed=4 * count * OBLK * BLK, transcendentals=0
        ),
        name="pick",
    )(block_lists, factors, *after)


def as_number(condition):
    return jnp.where(condition, 1.0, 0.0)


def place_facts(shape, axis):
    place = lax.broadcasted_iota(jnp.int32, shape, axis).astype(jnp.float32)
    orbital = jnp.floor((place + 0.5) / NB)
    block = place - NB * orbital
    quarter = jnp.floor((block + 0.5) / (NB // 4))
    return place, orbital, quarter, jnp.floor((quarter + 0.5) / 2), jnp.floor((orbital + 0.5) / 2)


def plan_kernel(slots, where, masks, out):
    rows = levels = 8
    wide = (rows, PLACES)
    _, orbital, quarter, half, origin = place_facts(wide, 1)
    row = lax.broadcasted_iota(jnp.int32, wide, 0)
    kept = jnp.broadcast_to(masks[...], wide)
    capacity = jnp.zeros(wide, jnp.float32)
    for index, size in enumerate(LEVELS + LEVELS[-1:] * (levels - len(LEVELS))):
        capacity = jnp.where(row == index, float(size), capacity)

    square = (PLACES, PLACES)
    down_place, down_orbital, _, _, _ = place_facts(square, 0)
    over_place, over_orbital, _, _, _ = place_facts(square, 1)
    same = as_number(down_orbital == over_orbital)
    before = as_number(down_place < over_place)
    within = (same * before).astype(jnp.bfloat16)
    same, before = same.astype(jnp.bfloat16), before.astype(jnp.bfloat16)

    def times(parts, matrix):
        stacked = jnp.concatenate(parts, axis=0).astype(jnp.bfloat16)
        product = jnp.dot(stacked, matrix, preferred_element_type=jnp.float32)
        return [product[index * rows:(index + 1) * rows] for index in range(len(parts))]

    touching = times([kept * as_number(quarter == z) for z in range(4)], same)
    need = [kept * as_number(touch > 0) for touch in touching]
    zero = jnp.zeros(wide, jnp.float32)

    def union(parts):
        best = zero
        for part in parts:
            best = jnp.maximum(best, part)
        return best

    x_need = []
    for x in range(2):
        touched = as_number(touching[2 * x] + touching[2 * x + 1] > 0)
        here = as_number(half == x)
        x_need.append([
            need[z] * jnp.maximum(here, as_number(quarter == z) * touched) for z in range(4)
        ])
    mine = [kept * as_number(origin == z) for z in range(4)]
    need_up = [union(need[z + 1:]) for z in range(4)]
    far_up = [union(need[z + 2:]) for z in range(4)]
    need_down = [union(need[:z]) for z in range(4)]
    far_down = [union(need[:max(z - 1, 0)]) for z in range(4)]
    up = [mine[z] * need_up[z] for z in range(4)]
    down = [mine[z] * need_down[z] for z in range(4)]
    cross = [[mine[z] * x_need[x][z] for z in range(4)] for x in range(2)]
    up_code, down_code = [zero] * 4, [zero] * 4
    cross_code = [[zero] * 4, [zero] * 4]

    for turn in range(ROUNDS):
        parts = []
        if turn < HOPS:
            for z in range(3):
                parts += [up[z] * far_up[z], up[z] - up[z] * far_up[z]]
                parts += [down[z + 1] * far_down[z + 1], down[z + 1] - down[z + 1] * far_down[z + 1]]
        parts += [cross[x][z] for x in range(2) for z in range(4)]
        ranks = iter(zip(parts, times(parts, before)))

        def taken(pairs):
            rank, total = zero, 0.0
            chosen = zero
            for part, counted in pairs:
                rank = rank + part * (counted + total)
                total = total + jnp.sum(part, axis=1, keepdims=True)
                chosen = chosen + part
            chosen = chosen * as_number(rank < capacity)
            return chosen, chosen * (rank + float(turn * STRIDE + 1))

        up_sent, down_sent = [], []
        if turn < HOPS:
            for z in range(3):
                sent, code = taken([next(ranks), next(ranks)])
                up_sent.append(sent)
                up_code[z] = up_code[z] + code
                up[z] = up[z] - sent
                sent, code = taken([next(ranks), next(ranks)])
                down_sent.append(sent)
                down_code[z + 1] = down_code[z + 1] + code
                down[z + 1] = down[z + 1] - sent
        for x in range(2):
            for z in range(4):
                sent, code = taken([next(ranks)])
                cross_code[x][z] = cross_code[x][z] + code
                cross[x][z] = cross[x][z] - sent
        if turn < HOPS:
            for z in range(3):
                up[z + 1] = up[z + 1] + up_sent[z] * need_up[z + 1]
                down[z] = down[z] + down_sent[z] * need_down[z]
                for x in range(2):
                    cross[x][z + 1] = cross[x][z + 1] + up_sent[z] * x_need[x][z + 1]
                    cross[x][z] = cross[x][z] + down_sent[z] * x_need[x][z]

    left = zero
    for part in up + down + cross[0] + cross[1]:
        left = left + part
    left = jnp.sum(left, axis=1, keepdims=True)
    order = lax.broadcasted_iota(jnp.int32, (levels, 1), 0).astype(jnp.float32)
    level = jnp.min(jnp.where(left > 0, float(len(LEVELS) - 1), order), axis=0, keepdims=True)
    level_row = as_number(
        lax.broadcasted_iota(jnp.int32, (levels, PLACES), 0).astype(jnp.float32) == level
    )
    me_x, me_z = where[0] // 2, where[1]
    odd = lax.rem(me_z, 2).astype(jnp.float32)

    def at(parts, z):
        total = jnp.zeros((levels, PLACES), jnp.float32)
        for index, part in enumerate(parts):
            total = total + jnp.where(z == index, 1.0, 0.0) * part[:levels]
        return jnp.sum(total * level_row, axis=0, keepdims=True)

    cross_here = [jnp.where(me_x == 0, cross_code[0][z], cross_code[1][z]) for z in range(4)]
    cross_there = [jnp.where(me_x == 0, cross_code[1][z], cross_code[0][z]) for z in range(4)]
    def turn_of(code):
        return jnp.floor((code - 0.5) / STRIDE)

    got_up, got_down = at(up_code, me_z - 1), at(down_code, me_z + 1)
    got_cross = at(cross_here, me_z)
    inner = jnp.dot(kept.astype(jnp.bfloat16), within, preferred_element_type=jnp.float32)[0:1]
    one_orbital, one_origin = orbital[0:1], origin[0:1]
    slot = inner + slots * (one_orbital - 2 * one_origin)
    owned = kept[0:1] * as_number(one_origin == me_z.astype(jnp.float32))
    held = (
        owned * (slot + 1)
        + as_number(got_up > 0) * (got_up + STRIDE * (2 - odd + turn_of(got_up)))
        + as_number(got_down > 0) * (got_down + STRIDE * (1 + odd + turn_of(got_down)))
        - 1
    )
    crossed = got_cross - 1
    near = jnp.maximum(
        as_number(quarter[0:1] == where[0].astype(jnp.float32)),
        as_number(quarter[0:1] == me_z.astype(jnp.float32)),
    )
    arrival = jnp.maximum(
        as_number(got_up + got_down > 0) * turn_of(got_up + got_down),
        as_number(got_cross > 0) * turn_of(got_cross),
    )
    lane = lax.broadcasted_iota(jnp.int32, (1, PLACES), 1)
    stage = jnp.zeros((1, PLACES), jnp.float32)
    for index in range(NOB):
        inside = as_number(one_orbital == float(index)) * near * kept[0:1]
        stage = jnp.where(
            lane == index, jnp.max(arrival * inside, axis=1, keepdims=True), stage
        )

    buffer = jnp.floor((held + 0.5) / STRIDE)
    tall = (PLACES, PLACES)
    target = lax.broadcasted_iota(jnp.int32, tall, 0).astype(jnp.float32) + 1
    blank = jnp.zeros_like(held)
    pair = jnp.concatenate([buffer, held - STRIDE * buffer, blank + 1] + [blank] * 5, axis=0)
    position = lax.broadcasted_iota(jnp.int32, (1, PLACES), 1).astype(jnp.float32)
    spare = position - STRIDE * jnp.floor((position + 0.5) / STRIDE)
    sends = []
    sent_up, sent_down = at(up_code, me_z), at(down_code, me_z)
    for sent in (
        jnp.where(odd > 0, sent_down, sent_up),
        jnp.where(odd > 0, sent_up, sent_down),
        at(cross_there, me_z),
    ):
        chosen = as_number(target == sent).astype(jnp.bfloat16)
        both = lax.dot_general(
            pair.astype(jnp.bfloat16), chosen, (((1,), (1,)), ((), ())),
            preferred_element_type=jnp.float32,
        )
        filled = both[0:1] * STRIDE + both[1:2]
        sends.append(jnp.where(both[2:3] > 0, filled, spare))
    flat = level + jnp.zeros((1, PLACES), jnp.float32)
    result = jnp.concatenate(sends + [held, crossed, stage, flat, flat], axis=0)
    out[...] = result.astype(jnp.int32)


def plan(where, masks, slots):
    in_vmem = pl.BlockSpec(memory_space=pltpu.VMEM)
    return pl.pallas_call(
        functools.partial(plan_kernel, slots),
        grid_spec=pltpu.PrefetchScalarGridSpec(
            num_scalar_prefetch=1, grid=(), in_specs=[in_vmem], out_specs=in_vmem
        ),
        out_shape=jax.ShapeDtypeStruct((8, PLACES), jnp.int32),
        compiler_params=pltpu.CompilerParams(vmem_limit_bytes=16 * MIB),
        name="plan",
    )(where, masks)


def branch(which, low, high, run):
    if high - low == 1:
        run(low)
        return
    middle = (low + high) // 2

    @pl.when(which < middle)
    def _():
        branch(which, low, middle, run)

    @pl.when(which >= middle)
    def _():
        branch(which, middle, high, run)


def gather_kernel(turn, held, streams, passed, table, *refs):
    buffers, sem = refs[:held], refs[-1]
    outs = refs[len(refs) - 1 - len(streams) - (passed > 0):-1]
    size = outs[0].shape[0]
    for place in range(passed):
        span = pl.ds(place * size, size)
        pltpu.make_async_copy(buffers[held - passed + place], outs[-1].at[span], sem).start()

    def load(stream, at, code, run):
        def copy(n):
            outs[stream][pl.ds(at, run)] = buffers[n][pl.ds(code & (STRIDE - 1), run)]

        branch(lax.shift_right_logical(code, 6), 0, held, copy)

    run = RUN if size < LEVELS[-1] else 1

    def step(part, carry):
        at = part * run
        for index, stream in enumerate(streams):
            start = stream * PLACES + turn * STRIDE + at
            if run == 1:
                load(index, at, table[start], 1)
                continue
            codes = [table[start + inner] for inner in range(RUN)]
            in_row = codes[1] - codes[0] == 1
            for inner in range(2, RUN):
                in_row = jnp.logical_and(in_row, codes[inner] - codes[inner - 1] == 1)

            @pl.when(in_row)
            def _(index=index, codes=codes):
                load(index, at, codes[0], RUN)

            @pl.when(jnp.logical_not(in_row))
            def _(index=index, start=start):
                def single(inner, carry):
                    load(index, at + inner, table[start + inner], 1)
                    return carry

                lax.fori_loop(0, RUN, single, 0)

        return carry

    lax.fori_loop(0, size // run, step, 0)
    if passed:
        pltpu.make_async_copy(outs[-1], outs[-1], sem).wait()


def gather(turn, size, table, buffers, streams, passed, after):
    dtype = buffers[0].dtype
    shapes = [jax.ShapeDtypeStruct((size, OBLK, BLK), dtype) for _ in streams]
    if passed:
        shapes.append(jax.ShapeDtypeStruct((size * passed, OBLK, BLK), dtype))
    in_vmem = pl.BlockSpec(memory_space=pltpu.VMEM)
    return pl.pallas_call(
        functools.partial(gather_kernel, turn, len(buffers), streams, passed),
        grid_spec=pltpu.PrefetchScalarGridSpec(
            num_scalar_prefetch=1,
            grid=(),
            in_specs=[in_vmem] * len(buffers) + [pl.BlockSpec(memory_space=pl.ANY)] * len(after),
            out_specs=[in_vmem] * len(shapes),
            scratch_shapes=[pltpu.SemaphoreType.DMA(())],
        ),
        out_shape=shapes,
        compiler_params=pltpu.CompilerParams(
            vmem_limit_bytes=2 * sum(array.size for array in [*buffers, *shapes]) + 3 * MIB
        ),
        cost_estimate=pl.CostEstimate(
            flops=0, bytes_accessed=4 * len(streams) * size * OBLK * BLK, transcendentals=0
        ),
        name="gather",
    )(table, *buffers, *after)


def relay_kernel(source, token, out):
    pass


def relay(source, token):
    in_any = pl.BlockSpec(memory_space=pl.ANY)
    return pl.pallas_call(
        relay_kernel,
        in_specs=[in_any, in_any],
        out_specs=in_any,
        out_shape=jax.ShapeDtypeStruct(source.shape, source.dtype),
        input_output_aliases={0: 0},
        compiler_params=pltpu.CompilerParams(vmem_limit_bytes=2 * MIB),
        name="relay",
    )(source, token)


def product_kernel(
    groups, orbitals, row_blocks, col_blocks, stages, first, extra, loc, meta, *refs
):
    flat = iter(refs)
    before = None if first else next(flat)
    sources = [
        [[(next(flat), offset) for offset in offsets] for offsets in buffers] for buffers in groups
    ]
    for _ in range(extra):
        next(flat)
    out, done, items, acc, unit, state, in_sems, acc_sems, out_sems = flat
    group_aux = [len(buffers[0]) for buffers in groups]
    row_tile, col_tile = tile_of(row_blocks), tile_of(col_blocks)
    step_tile = unit.shape[0] // BLK
    col_tiles = col_blocks // col_tile
    first_row, first_col = meta[0], meta[1]
    room = items.shape[0]
    quad = math.gcd(row_blocks, col_blocks, 4)
    if quad == 1:
        quad = math.gcd(row_blocks, col_blocks)
    if stages[0] < stages[1] - 1:
        quad = 1
    blocks, first_right = row_blocks + col_blocks, row_blocks
    if row_blocks == col_blocks:
        alike = first_row == first_col
        blocks = jnp.where(alike, row_blocks, blocks)
        first_right = jnp.where(alike, 0, first_right)
    depth = sum(group_aux) * OBLK
    padded = items.shape[2]
    height, width = row_tile * BLK, col_tile * BLK
    row_tiles = row_blocks // row_tile
    met_at, columns_at = orbitals, orbitals + row_tiles

    def code_of(group, orbital, block):
        return loc[group * PLACES + orbital * NB + block]

    def any_kept(orbital, start, count):
        best = code_of(0, orbital, start)
        for step in range(1, count):
            best = jnp.maximum(best, code_of(0, orbital, start + step))
        return best >= 0

    def whole_block(block):
        return jnp.where(block < row_blocks, first_row + block, first_col + block - row_blocks)

    def span_of(tile):
        return pl.ds(pl.multiple_of(tile * height, height), height)

    def entering(tile):
        return pltpu.make_async_copy(before.at[span_of(tile)], acc.at[span_of(tile)], acc_sems.at[tile])

    def leaving(tile):
        return pltpu.make_async_copy(acc.at[span_of(tile)], out.at[span_of(tile)], out_sems.at[tile])

    def survey(orbital, count):
        stage = loc[len(groups) * PLACES + orbital]
        wanted = jnp.logical_and(stage >= stages[0], stage <= stages[1])
        state[columns_at + count] = 0

        @pl.when(wanted)
        def _():
            @pl.when(any_kept(orbital, first_row, row_blocks))
            def _():
                columns = jnp.int32(0)
                for col in range(col_tiles):
                    held = any_kept(orbital, first_col + col * col_tile, col_tile)
                    columns = columns + jnp.where(held, 1 << col, 0)
                state[columns_at + count] = columns

        wanted = state[columns_at + count] > 0

        @pl.when(wanted)
        def _():
            state[count] = orbital
            for tile in range(row_tiles):
                held = any_kept(orbital, first_row + tile * row_tile, row_tile)
                state[met_at + tile] = state[met_at + tile] + jnp.where(held, 1 << count, 0)

        return count + jnp.where(wanted, 1, 0)

    for tile in range(row_tiles):
        state[met_at + tile] = 0
    count = lax.fori_loop(0, orbitals, survey, jnp.int32(0))
    done[...] = jnp.zeros(done.shape, done.dtype)

    def fetch(begin):
        def one(slot, carry):
            orbital = state[begin + slot]

            def load(block, run):
                start_aux = 0
                for group, buffers in enumerate(sources):
                    place = code_of(group, orbital, whole_block(block))

                    def copy(n, buffers=buffers, place=place, start_aux=start_aux):
                        for aux, (buffer, offset) in enumerate(buffers[n]):
                            pltpu.make_async_copy(
                                buffer.at[pl.ds((place & (STRIDE - 1)) + offset, run)],
                                items.at[
                                    slot, pl.ds(block, run), pl.ds((start_aux + aux) * OBLK, OBLK)
                                ],
                                in_sems.at[slot],
                            ).start()

                    branch(lax.shift_right_logical(place, 6), 0, len(buffers), copy)
                    start_aux += group_aux[group]
                if padded > depth:
                    items[slot, pl.ds(block, run), depth:] = jnp.zeros(
                        (run, padded - depth, BLK), items.dtype
                    )

            def step(part, carry):
                block = part * quad

                def single(inner, carry):
                    held = code_of(0, orbital, whole_block(block + inner)) >= 0

                    @pl.when(held)
                    def _():
                        load(block + inner, 1)

                    @pl.when(jnp.logical_not(held))
                    def _():
                        items[slot, block + inner] = jnp.zeros((padded, BLK), items.dtype)

                    return carry

                if quad == 1:
                    return single(0, carry)
                in_row = code_of(0, orbital, whole_block(block)) >= 0
                for group in range(len(groups)):
                    low = code_of(group, orbital, whole_block(block))
                    high = code_of(group, orbital, whole_block(block) + quad - 1)
                    in_row = jnp.logical_and(in_row, high - low == quad - 1)

                @pl.when(in_row)
                def _():
                    load(block, quad)

                @pl.when(jnp.logical_not(in_row))
                def _():
                    lax.fori_loop(0, quad, single, 0)

                return carry

            return lax.fori_loop(0, blocks // quad, step, carry)

        lax.fori_loop(0, jnp.minimum(count - begin, room), one, 0)

    def landed(begin):
        def one(slot, carry):
            orbital = state[begin + slot]

            def step(block, carry):
                @pl.when(code_of(0, orbital, whole_block(block)) >= 0)
                def _():
                    whole = items.at[slot, block, pl.ds(0, depth)]
                    pltpu.make_async_copy(whole, whole, in_sems.at[slot]).wait()

                return carry

            return lax.fori_loop(0, blocks, step, carry)

        lax.fori_loop(0, jnp.minimum(count - begin, room), one, 0)

    def multiply(begin, tile):
        rows = span_of(tile)

        def one(slot, carry):
            @pl.when(lax.rem(lax.shift_right_logical(state[met_at + tile], begin + slot), 2) == 1)
            def _():
                turned = []
                for start in range(0, row_tile, step_tile):
                    left = jnp.concatenate(
                        [items[slot, tile * row_tile + start + step] for step in range(step_tile)],
                        axis=1,
                    )
                    turned.append(lax.dot_general(
                        unit[...], left, (((1,), (1,)), ((), ())), preferred_element_type=jnp.float32
                    ).astype(left.dtype))
                turned = jnp.concatenate(turned, axis=0)
                columns = state[columns_at + begin + slot]

                def column(col, carry):
                    @pl.when(lax.rem(lax.shift_right_logical(columns, col), 2) == 1)
                    def _():
                        right = jnp.concatenate(
                            [items[slot, first_right + col * col_tile + step] for step in range(col_tile)],
                            axis=1,
                        )
                        span = pl.ds(pl.multiple_of(col * width, width), width)
                        acc[rows, span] += jnp.dot(turned, right, preferred_element_type=jnp.float32)

                    return carry

                lax.fori_loop(0, col_tiles, column, 0)

            return carry

        lax.fori_loop(0, jnp.minimum(count - begin, room), one, 0)

    fetch(0)
    if first:
        def clear(tile, carry):
            acc[span_of(tile)] = jnp.zeros((height, acc.shape[1]), acc.dtype)
            return carry
    else:
        def clear(tile, carry):
            @pl.when(state[met_at + tile] > 0)
            def _():
                entering(tile).start()
            return carry

    lax.fori_loop(0, row_tiles, clear, 0)
    across = lax.broadcasted_iota(jnp.int32, unit.shape, 1)
    unit[...] = as_number(lax.broadcasted_iota(jnp.int32, unit.shape, 0) == across).astype(unit.dtype)
    passes = (count + room - 1) // room
    if first:
        passes = jnp.maximum(passes, 1)

    def one_pass(turn, carry):
        begin = turn * room

        @pl.when(turn > 0)
        def _():
            fetch(begin)

        landed(begin)

        def row_step(tile, carry):
            touched = jnp.logical_or(first, state[met_at + tile] > 0)

            @pl.when(touched)
            def _():
                if not first:
                    @pl.when(turn == 0)
                    def _():
                        entering(tile).wait()
                multiply(begin, tile)

                @pl.when(turn == passes - 1)
                def _():
                    leaving(tile).start()

            return carry

        lax.fori_loop(0, row_tiles, row_step, 0)
        return carry

    lax.fori_loop(0, passes, one_pass, 0)

    def row_end(tile, carry):
        @pl.when(jnp.logical_or(first, state[met_at + tile] > 0))
        def _():
            leaving(tile).wait()

        return carry

    lax.fori_loop(0, row_tiles, row_end, 0)


def tile_of(blocks):
    return 4 if blocks % 4 == 0 else 3 if blocks % 3 == 0 else 1


def product(loc, meta, sources, held, after, stages, orbitals, row_blocks, col_blocks):
    groups = [[[offset for _, offset in refs] for refs in group] for group in sources]
    flat = [array for group in sources for refs in group for array, _ in refs]
    total_aux = sum(len(group[0]) for group in sources)
    rows, cols = row_blocks * BLK, col_blocks * BLK
    row_tile = tile_of(row_blocks)
    step_tile = 2 if row_tile % 2 == 0 else row_tile
    row_tiles = row_blocks // row_tile
    padded = -(-total_aux * OBLK // 256) * 256
    room = 2
    first = held is None
    in_hbm = pl.BlockSpec(memory_space=pltpu.HBM)
    in_any = pl.BlockSpec(memory_space=pl.ANY)
    return pl.pallas_call(
        functools.partial(
            product_kernel, groups, orbitals, row_blocks, col_blocks, stages, first, len(after)
        ),
        grid_spec=pltpu.PrefetchScalarGridSpec(
            num_scalar_prefetch=2,
            grid=(),
            in_specs=[in_hbm] * (not first)
            + [in_any] * (len(flat) + len(after)),
            out_specs=[in_hbm, pl.BlockSpec(memory_space=pltpu.VMEM)],
            scratch_shapes=[
                pltpu.VMEM((room, row_blocks + col_blocks, padded, BLK), jnp.bfloat16),
                pltpu.VMEM((rows, cols), jnp.float32),
                pltpu.VMEM((step_tile * BLK, step_tile * BLK), jnp.bfloat16),
                pltpu.SMEM((2 * orbitals + row_tiles + 1,), jnp.int32),
                pltpu.SemaphoreType.DMA((room,)),
                pltpu.SemaphoreType.DMA((row_tiles,)),
                pltpu.SemaphoreType.DMA((row_tiles,)),
            ],
        ),
        out_shape=[
            jax.ShapeDtypeStruct((rows, cols), jnp.float32),
            jax.ShapeDtypeStruct((8, 128), jnp.float32),
        ],
        input_output_aliases={} if first else {2: 0},
        compiler_params=pltpu.CompilerParams(
            vmem_limit_bytes=2 * room * padded * (rows + cols) + 4 * rows * cols + 4 * MIB
        ),
        cost_estimate=pl.CostEstimate(
            flops=2 * rows * cols * total_aux * OBLK * orbitals,
            bytes_accessed=4 * rows * cols,
            transcendentals=0,
        ),
        name="product",
    )(loc, meta, *([] if first else [held]), *flat, *after)


def rounds(size, add, table, own):
    first = [(0, 1), (1, 0), (2, 3), (3, 2)]
    second = []
    for aux in range(4):
        here, there = aux * 4, (aux ^ 1) * 4
        second += [(here, there), (here + 1, here + 2), (here + 2, here + 1), (here + 3, there + 3)]
    across = [(0, 2), (2, 0), (1, 3), (3, 1)]

    def to_core(held):
        return lax.ppermute(held, "aux", first)

    moved, crossed, passed, core_crossed = [], [], [], []
    core_own = to_core(own)
    total, done = None, []
    calls = {2: (0, 1), 3: (2, 2), 4: (3, 3), 5: (4, 4)}
    if size == LEVELS[-1]:
        calls = {ROUNDS: (0, HOPS)}
    for turn in range(ROUNDS + 1):
        chunks = []
        if turn < ROUNDS:
            streams = (0, 1, 2) if turn < HOPS else (2,)
            after = crossed[-1:] + ([core_own] if turn == 1 else done)
            chunks = gather(turn, size, table, [own] + moved, streams, len(moved[-2:]), after)
        if turn > 0:
            if turn < ROUNDS:
                passed.append(to_core(chunks[-1]))
            crossed[-1] = relay(crossed[-1], (chunks or done or [own])[0])
            core_crossed.append(to_core(crossed[-1]))
        if turn in calls:
            near = [[(own, 0), (core_own, 0)]]
            for index, held in enumerate(moved):
                near.append([(held, 0), (passed[index // 2], index % 2 * size)])
            far = [[(held, 0), (other, 0)] for held, other in zip(crossed, core_crossed)]
            total, token = add(
                table[3 * PLACES:6 * PLACES], [near, far], total, chunks[:1], calls[turn]
            )
            done = [token]
        if turn < HOPS:
            moved.append(lax.ppermute(chunks[0], "occ", first))
            moved.append(lax.ppermute(chunks[1], ("aux", "occ"), second))
        if turn < ROUNDS:
            crossed.append(lax.ppermute(chunks[2 if turn < HOPS else 0], "aux", across))
    return total


def on_device(shape, factors, block_mask, block_lists):
    aux_count, occ_count = shape["aux"], shape["occ"]
    own_orbitals, slots = block_lists.shape
    aux, occ = lax.axis_index("aux"), lax.axis_index("occ")
    row_blocks, col_blocks = NB // aux_count, NB // occ_count
    meta = jnp.stack([aux * row_blocks, occ * col_blocks]).astype(jnp.int32)

    def add(loc, sources, held, after, stages):
        return product(loc, meta, sources, held, after, stages, NOB, row_blocks, col_blocks)

    kept = block_mask.T > 0
    if aux_count == 4 and occ_count == 4:
        mask = as_number(kept).reshape(1, PLACES)
        where = jnp.stack([aux, occ]).astype(jnp.int32)
        table = plan(where, mask, slots)
        own = pick(factors, block_lists)
        return lax.switch(
            table[6, 0],
            [functools.partial(rounds, size, add) for size in LEVELS],
            table.reshape(-1),
            own,
        )
    own = pick(factors, block_lists)
    everything = lax.all_gather(lax.all_gather(own, "aux"), "occ")
    sources = [[(everything[z, a], 0) for a in range(aux_count)] for z in range(occ_count)]
    earlier = jnp.arange(NB)[None, :] < jnp.arange(NB)[:, None]
    rank = jnp.sum(kept[:, None, :] & earlier[None], axis=2, dtype=jnp.int32)
    orbital = jnp.arange(NOB, dtype=jnp.int32)[:, None]
    start = orbital // own_orbitals * STRIDE + orbital % own_orbitals * slots
    loc = jnp.concatenate([
        jnp.where(kept, rank + start, -1).reshape(-1), jnp.zeros(PLACES, jnp.int32)
    ])
    return add(loc, [sources], None, [], (0, 0))[0]


def solution(mesh):
    placed = (P(("parts", "aux"), "occ", None), P("parts", None), P(("parts", "occ"), None))
    return jax.shard_map(
        functools.partial(on_device, dict(mesh.shape)),
        mesh=mesh,
        in_specs=placed,
        out_specs=P(("parts", "aux"), "occ"),
        check_vma=False,
    )
```

```python
import functools
import math

import jax
import jax.numpy as jnp
from jax import lax
from jax.experimental import pallas as pl
from jax.experimental.pallas import tpu as pltpu
from jax.sharding import PartitionSpec as P

BLK = 128
OBLK = 112
NB = 48
NOB = 8
PLACES = NOB * NB
STRIDE = 64
ROUNDS = 5
HOPS = ROUNDS - 1
LEVELS = (15, 18, 21, 48)
RUN = 3
MIB = 1024 * 1024


def pick_kernel(lists, factors, *refs):
    items = refs[-1]
    orbitals, slots = lists.shape

    def step(slot, carry):
        for orbital in range(orbitals):
            block = jnp.maximum(lists[orbital, slot], 0)
            columns = pl.ds(pl.multiple_of(block * BLK, BLK), BLK)
            rows = slice(orbital * OBLK, (orbital + 1) * OBLK)
            items[orbital * slots + slot] = factors[0, rows, columns]
        return carry

    lax.fori_loop(0, slots, step, 0)


def pick(factors, block_lists, after=()):
    orbitals, slots = block_lists.shape
    count = orbitals * slots
    return pl.pallas_call(
        pick_kernel,
        grid_spec=pltpu.PrefetchScalarGridSpec(
            num_scalar_prefetch=1,
            grid=(),
            in_specs=[pl.BlockSpec(memory_space=pltpu.VMEM)]
            + [pl.BlockSpec(memory_space=pl.ANY)] * len(after),
            out_specs=pl.BlockSpec(memory_space=pltpu.VMEM),
        ),
        out_shape=jax.ShapeDtypeStruct((count, OBLK, BLK), factors.dtype),
        compiler_params=pltpu.CompilerParams(vmem_limit_bytes=16 * MIB),
        cost_estimate=pl.CostEstimate(
            flops=0, bytes_accessed=4 * count * OBLK * BLK, transcendentals=0
        ),
        name="pick",
    )(block_lists, factors, *after)


def as_number(condition):
    return jnp.where(condition, 1.0, 0.0)


def place_facts(shape, axis):
    place = lax.broadcasted_iota(jnp.int32, shape, axis).astype(jnp.float32)
    orbital = jnp.floor((place + 0.5) / NB)
    block = place - NB * orbital
    quarter = jnp.floor((block + 0.5) / (NB // 4))
    return place, orbital, quarter, jnp.floor((quarter + 0.5) / 2), jnp.floor((orbital + 0.5) / 2)


def plan_kernel(slots, where, masks, out):
    rows = levels = 8
    wide = (rows, PLACES)
    _, orbital, quarter, half, origin = place_facts(wide, 1)
    row = lax.broadcasted_iota(jnp.int32, wide, 0)
    kept = jnp.broadcast_to(masks[...], wide)
    capacity = jnp.zeros(wide, jnp.float32)
    for index, size in enumerate(LEVELS + LEVELS[-1:] * (levels - len(LEVELS))):
        capacity = jnp.where(row == index, float(size), capacity)

    square = (PLACES, PLACES)
    down_place, down_orbital, _, _, _ = place_facts(square, 0)
    over_place, over_orbital, _, _, _ = place_facts(square, 1)
    same = as_number(down_orbital == over_orbital)
    before = as_number(down_place < over_place)
    within = (same * before).astype(jnp.bfloat16)
    same, before = same.astype(jnp.bfloat16), before.astype(jnp.bfloat16)

    def times(parts, matrix):
        stacked = jnp.concatenate(parts, axis=0).astype(jnp.bfloat16)
        product = jnp.dot(stacked, matrix, preferred_element_type=jnp.float32)
        return [product[index * rows:(index + 1) * rows] for index in range(len(parts))]

    touching = times([kept * as_number(quarter == z) for z in range(4)], same)
    need = [kept * as_number(touch > 0) for touch in touching]
    zero = jnp.zeros(wide, jnp.float32)

    def union(parts):
        best = zero
        for part in parts:
            best = jnp.maximum(best, part)
        return best

    x_need = []
    for x in range(2):
        touched = as_number(touching[2 * x] + touching[2 * x + 1] > 0)
        here = as_number(half == x)
        x_need.append([
            need[z] * jnp.maximum(here, as_number(quarter == z) * touched) for z in range(4)
        ])
    mine = [kept * as_number(origin == z) for z in range(4)]
    need_up = [union(need[z + 1:]) for z in range(4)]
    far_up = [union(need[z + 2:]) for z in range(4)]
    need_down = [union(need[:z]) for z in range(4)]
    far_down = [union(need[:max(z - 1, 0)]) for z in range(4)]
    up = [mine[z] * need_up[z] for z in range(4)]
    down = [mine[z] * need_down[z] for z in range(4)]
    cross = [[mine[z] * x_need[x][z] for z in range(4)] for x in range(2)]
    up_code, down_code = [zero] * 4, [zero] * 4
    cross_code = [[zero] * 4, [zero] * 4]

    for turn in range(ROUNDS):
        parts = []
        if turn < HOPS:
            for z in range(3):
                parts += [up[z] * far_up[z], up[z] - up[z] * far_up[z]]
                parts += [down[z + 1] * far_down[z + 1], down[z + 1] - down[z + 1] * far_down[z + 1]]
        parts += [cross[x][z] for x in range(2) for z in range(4)]
        ranks = iter(zip(parts, times(parts, before)))

        def taken(pairs):
            rank, total = zero, 0.0
            chosen = zero
            for part, counted in pairs:
                rank = rank + part * (counted + total)
                total = total + jnp.sum(part, axis=1, keepdims=True)
                chosen = chosen + part
            chosen = chosen * as_number(rank < capacity)
            return chosen, chosen * (rank + float(turn * STRIDE + 1))

        up_sent, down_sent = [], []
        if turn < HOPS:
            for z in range(3):
                sent, code = taken([next(ranks), next(ranks)])
                up_sent.append(sent)
                up_code[z] = up_code[z] + code
                up[z] = up[z] - sent
                sent, code = taken([next(ranks), next(ranks)])
                down_sent.append(sent)
                down_code[z + 1] = down_code[z + 1] + code
                down[z + 1] = down[z + 1] - sent
        for x in range(2):
            for z in range(4):
                sent, code = taken([next(ranks)])
                cross_code[x][z] = cross_code[x][z] + code
                cross[x][z] = cross[x][z] - sent
        if turn < HOPS:
            for z in range(3):
                up[z + 1] = up[z + 1] + up_sent[z] * need_up[z + 1]
                down[z] = down[z] + down_sent[z] * need_down[z]
                for x in range(2):
                    cross[x][z + 1] = cross[x][z + 1] + up_sent[z] * x_need[x][z + 1]
                    cross[x][z] = cross[x][z] + down_sent[z] * x_need[x][z]

    left = zero
    for part in up + down + cross[0] + cross[1]:
        left = left + part
    left = jnp.sum(left, axis=1, keepdims=True)
    order = lax.broadcasted_iota(jnp.int32, (levels, 1), 0).astype(jnp.float32)
    level = jnp.min(jnp.where(left > 0, float(len(LEVELS) - 1), order), axis=0, keepdims=True)
    level_row = as_number(
        lax.broadcasted_iota(jnp.int32, (levels, PLACES), 0).astype(jnp.float32) == level
    )
    me_x, me_z = where[0] // 2, where[1]
    odd = lax.rem(me_z, 2).astype(jnp.float32)

    def at(parts, z):
        total = jnp.zeros((levels, PLACES), jnp.float32)
        for index, part in enumerate(parts):
            total = total + jnp.where(z == index, 1.0, 0.0) * part[:levels]
        return jnp.sum(total * level_row, axis=0, keepdims=True)

    cross_here = [jnp.where(me_x == 0, cross_code[0][z], cross_code[1][z]) for z in range(4)]
    cross_there = [jnp.where(me_x == 0, cross_code[1][z], cross_code[0][z]) for z in range(4)]
    def turn_of(code):
        return jnp.floor((code - 0.5) / STRIDE)

    got_up, got_down = at(up_code, me_z - 1), at(down_code, me_z + 1)
    got_cross = at(cross_here, me_z)
    inner = jnp.dot(kept.astype(jnp.bfloat16), within, preferred_element_type=jnp.float32)[0:1]
    one_orbital, one_origin = orbital[0:1], origin[0:1]
    slot = inner + slots * (one_orbital - 2 * one_origin)
    owned = kept[0:1] * as_number(one_origin == me_z.astype(jnp.float32))
    held = (
        owned * (slot + 1)
        + as_number(got_up > 0) * (got_up + STRIDE * (2 - odd + turn_of(got_up)))
        + as_number(got_down > 0) * (got_down + STRIDE * (1 + odd + turn_of(got_down)))
        - 1
    )
    crossed = got_cross - 1
    near = jnp.maximum(
        as_number(quarter[0:1] == where[0].astype(jnp.float32)),
        as_number(quarter[0:1] == me_z.astype(jnp.float32)),
    )
    arrival = jnp.maximum(
        as_number(got_up + got_down > 0) * turn_of(got_up + got_down),
        as_number(got_cross > 0) * turn_of(got_cross),
    )
    lane = lax.broadcasted_iota(jnp.int32, (1, PLACES), 1)
    stage = jnp.zeros((1, PLACES), jnp.float32)
    for index in range(NOB):
        inside = as_number(one_orbital == float(index)) * near * kept[0:1]
        stage = jnp.where(
            lane == index, jnp.max(arrival * inside, axis=1, keepdims=True), stage
        )

    buffer = jnp.floor((held + 0.5) / STRIDE)
    tall = (PLACES, PLACES)
    target = lax.broadcasted_iota(jnp.int32, tall, 0).astype(jnp.float32) + 1
    blank = jnp.zeros_like(held)
    pair = jnp.concatenate([buffer, held - STRIDE * buffer, blank + 1] + [blank] * 5, axis=0)
    position = lax.broadcasted_iota(jnp.int32, (1, PLACES), 1).astype(jnp.float32)
    spare = position - STRIDE * jnp.floor((position + 0.5) / STRIDE)
    sends = []
    sent_up, sent_down = at(up_code, me_z), at(down_code, me_z)
    for sent in (
        jnp.where(odd > 0, sent_down, sent_up),
        jnp.where(odd > 0, sent_up, sent_down),
        at(cross_there, me_z),
    ):
        chosen = as_number(target == sent).astype(jnp.bfloat16)
        both = lax.dot_general(
            pair.astype(jnp.bfloat16), chosen, (((1,), (1,)), ((), ())),
            preferred_element_type=jnp.float32,
        )
        filled = both[0:1] * STRIDE + both[1:2]
        sends.append(jnp.where(both[2:3] > 0, filled, spare))
    flat = level + jnp.zeros((1, PLACES), jnp.float32)
    result = jnp.concatenate(sends + [held, crossed, stage, flat, flat], axis=0)
    out[...] = result.astype(jnp.int32)


def plan(where, masks, slots):
    in_vmem = pl.BlockSpec(memory_space=pltpu.VMEM)
    return pl.pallas_call(
        functools.partial(plan_kernel, slots),
        grid_spec=pltpu.PrefetchScalarGridSpec(
            num_scalar_prefetch=1, grid=(), in_specs=[in_vmem], out_specs=in_vmem
        ),
        out_shape=jax.ShapeDtypeStruct((8, PLACES), jnp.int32),
        compiler_params=pltpu.CompilerParams(vmem_limit_bytes=16 * MIB),
        name="plan",
    )(where, masks)


def branch(which, low, high, run):
    if high - low == 1:
        run(low)
        return
    middle = (low + high) // 2

    @pl.when(which < middle)
    def _():
        branch(which, low, middle, run)

    @pl.when(which >= middle)
    def _():
        branch(which, middle, high, run)


def gather_kernel(turn, held, streams, passed, table, *refs):
    buffers, sem = refs[:held], refs[-1]
    outs = refs[len(refs) - 1 - len(streams) - (passed > 0):-1]
    size = outs[0].shape[0]
    for place in range(passed):
        span = pl.ds(place * size, size)
        pltpu.make_async_copy(buffers[held - passed + place], outs[-1].at[span], sem).start()

    def load(stream, at, code, run):
        def copy(n):
            outs[stream][pl.ds(at, run)] = buffers[n][pl.ds(code & (STRIDE - 1), run)]

        branch(lax.shift_right_logical(code, 6), 0, held, copy)

    run = RUN if size < LEVELS[-1] else 1

    def step(part, carry):
        at = part * run
        for index, stream in enumerate(streams):
            start = stream * PLACES + turn * STRIDE + at
            if run == 1:
                load(index, at, table[start], 1)
                continue
            codes = [table[start + inner] for inner in range(RUN)]
            in_row = codes[1] - codes[0] == 1
            for inner in range(2, RUN):
                in_row = jnp.logical_and(in_row, codes[inner] - codes[inner - 1] == 1)

            @pl.when(in_row)
            def _(index=index, codes=codes):
                load(index, at, codes[0], RUN)

            @pl.when(jnp.logical_not(in_row))
            def _(index=index, start=start):
                def single(inner, carry):
                    load(index, at + inner, table[start + inner], 1)
                    return carry

                lax.fori_loop(0, RUN, single, 0)

        return carry

    lax.fori_loop(0, size // run, step, 0)
    if passed:
        pltpu.make_async_copy(outs[-1], outs[-1], sem).wait()


def gather(turn, size, table, buffers, streams, passed, after):
    dtype = buffers[0].dtype
    shapes = [jax.ShapeDtypeStruct((size, OBLK, BLK), dtype) for _ in streams]
    if passed:
        shapes.append(jax.ShapeDtypeStruct((size * passed, OBLK, BLK), dtype))
    in_vmem = pl.BlockSpec(memory_space=pltpu.VMEM)
    return pl.pallas_call(
        functools.partial(gather_kernel, turn, len(buffers), streams, passed),
        grid_spec=pltpu.PrefetchScalarGridSpec(
            num_scalar_prefetch=1,
            grid=(),
            in_specs=[in_vmem] * len(buffers) + [pl.BlockSpec(memory_space=pl.ANY)] * len(after),
            out_specs=[in_vmem] * len(shapes),
            scratch_shapes=[pltpu.SemaphoreType.DMA(())],
        ),
        out_shape=shapes,
        compiler_params=pltpu.CompilerParams(
            vmem_limit_bytes=2 * sum(array.size for array in [*buffers, *shapes]) + 3 * MIB
        ),
        cost_estimate=pl.CostEstimate(
            flops=0, bytes_accessed=4 * len(streams) * size * OBLK * BLK, transcendentals=0
        ),
        name="gather",
    )(table, *buffers, *after)


def relay_kernel(source, token, out):
    pass


def relay(source, token):
    in_any = pl.BlockSpec(memory_space=pl.ANY)
    return pl.pallas_call(
        relay_kernel,
        in_specs=[in_any, in_any],
        out_specs=in_any,
        out_shape=jax.ShapeDtypeStruct(source.shape, source.dtype),
        input_output_aliases={0: 0},
        compiler_params=pltpu.CompilerParams(vmem_limit_bytes=2 * MIB),
        name="relay",
    )(source, token)


def product_kernel(
    groups, orbitals, row_blocks, col_blocks, stages, first, extra, loc, meta, *refs
):
    flat = iter(refs)
    before = None if first else next(flat)
    sources = [
        [[(next(flat), offset) for offset in offsets] for offsets in buffers] for buffers in groups
    ]
    for _ in range(extra):
        next(flat)
    out, done, items, acc, unit, state, in_sems, acc_sems, out_sems = flat
    group_aux = [len(buffers[0]) for buffers in groups]
    row_tile, col_tile = tile_of(row_blocks), tile_of(col_blocks)
    early = stages[1] <= 1
    if (early or stages[0] < stages[1]) and col_blocks % 2 == 0:
        col_tile = 2
    step_tile = unit.shape[0] // BLK
    col_tiles = col_blocks // col_tile
    first_row, first_col = meta[0], meta[1]
    room = items.shape[0]
    quad = math.gcd(row_blocks, col_blocks, 4)
    if quad == 1:
        quad = math.gcd(row_blocks, col_blocks)
    if stages[0] < stages[1] or stages[1] <= 2:
        quad = 1
    blocks, first_right = row_blocks + col_blocks, row_blocks
    if row_blocks == col_blocks:
        alike = first_row == first_col
        blocks = jnp.where(alike, row_blocks, blocks)
        first_right = jnp.where(alike, 0, first_right)
    depth = sum(group_aux) * OBLK
    padded = items.shape[2]
    height, width = row_tile * BLK, col_tile * BLK
    row_tiles = row_blocks // row_tile
    met_at, columns_at = orbitals, orbitals + row_tiles

    def code_of(group, orbital, block):
        return loc[group * PLACES + orbital * NB + block]

    def any_kept(orbital, start, count):
        best = code_of(0, orbital, start)
        for step in range(1, count):
            best = jnp.maximum(best, code_of(0, orbital, start + step))
        return best >= 0

    def whole_block(block):
        return jnp.where(block < row_blocks, first_row + block, first_col + block - row_blocks)

    def span_of(tile):
        return pl.ds(pl.multiple_of(tile * height, height), height)

    def entering(tile):
        return pltpu.make_async_copy(before.at[span_of(tile)], acc.at[span_of(tile)], acc_sems.at[tile])

    def leaving(tile):
        return pltpu.make_async_copy(acc.at[span_of(tile)], out.at[span_of(tile)], out_sems.at[tile])

    def survey(orbital, count):
        stage = loc[len(groups) * PLACES + orbital]
        wanted = jnp.logical_and(stage >= stages[0], stage <= stages[1])
        state[columns_at + count] = 0

        @pl.when(wanted)
        def _():
            @pl.when(any_kept(orbital, first_row, row_blocks))
            def _():
                columns = jnp.int32(0)
                for col in range(col_tiles):
                    held = any_kept(orbital, first_col + col * col_tile, col_tile)
                    columns = columns + jnp.where(held, 1 << col, 0)
                state[columns_at + count] = columns

        wanted = state[columns_at + count] > 0

        @pl.when(wanted)
        def _():
            state[count] = orbital
            for tile in range(row_tiles):
                held = any_kept(orbital, first_row + tile * row_tile, row_tile)
                state[met_at + tile] = state[met_at + tile] + jnp.where(held, 1 << count, 0)

        return count + jnp.where(wanted, 1, 0)

    for tile in range(row_tiles):
        state[met_at + tile] = 0
    count = lax.fori_loop(0, orbitals, survey, jnp.int32(0))
    done[...] = jnp.zeros(done.shape, done.dtype)

    def fetch(begin):
        def one(slot, carry):
            orbital = state[begin + slot]

            def load(block, run):
                start_aux = 0
                for group, buffers in enumerate(sources):
                    place = code_of(group, orbital, whole_block(block))

                    def copy(n, buffers=buffers, place=place, start_aux=start_aux):
                        for aux, (buffer, offset) in enumerate(buffers[n]):
                            pltpu.make_async_copy(
                                buffer.at[pl.ds((place & (STRIDE - 1)) + offset, run)],
                                items.at[
                                    slot, pl.ds(block, run), pl.ds((start_aux + aux) * OBLK, OBLK)
                                ],
                                in_sems.at[slot],
                            ).start()

                    branch(lax.shift_right_logical(place, 6), 0, len(buffers), copy)
                    start_aux += group_aux[group]
                if padded > depth:
                    items[slot, pl.ds(block, run), depth:] = jnp.zeros(
                        (run, padded - depth, BLK), items.dtype
                    )

            def step(part, carry):
                block = part * quad

                def single(inner, carry):
                    held = code_of(0, orbital, whole_block(block + inner)) >= 0

                    @pl.when(held)
                    def _():
                        load(block + inner, 1)

                    @pl.when(jnp.logical_not(held))
                    def _():
                        items[slot, block + inner] = jnp.zeros((padded, BLK), items.dtype)

                    return carry

                if quad == 1:
                    return single(0, carry)
                in_row = code_of(0, orbital, whole_block(block)) >= 0
                for group in range(len(groups)):
                    low = code_of(group, orbital, whole_block(block))
                    high = code_of(group, orbital, whole_block(block) + quad - 1)
                    in_row = jnp.logical_and(in_row, high - low == quad - 1)

                @pl.when(in_row)
                def _():
                    load(block, quad)

                @pl.when(jnp.logical_not(in_row))
                def _():
                    lax.fori_loop(0, quad, single, 0)

                return carry

            return lax.fori_loop(0, blocks // quad, step, carry)

        lax.fori_loop(0, jnp.minimum(count - begin, room), one, 0)

    def landed(begin):
        def one(slot, carry):
            orbital = state[begin + slot]

            def step(block, carry):
                @pl.when(code_of(0, orbital, whole_block(block)) >= 0)
                def _():
                    whole = items.at[slot, block, pl.ds(0, depth)]
                    pltpu.make_async_copy(whole, whole, in_sems.at[slot]).wait()

                return carry

            return lax.fori_loop(0, blocks, step, carry)

        lax.fori_loop(0, jnp.minimum(count - begin, room), one, 0)

    def multiply(begin, tile):
        rows = span_of(tile)

        def one(slot, carry):
            @pl.when(lax.rem(lax.shift_right_logical(state[met_at + tile], begin + slot), 2) == 1)
            def _():
                turned = []
                for start in range(0, row_tile, step_tile):
                    left = jnp.concatenate(
                        [items[slot, tile * row_tile + start + step] for step in range(step_tile)],
                        axis=1,
                    )
                    turned.append(lax.dot_general(
                        unit[...], left, (((1,), (1,)), ((), ())), preferred_element_type=jnp.float32
                    ).astype(left.dtype))
                turned = jnp.concatenate(turned, axis=0)
                columns = state[columns_at + begin + slot]

                def column(col, carry):
                    @pl.when(lax.rem(lax.shift_right_logical(columns, col), 2) == 1)
                    def _():
                        right = jnp.concatenate(
                            [items[slot, first_right + col * col_tile + step] for step in range(col_tile)],
                            axis=1,
                        )
                        span = pl.ds(pl.multiple_of(col * width, width), width)
                        acc[rows, span] += jnp.dot(turned, right, preferred_element_type=jnp.float32)

                    return carry

                lax.fori_loop(0, col_tiles, column, 0)

            return carry

        lax.fori_loop(0, jnp.minimum(count - begin, room), one, 0)

    fetch(0)
    if first:
        def clear(tile, carry):
            acc[span_of(tile)] = jnp.zeros((height, acc.shape[1]), acc.dtype)
            return carry
    else:
        def clear(tile, carry):
            @pl.when(state[met_at + tile] > 0)
            def _():
                entering(tile).start()
            return carry

    lax.fori_loop(0, row_tiles, clear, 0)
    across = lax.broadcasted_iota(jnp.int32, unit.shape, 1)
    unit[...] = as_number(lax.broadcasted_iota(jnp.int32, unit.shape, 0) == across).astype(unit.dtype)
    passes = (count + room - 1) // room
    if first:
        passes = jnp.maximum(passes, 1)

    def one_pass(turn, carry):
        begin = turn * room

        @pl.when(turn > 0)
        def _():
            fetch(begin)

        landed(begin)

        def row_step(tile, carry):
            touched = jnp.logical_or(first, state[met_at + tile] > 0)

            @pl.when(touched)
            def _():
                if not first:
                    @pl.when(turn == 0)
                    def _():
                        entering(tile).wait()
                multiply(begin, tile)

                @pl.when(turn == passes - 1)
                def _():
                    leaving(tile).start()

            return carry

        lax.fori_loop(0, row_tiles, row_step, 0)
        return carry

    lax.fori_loop(0, passes, one_pass, 0)

    def row_end(tile, carry):
        @pl.when(jnp.logical_or(first, state[met_at + tile] > 0))
        def _():
            leaving(tile).wait()

        return carry

    lax.fori_loop(0, row_tiles, row_end, 0)


def tile_of(blocks):
    return 4 if blocks % 4 == 0 else 3 if blocks % 3 == 0 else 1


def product(loc, meta, sources, held, after, stages, orbitals, row_blocks, col_blocks):
    groups = [[[offset for _, offset in refs] for refs in group] for group in sources]
    flat = [array for group in sources for refs in group for array, _ in refs]
    total_aux = sum(len(group[0]) for group in sources)
    rows, cols = row_blocks * BLK, col_blocks * BLK
    row_tile = tile_of(row_blocks)
    step_tile = 2 if row_tile % 2 == 0 else row_tile
    row_tiles = row_blocks // row_tile
    padded = -(-total_aux * OBLK // 256) * 256
    room = 2
    first = held is None
    in_hbm = pl.BlockSpec(memory_space=pltpu.HBM)
    in_any = pl.BlockSpec(memory_space=pl.ANY)
    return pl.pallas_call(
        functools.partial(
            product_kernel, groups, orbitals, row_blocks, col_blocks, stages, first, len(after)
        ),
        grid_spec=pltpu.PrefetchScalarGridSpec(
            num_scalar_prefetch=2,
            grid=(),
            in_specs=[in_hbm] * (not first)
            + [in_any] * (len(flat) + len(after)),
            out_specs=[in_hbm, pl.BlockSpec(memory_space=pltpu.VMEM)],
            scratch_shapes=[
                pltpu.VMEM((room, row_blocks + col_blocks, padded, BLK), jnp.bfloat16),
                pltpu.VMEM((rows, cols), jnp.float32),
                pltpu.VMEM((step_tile * BLK, step_tile * BLK), jnp.bfloat16),
                pltpu.SMEM((2 * orbitals + row_tiles + 1,), jnp.int32),
                pltpu.SemaphoreType.DMA((room,)),
                pltpu.SemaphoreType.DMA((row_tiles,)),
                pltpu.SemaphoreType.DMA((row_tiles,)),
            ],
        ),
        out_shape=[
            jax.ShapeDtypeStruct((rows, cols), jnp.float32),
            jax.ShapeDtypeStruct((8, 128), jnp.float32),
        ],
        input_output_aliases={} if first else {2: 0},
        compiler_params=pltpu.CompilerParams(
            vmem_limit_bytes=2 * room * padded * (rows + cols) + 4 * rows * cols + 4 * MIB
        ),
        cost_estimate=pl.CostEstimate(
            flops=2 * rows * cols * total_aux * OBLK * orbitals,
            bytes_accessed=4 * rows * cols,
            transcendentals=0,
        ),
        name="product",
    )(loc, meta, *([] if first else [held]), *flat, *after)


def rounds(size, add, table, own):
    first = [(0, 1), (1, 0), (2, 3), (3, 2)]
    second = []
    for aux in range(4):
        here, there = aux * 4, (aux ^ 1) * 4
        second += [(here, there), (here + 1, here + 2), (here + 2, here + 1), (here + 3, there + 3)]
    across = [(0, 2), (2, 0), (1, 3), (3, 1)]

    def to_core(held):
        return lax.ppermute(held, "aux", first)

    moved, crossed, passed, core_crossed = [], [], [], []
    core_own = to_core(own)
    total, done = None, []
    calls = {turn + 1: (turn, turn) for turn in range(ROUNDS)}
    if size == LEVELS[-1]:
        calls = {ROUNDS: (0, HOPS)}
    for turn in range(ROUNDS + 1):
        chunks = []
        if turn < ROUNDS:
            streams = (0, 1, 2) if turn < HOPS else (2,)
            after = crossed[-1:] + ([core_own] if turn == 1 else done)
            chunks = gather(turn, size, table, [own] + moved, streams, len(moved[-2:]), after)
        if turn > 0:
            if turn < ROUNDS:
                passed.append(to_core(chunks[-1]))
            crossed[-1] = relay(crossed[-1], (chunks or done or [own])[0])
            core_crossed.append(to_core(crossed[-1]))
        if turn in calls:
            near = [[(own, 0), (core_own, 0)]]
            for index, held in enumerate(moved):
                near.append([(held, 0), (passed[index // 2], index % 2 * size)])
            far = [[(held, 0), (other, 0)] for held, other in zip(crossed, core_crossed)]
            total, token = add(
                table[3 * PLACES:6 * PLACES], [near, far], total, chunks[:1], calls[turn]
            )
            done = [token]
        if turn < HOPS:
            moved.append(lax.ppermute(chunks[0], "occ", first))
            moved.append(lax.ppermute(chunks[1], ("aux", "occ"), second))
        if turn < ROUNDS:
            crossed.append(lax.ppermute(chunks[2 if turn < HOPS else 0], "aux", across))
    return total


def on_device(shape, factors, block_mask, block_lists):
    aux_count, occ_count = shape["aux"], shape["occ"]
    own_orbitals, slots = block_lists.shape
    aux, occ = lax.axis_index("aux"), lax.axis_index("occ")
    row_blocks, col_blocks = NB // aux_count, NB // occ_count
    meta = jnp.stack([aux * row_blocks, occ * col_blocks]).astype(jnp.int32)

    def add(loc, sources, held, after, stages):
        return product(loc, meta, sources, held, after, stages, NOB, row_blocks, col_blocks)

    kept = block_mask.T > 0
    if aux_count == 4 and occ_count == 4:
        mask = as_number(kept).reshape(1, PLACES)
        where = jnp.stack([aux, occ]).astype(jnp.int32)
        table = plan(where, mask, slots)
        own = pick(factors, block_lists)
        return lax.switch(
            table[6, 0],
            [functools.partial(rounds, size, add) for size in LEVELS],
            table.reshape(-1),
            own,
        )
    own = pick(factors, block_lists)
    everything = lax.all_gather(lax.all_gather(own, "aux"), "occ")
    sources = [[(everything[z, a], 0) for a in range(aux_count)] for z in range(occ_count)]
    earlier = jnp.arange(NB)[None, :] < jnp.arange(NB)[:, None]
    rank = jnp.sum(kept[:, None, :] & earlier[None], axis=2, dtype=jnp.int32)
    orbital = jnp.arange(NOB, dtype=jnp.int32)[:, None]
    start = orbital // own_orbitals * STRIDE + orbital % own_orbitals * slots
    loc = jnp.concatenate([
        jnp.where(kept, rank + start, -1).reshape(-1), jnp.zeros(PLACES, jnp.int32)
    ])
    return add(loc, [sources], None, [], (0, 0))[0]


def solution(mesh):
    placed = (P(("parts", "aux"), "occ", None), P("parts", None), P(("parts", "occ"), None))
    return jax.shard_map(
        functools.partial(on_device, dict(mesh.shape)),
        mesh=mesh,
        in_specs=placed,
        out_specs=P(("parts", "aux"), "occ"),
        check_vma=False,
    )
```

```python
import functools
import math

import jax
import jax.numpy as jnp
from jax import lax
from jax.experimental import pallas as pl
from jax.experimental.pallas import tpu as pltpu
from jax.sharding import PartitionSpec as P

BLK = 128
OBLK = 112
NB = 48
NOB = 8
PLACES = NOB * NB
STRIDE = 64
ROUNDS = 5
HOPS = ROUNDS - 1
LEVELS = (15, 18, 21, 48)
RUN = 3
MIB = 1024 * 1024


def pick_kernel(lists, factors, *refs):
    items = refs[-1]
    orbitals, slots = lists.shape

    def step(slot, carry):
        for orbital in range(orbitals):
            block = jnp.maximum(lists[orbital, slot], 0)
            columns = pl.ds(pl.multiple_of(block * BLK, BLK), BLK)
            rows = slice(orbital * OBLK, (orbital + 1) * OBLK)
            items[orbital * slots + slot] = factors[0, rows, columns]
        return carry

    lax.fori_loop(0, slots, step, 0)


def pick(factors, block_lists, after=()):
    orbitals, slots = block_lists.shape
    count = orbitals * slots
    return pl.pallas_call(
        pick_kernel,
        grid_spec=pltpu.PrefetchScalarGridSpec(
            num_scalar_prefetch=1,
            grid=(),
            in_specs=[pl.BlockSpec(memory_space=pltpu.VMEM)]
            + [pl.BlockSpec(memory_space=pl.ANY)] * len(after),
            out_specs=pl.BlockSpec(memory_space=pltpu.VMEM),
        ),
        out_shape=jax.ShapeDtypeStruct((count, OBLK, BLK), factors.dtype),
        compiler_params=pltpu.CompilerParams(vmem_limit_bytes=16 * MIB),
        cost_estimate=pl.CostEstimate(
            flops=0, bytes_accessed=4 * count * OBLK * BLK, transcendentals=0
        ),
        name="pick",
    )(block_lists, factors, *after)


def as_number(condition):
    return jnp.where(condition, 1.0, 0.0)


def place_facts(shape, axis):
    place = lax.broadcasted_iota(jnp.int32, shape, axis).astype(jnp.float32)
    orbital = jnp.floor((place + 0.5) / NB)
    block = place - NB * orbital
    quarter = jnp.floor((block + 0.5) / (NB // 4))
    return place, orbital, quarter, jnp.floor((quarter + 0.5) / 2), jnp.floor((orbital + 0.5) / 2)


def plan_kernel(slots, where, masks, out):
    rows = levels = 8
    wide = (rows, PLACES)
    _, orbital, quarter, half, origin = place_facts(wide, 1)
    row = lax.broadcasted_iota(jnp.int32, wide, 0)
    kept = jnp.broadcast_to(masks[...], wide)
    capacity = jnp.zeros(wide, jnp.float32)
    for index, size in enumerate(LEVELS + LEVELS[-1:] * (levels - len(LEVELS))):
        capacity = jnp.where(row == index, float(size), capacity)

    square = (PLACES, PLACES)
    down_place, down_orbital, _, _, _ = place_facts(square, 0)
    over_place, over_orbital, _, _, _ = place_facts(square, 1)
    same = as_number(down_orbital == over_orbital)
    before = as_number(down_place < over_place)
    within = (same * before).astype(jnp.bfloat16)
    same, before = same.astype(jnp.bfloat16), before.astype(jnp.bfloat16)

    def times(parts, matrix):
        stacked = jnp.concatenate(parts, axis=0).astype(jnp.bfloat16)
        product = jnp.dot(stacked, matrix, preferred_element_type=jnp.float32)
        return [product[index * rows:(index + 1) * rows] for index in range(len(parts))]

    touching = times([kept * as_number(quarter == z) for z in range(4)], same)
    need = [kept * as_number(touch > 0) for touch in touching]
    zero = jnp.zeros(wide, jnp.float32)

    def union(parts):
        best = zero
        for part in parts:
            best = jnp.maximum(best, part)
        return best

    x_need = []
    for x in range(2):
        touched = as_number(touching[2 * x] + touching[2 * x + 1] > 0)
        here = as_number(half == x)
        x_need.append([
            need[z] * jnp.maximum(here, as_number(quarter == z) * touched) for z in range(4)
        ])
    mine = [kept * as_number(origin == z) for z in range(4)]
    need_up = [union(need[z + 1:]) for z in range(4)]
    far_up = [union(need[z + 2:]) for z in range(4)]
    need_down = [union(need[:z]) for z in range(4)]
    far_down = [union(need[:max(z - 1, 0)]) for z in range(4)]
    up = [mine[z] * need_up[z] for z in range(4)]
    down = [mine[z] * need_down[z] for z in range(4)]
    cross = [[mine[z] * x_need[x][z] for z in range(4)] for x in range(2)]
    up_code, down_code = [zero] * 4, [zero] * 4
    cross_code = [[zero] * 4, [zero] * 4]

    for turn in range(ROUNDS):
        parts = []
        if turn < HOPS:
            for z in range(3):
                parts += [up[z] * far_up[z], up[z] - up[z] * far_up[z]]
                parts += [down[z + 1] * far_down[z + 1], down[z + 1] - down[z + 1] * far_down[z + 1]]
        parts += [cross[x][z] for x in range(2) for z in range(4)]
        ranks = iter(zip(parts, times(parts, before)))

        def taken(pairs):
            rank, total = zero, 0.0
            chosen = zero
            for part, counted in pairs:
                rank = rank + part * (counted + total)
                total = total + jnp.sum(part, axis=1, keepdims=True)
                chosen = chosen + part
            chosen = chosen * as_number(rank < capacity)
            return chosen, chosen * (rank + float(turn * STRIDE + 1))

        up_sent, down_sent = [], []
        if turn < HOPS:
            for z in range(3):
                sent, code = taken([next(ranks), next(ranks)])
                up_sent.append(sent)
                up_code[z] = up_code[z] + code
                up[z] = up[z] - sent
                sent, code = taken([next(ranks), next(ranks)])
                down_sent.append(sent)
                down_code[z + 1] = down_code[z + 1] + code
                down[z + 1] = down[z + 1] - sent
        for x in range(2):
            for z in range(4):
                sent, code = taken([next(ranks)])
                cross_code[x][z] = cross_code[x][z] + code
                cross[x][z] = cross[x][z] - sent
        if turn < HOPS:
            for z in range(3):
                up[z + 1] = up[z + 1] + up_sent[z] * need_up[z + 1]
                down[z] = down[z] + down_sent[z] * need_down[z]
                for x in range(2):
                    cross[x][z + 1] = cross[x][z + 1] + up_sent[z] * x_need[x][z + 1]
                    cross[x][z] = cross[x][z] + down_sent[z] * x_need[x][z]

    left = zero
    for part in up + down + cross[0] + cross[1]:
        left = left + part
    left = jnp.sum(left, axis=1, keepdims=True)
    order = lax.broadcasted_iota(jnp.int32, (levels, 1), 0).astype(jnp.float32)
    level = jnp.min(jnp.where(left > 0, float(len(LEVELS) - 1), order), axis=0, keepdims=True)
    level_row = as_number(
        lax.broadcasted_iota(jnp.int32, (levels, PLACES), 0).astype(jnp.float32) == level
    )
    me_x, me_z = where[0] // 2, where[1]
    odd = lax.rem(me_z, 2).astype(jnp.float32)

    def at(parts, z):
        total = jnp.zeros((levels, PLACES), jnp.float32)
        for index, part in enumerate(parts):
            total = total + jnp.where(z == index, 1.0, 0.0) * part[:levels]
        return jnp.sum(total * level_row, axis=0, keepdims=True)

    cross_here = [jnp.where(me_x == 0, cross_code[0][z], cross_code[1][z]) for z in range(4)]
    cross_there = [jnp.where(me_x == 0, cross_code[1][z], cross_code[0][z]) for z in range(4)]
    def turn_of(code):
        return jnp.floor((code - 0.5) / STRIDE)

    got_up, got_down = at(up_code, me_z - 1), at(down_code, me_z + 1)
    got_cross = at(cross_here, me_z)
    inner = jnp.dot(kept.astype(jnp.bfloat16), within, preferred_element_type=jnp.float32)[0:1]
    one_orbital, one_origin = orbital[0:1], origin[0:1]
    slot = inner + slots * (one_orbital - 2 * one_origin)
    owned = kept[0:1] * as_number(one_origin == me_z.astype(jnp.float32))
    held = (
        owned * (slot + 1)
        + as_number(got_up > 0) * (got_up + STRIDE * (2 - odd + turn_of(got_up)))
        + as_number(got_down > 0) * (got_down + STRIDE * (1 + odd + turn_of(got_down)))
        - 1
    )
    crossed = got_cross - 1
    near = jnp.maximum(
        as_number(quarter[0:1] == where[0].astype(jnp.float32)),
        as_number(quarter[0:1] == me_z.astype(jnp.float32)),
    )
    arrival = jnp.maximum(
        as_number(got_up + got_down > 0) * turn_of(got_up + got_down),
        as_number(got_cross > 0) * turn_of(got_cross),
    )
    lane = lax.broadcasted_iota(jnp.int32, (1, PLACES), 1)
    stage = jnp.zeros((1, PLACES), jnp.float32)
    for index in range(NOB):
        inside = as_number(one_orbital == float(index)) * near * kept[0:1]
        stage = jnp.where(
            lane == index, jnp.max(arrival * inside, axis=1, keepdims=True), stage
        )

    buffer = jnp.floor((held + 0.5) / STRIDE)
    tall = (PLACES, PLACES)
    target = lax.broadcasted_iota(jnp.int32, tall, 0).astype(jnp.float32) + 1
    blank = jnp.zeros_like(held)
    pair = jnp.concatenate([buffer, held - STRIDE * buffer, blank + 1] + [blank] * 5, axis=0)
    position = lax.broadcasted_iota(jnp.int32, (1, PLACES), 1).astype(jnp.float32)
    spare = position - STRIDE * jnp.floor((position + 0.5) / STRIDE)
    sends = []
    sent_up, sent_down = at(up_code, me_z), at(down_code, me_z)
    for sent in (
        jnp.where(odd > 0, sent_down, sent_up),
        jnp.where(odd > 0, sent_up, sent_down),
        at(cross_there, me_z),
    ):
        chosen = as_number(target == sent).astype(jnp.bfloat16)
        both = lax.dot_general(
            pair.astype(jnp.bfloat16), chosen, (((1,), (1,)), ((), ())),
            preferred_element_type=jnp.float32,
        )
        filled = both[0:1] * STRIDE + both[1:2]
        sends.append(jnp.where(both[2:3] > 0, filled, spare))
    flat = level + jnp.zeros((1, PLACES), jnp.float32)
    result = jnp.concatenate(sends + [held, crossed, stage, flat, flat], axis=0)
    out[...] = result.astype(jnp.int32)


def plan(where, masks, slots):
    in_vmem = pl.BlockSpec(memory_space=pltpu.VMEM)
    return pl.pallas_call(
        functools.partial(plan_kernel, slots),
        grid_spec=pltpu.PrefetchScalarGridSpec(
            num_scalar_prefetch=1, grid=(), in_specs=[in_vmem], out_specs=in_vmem
        ),
        out_shape=jax.ShapeDtypeStruct((8, PLACES), jnp.int32),
        compiler_params=pltpu.CompilerParams(vmem_limit_bytes=16 * MIB),
        name="plan",
    )(where, masks)


def branch(which, low, high, run):
    if high - low == 1:
        run(low)
        return
    middle = (low + high) // 2

    @pl.when(which < middle)
    def _():
        branch(which, low, middle, run)

    @pl.when(which >= middle)
    def _():
        branch(which, middle, high, run)


def gather_kernel(turn, held, streams, passed, table, *refs):
    buffers, sem = refs[:held], refs[-1]
    outs = refs[len(refs) - 1 - len(streams) - (passed > 0):-1]
    size = outs[0].shape[0]
    for place in range(passed):
        span = pl.ds(place * size, size)
        pltpu.make_async_copy(buffers[held - passed + place], outs[-1].at[span], sem).start()

    def load(stream, at, code, run):
        def copy(n):
            outs[stream][pl.ds(at, run)] = buffers[n][pl.ds(code & (STRIDE - 1), run)]

        branch(lax.shift_right_logical(code, 6), 0, held, copy)

    run = RUN if size < LEVELS[-1] else 1

    def step(part, carry):
        at = part * run
        for index, stream in enumerate(streams):
            start = stream * PLACES + turn * STRIDE + at
            if run == 1:
                load(index, at, table[start], 1)
                continue
            codes = [table[start + inner] for inner in range(RUN)]
            in_row = codes[1] - codes[0] == 1
            for inner in range(2, RUN):
                in_row = jnp.logical_and(in_row, codes[inner] - codes[inner - 1] == 1)

            @pl.when(in_row)
            def _(index=index, codes=codes):
                load(index, at, codes[0], RUN)

            @pl.when(jnp.logical_not(in_row))
            def _(index=index, start=start):
                def single(inner, carry):
                    load(index, at + inner, table[start + inner], 1)
                    return carry

                lax.fori_loop(0, RUN, single, 0)

        return carry

    lax.fori_loop(0, size // run, step, 0)
    if passed:
        pltpu.make_async_copy(outs[-1], outs[-1], sem).wait()


def gather(turn, size, table, buffers, streams, passed, after):
    dtype = buffers[0].dtype
    shapes = [jax.ShapeDtypeStruct((size, OBLK, BLK), dtype) for _ in streams]
    if passed:
        shapes.append(jax.ShapeDtypeStruct((size * passed, OBLK, BLK), dtype))
    in_vmem = pl.BlockSpec(memory_space=pltpu.VMEM)
    return pl.pallas_call(
        functools.partial(gather_kernel, turn, len(buffers), streams, passed),
        grid_spec=pltpu.PrefetchScalarGridSpec(
            num_scalar_prefetch=1,
            grid=(),
            in_specs=[in_vmem] * len(buffers) + [pl.BlockSpec(memory_space=pl.ANY)] * len(after),
            out_specs=[in_vmem] * len(shapes),
            scratch_shapes=[pltpu.SemaphoreType.DMA(())],
        ),
        out_shape=shapes,
        compiler_params=pltpu.CompilerParams(
            vmem_limit_bytes=2 * sum(array.size for array in [*buffers, *shapes]) + 3 * MIB
        ),
        cost_estimate=pl.CostEstimate(
            flops=0, bytes_accessed=4 * len(streams) * size * OBLK * BLK, transcendentals=0
        ),
        name="gather",
    )(table, *buffers, *after)


def relay_kernel(source, token, out):
    pass


def relay(source, token):
    in_any = pl.BlockSpec(memory_space=pl.ANY)
    return pl.pallas_call(
        relay_kernel,
        in_specs=[in_any, in_any],
        out_specs=in_any,
        out_shape=jax.ShapeDtypeStruct(source.shape, source.dtype),
        input_output_aliases={0: 0},
        compiler_params=pltpu.CompilerParams(vmem_limit_bytes=2 * MIB),
        name="relay",
    )(source, token)


def product_kernel(
    groups, orbitals, row_blocks, col_blocks, stages, first, extra, loc, meta, *refs
):
    flat = iter(refs)
    before = None if first else next(flat)
    sources = [
        [[(next(flat), offset) for offset in offsets] for offsets in buffers] for buffers in groups
    ]
    for _ in range(extra):
        next(flat)
    out, done, items, acc, unit, state, in_sems, acc_sems, out_sems = flat
    group_aux = [len(buffers[0]) for buffers in groups]
    row_tile, col_tile = tile_of(row_blocks), tile_of(col_blocks)
    step_tile = unit.shape[0] // BLK
    col_tiles = col_blocks // col_tile
    first_row, first_col = meta[0], meta[1]
    room = items.shape[0]
    quad = math.gcd(row_blocks, col_blocks, 4)
    if quad == 1:
        quad = math.gcd(row_blocks, col_blocks)
    if stages[0] < stages[1] - 1:
        quad = 1
    blocks, first_right = row_blocks + col_blocks, row_blocks
    if row_blocks == col_blocks:
        alike = first_row == first_col
        blocks = jnp.where(alike, row_blocks, blocks)
        first_right = jnp.where(alike, 0, first_right)
    depth = sum(group_aux) * OBLK
    padded = items.shape[2]
    height, width = row_tile * BLK, col_tile * BLK
    row_tiles = row_blocks // row_tile
    met_at, columns_at = orbitals, orbitals + row_tiles

    def code_of(group, orbital, block):
        return loc[group * PLACES + orbital * NB + block]

    def any_kept(orbital, start, count):
        best = code_of(0, orbital, start)
        for step in range(1, count):
            best = jnp.maximum(best, code_of(0, orbital, start + step))
        return best >= 0

    def whole_block(block):
        return jnp.where(block < row_blocks, first_row + block, first_col + block - row_blocks)

    def span_of(tile):
        return pl.ds(pl.multiple_of(tile * height, height), height)

    def entering(tile):
        return pltpu.make_async_copy(before.at[span_of(tile)], acc.at[span_of(tile)], acc_sems.at[tile])

    def leaving(tile):
        return pltpu.make_async_copy(acc.at[span_of(tile)], out.at[span_of(tile)], out_sems.at[tile])

    def survey(orbital, count):
        stage = loc[len(groups) * PLACES + orbital]
        wanted = jnp.logical_and(stage >= stages[0], stage <= stages[1])
        state[columns_at + count] = 0

        @pl.when(wanted)
        def _():
            @pl.when(any_kept(orbital, first_row, row_blocks))
            def _():
                columns = jnp.int32(0)
                for col in range(col_tiles):
                    held = any_kept(orbital, first_col + col * col_tile, col_tile)
                    columns = columns + jnp.where(held, 1 << col, 0)
                state[columns_at + count] = columns

        wanted = state[columns_at + count] > 0

        @pl.when(wanted)
        def _():
            state[count] = orbital
            for tile in range(row_tiles):
                held = any_kept(orbital, first_row + tile * row_tile, row_tile)
                state[met_at + tile] = state[met_at + tile] + jnp.where(held, 1 << count, 0)

        return count + jnp.where(wanted, 1, 0)

    for tile in range(row_tiles):
        state[met_at + tile] = 0
    count = lax.fori_loop(0, orbitals, survey, jnp.int32(0))
    done[...] = jnp.zeros(done.shape, done.dtype)

    def fetch(begin):
        def one(slot, carry):
            orbital = state[begin + slot]

            def load(block, run):
                start_aux = 0
                for group, buffers in enumerate(sources):
                    place = code_of(group, orbital, whole_block(block))

                    def copy(n, buffers=buffers, place=place, start_aux=start_aux):
                        for aux, (buffer, offset) in enumerate(buffers[n]):
                            pltpu.make_async_copy(
                                buffer.at[pl.ds((place & (STRIDE - 1)) + offset, run)],
                                items.at[
                                    slot, pl.ds(block, run), pl.ds((start_aux + aux) * OBLK, OBLK)
                                ],
                                in_sems.at[slot],
                            ).start()

                    branch(lax.shift_right_logical(place, 6), 0, len(buffers), copy)
                    start_aux += group_aux[group]
                if padded > depth:
                    items[slot, pl.ds(block, run), depth:] = jnp.zeros(
                        (run, padded - depth, BLK), items.dtype
                    )

            def step(part, carry):
                block = part * quad

                def single(inner, carry):
                    held = code_of(0, orbital, whole_block(block + inner)) >= 0

                    @pl.when(held)
                    def _():
                        load(block + inner, 1)

                    @pl.when(jnp.logical_not(held))
                    def _():
                        items[slot, block + inner] = jnp.zeros((padded, BLK), items.dtype)

                    return carry

                if quad == 1:
                    return single(0, carry)
                in_row = code_of(0, orbital, whole_block(block)) >= 0
                for group in range(len(groups)):
                    low = code_of(group, orbital, whole_block(block))
                    high = code_of(group, orbital, whole_block(block) + quad - 1)
                    in_row = jnp.logical_and(in_row, high - low == quad - 1)

                @pl.when(in_row)
                def _():
                    load(block, quad)

                @pl.when(jnp.logical_not(in_row))
                def _():
                    lax.fori_loop(0, quad, single, 0)

                return carry

            return lax.fori_loop(0, blocks // quad, step, carry)

        lax.fori_loop(0, jnp.minimum(count - begin, room), one, 0)

    def landed(begin):
        def one(slot, carry):
            orbital = state[begin + slot]

            def step(block, carry):
                @pl.when(code_of(0, orbital, whole_block(block)) >= 0)
                def _():
                    whole = items.at[slot, block, pl.ds(0, depth)]
                    pltpu.make_async_copy(whole, whole, in_sems.at[slot]).wait()

                return carry

            return lax.fori_loop(0, blocks, step, carry)

        lax.fori_loop(0, jnp.minimum(count - begin, room), one, 0)

    def multiply(begin, tile):
        rows = span_of(tile)

        def one(slot, carry):
            @pl.when(lax.rem(lax.shift_right_logical(state[met_at + tile], begin + slot), 2) == 1)
            def _():
                turned = []
                for start in range(0, row_tile, step_tile):
                    left = jnp.concatenate(
                        [items[slot, tile * row_tile + start + step] for step in range(step_tile)],
                        axis=1,
                    )
                    turned.append(lax.dot_general(
                        unit[...], left, (((1,), (1,)), ((), ())), preferred_element_type=jnp.float32
                    ).astype(left.dtype))
                turned = jnp.concatenate(turned, axis=0)
                columns = state[columns_at + begin + slot]

                def column(col, carry):
                    @pl.when(lax.rem(lax.shift_right_logical(columns, col), 2) == 1)
                    def _():
                        right = jnp.concatenate(
                            [items[slot, first_right + col * col_tile + step] for step in range(col_tile)],
                            axis=1,
                        )
                        span = pl.ds(pl.multiple_of(col * width, width), width)
                        acc[rows, span] += jnp.dot(turned, right, preferred_element_type=jnp.float32)

                    return carry

                lax.fori_loop(0, col_tiles, column, 0)

            return carry

        lax.fori_loop(0, jnp.minimum(count - begin, room), one, 0)

    fetch(0)
    if first:
        def clear(tile, carry):
            acc[span_of(tile)] = jnp.zeros((height, acc.shape[1]), acc.dtype)
            return carry
    else:
        def clear(tile, carry):
            @pl.when(state[met_at + tile] > 0)
            def _():
                entering(tile).start()
            return carry

    lax.fori_loop(0, row_tiles, clear, 0)
    across = lax.broadcasted_iota(jnp.int32, unit.shape, 1)
    unit[...] = as_number(lax.broadcasted_iota(jnp.int32, unit.shape, 0) == across).astype(unit.dtype)
    passes = (count + room - 1) // room
    if first:
        passes = jnp.maximum(passes, 1)

    def one_pass(turn, carry):
        begin = turn * room

        @pl.when(turn > 0)
        def _():
            fetch(begin)

        landed(begin)

        def row_step(tile, carry):
            touched = jnp.logical_or(first, state[met_at + tile] > 0)

            @pl.when(touched)
            def _():
                if not first:
                    @pl.when(turn == 0)
                    def _():
                        entering(tile).wait()
                multiply(begin, tile)

                @pl.when(turn == passes - 1)
                def _():
                    leaving(tile).start()

            return carry

        lax.fori_loop(0, row_tiles, row_step, 0)
        return carry

    lax.fori_loop(0, passes, one_pass, 0)

    def row_end(tile, carry):
        @pl.when(jnp.logical_or(first, state[met_at + tile] > 0))
        def _():
            leaving(tile).wait()

        return carry

    lax.fori_loop(0, row_tiles, row_end, 0)


def tile_of(blocks):
    return 4 if blocks % 4 == 0 else 3 if blocks % 3 == 0 else 1


def product(loc, meta, sources, held, after, stages, orbitals, row_blocks, col_blocks):
    groups = [[[offset for _, offset in refs] for refs in group] for group in sources]
    flat = [array for group in sources for refs in group for array, _ in refs]
    total_aux = sum(len(group[0]) for group in sources)
    rows, cols = row_blocks * BLK, col_blocks * BLK
    row_tile = tile_of(row_blocks)
    step_tile = 2 if row_tile % 2 == 0 else row_tile
    row_tiles = row_blocks // row_tile
    padded = -(-total_aux * OBLK // 256) * 256
    room = 1
    first = held is None
    in_hbm = pl.BlockSpec(memory_space=pltpu.HBM)
    in_any = pl.BlockSpec(memory_space=pl.ANY)
    return pl.pallas_call(
        functools.partial(
            product_kernel, groups, orbitals, row_blocks, col_blocks, stages, first, len(after)
        ),
        grid_spec=pltpu.PrefetchScalarGridSpec(
            num_scalar_prefetch=2,
            grid=(),
            in_specs=[in_hbm] * (not first)
            + [in_any] * (len(flat) + len(after)),
            out_specs=[in_hbm, pl.BlockSpec(memory_space=pltpu.VMEM)],
            scratch_shapes=[
                pltpu.VMEM((room, row_blocks + col_blocks, padded, BLK), jnp.bfloat16),
                pltpu.VMEM((rows, cols), jnp.float32),
                pltpu.VMEM((step_tile * BLK, step_tile * BLK), jnp.bfloat16),
                pltpu.SMEM((2 * orbitals + row_tiles + 1,), jnp.int32),
                pltpu.SemaphoreType.DMA((room,)),
                pltpu.SemaphoreType.DMA((row_tiles,)),
                pltpu.SemaphoreType.DMA((row_tiles,)),
            ],
        ),
        out_shape=[
            jax.ShapeDtypeStruct((rows, cols), jnp.float32),
            jax.ShapeDtypeStruct((8, 128), jnp.float32),
        ],
        input_output_aliases={} if first else {2: 0},
        compiler_params=pltpu.CompilerParams(
            vmem_limit_bytes=2 * room * padded * (rows + cols) + 4 * rows * cols + 4 * MIB
        ),
        cost_estimate=pl.CostEstimate(
            flops=2 * rows * cols * total_aux * OBLK * orbitals,
            bytes_accessed=4 * rows * cols,
            transcendentals=0,
        ),
        name="product",
    )(loc, meta, *([] if first else [held]), *flat, *after)


def rounds(size, add, table, own):
    first = [(0, 1), (1, 0), (2, 3), (3, 2)]
    second = []
    for aux in range(4):
        here, there = aux * 4, (aux ^ 1) * 4
        second += [(here, there), (here + 1, here + 2), (here + 2, here + 1), (here + 3, there + 3)]
    across = [(0, 2), (2, 0), (1, 3), (3, 1)]

    def to_core(held):
        return lax.ppermute(held, "aux", first)

    moved, crossed, passed, core_crossed = [], [], [], []
    core_own = to_core(own)
    total, done = None, []
    calls = {2: (0, 1), 3: (2, 2), 4: (3, 3), 5: (4, 4)}
    if size == LEVELS[-1]:
        calls = {ROUNDS: (0, HOPS)}
    for turn in range(ROUNDS + 1):
        chunks = []
        if turn < ROUNDS:
            streams = (0, 1, 2) if turn < HOPS else (2,)
            after = crossed[-1:] + ([core_own] if turn == 1 else done)
            chunks = gather(turn, size, table, [own] + moved, streams, len(moved[-2:]), after)
        if turn > 0:
            if turn < ROUNDS:
                passed.append(to_core(chunks[-1]))
            crossed[-1] = relay(crossed[-1], (chunks or done or [own])[0])
            core_crossed.append(to_core(crossed[-1]))
        if turn in calls:
            near = [[(own, 0), (core_own, 0)]]
            for index, held in enumerate(moved):
                near.append([(held, 0), (passed[index // 2], index % 2 * size)])
            far = [[(held, 0), (other, 0)] for held, other in zip(crossed, core_crossed)]
            total, token = add(
                table[3 * PLACES:6 * PLACES], [near, far], total, chunks[:1], calls[turn]
            )
            done = [token]
        if turn < HOPS:
            moved.append(lax.ppermute(chunks[0], "occ", first))
            moved.append(lax.ppermute(chunks[1], ("aux", "occ"), second))
        if turn < ROUNDS:
            crossed.append(lax.ppermute(chunks[2 if turn < HOPS else 0], "aux", across))
    return total


def on_device(shape, factors, block_mask, block_lists):
    aux_count, occ_count = shape["aux"], shape["occ"]
    own_orbitals, slots = block_lists.shape
    aux, occ = lax.axis_index("aux"), lax.axis_index("occ")
    row_blocks, col_blocks = NB // aux_count, NB // occ_count
    meta = jnp.stack([aux * row_blocks, occ * col_blocks]).astype(jnp.int32)

    def add(loc, sources, held, after, stages):
        return product(loc, meta, sources, held, after, stages, NOB, row_blocks, col_blocks)

    kept = block_mask.T > 0
    if aux_count == 4 and occ_count == 4:
        mask = as_number(kept).reshape(1, PLACES)
        where = jnp.stack([aux, occ]).astype(jnp.int32)
        table = plan(where, mask, slots)
        own = pick(factors, block_lists)
        return lax.switch(
            table[6, 0],
            [functools.partial(rounds, size, add) for size in LEVELS],
            table.reshape(-1),
            own,
        )
    own = pick(factors, block_lists)
    everything = lax.all_gather(lax.all_gather(own, "aux"), "occ")
    sources = [[(everything[z, a], 0) for a in range(aux_count)] for z in range(occ_count)]
    earlier = jnp.arange(NB)[None, :] < jnp.arange(NB)[:, None]
    rank = jnp.sum(kept[:, None, :] & earlier[None], axis=2, dtype=jnp.int32)
    orbital = jnp.arange(NOB, dtype=jnp.int32)[:, None]
    start = orbital // own_orbitals * STRIDE + orbital % own_orbitals * slots
    loc = jnp.concatenate([
        jnp.where(kept, rank + start, -1).reshape(-1), jnp.zeros(PLACES, jnp.int32)
    ])
    return add(loc, [sources], None, [], (0, 0))[0]


def solution(mesh):
    placed = (P(("parts", "aux"), "occ", None), P("parts", None), P(("parts", "occ"), None))
    return jax.shard_map(
        functools.partial(on_device, dict(mesh.shape)),
        mesh=mesh,
        in_specs=placed,
        out_specs=P(("parts", "aux"), "occ"),
        check_vma=False,
    )
```
